128 devices in a mesh: row: 8 (over x, core), col: 16 (over y, z).
Axes of the slice: x: 4, y: 4, z: 4, core: 2. Of those that a mesh axis runs over, the one named last changes fastest.
Arguments:
- embeddings: bfloat16 [65536, 384], P(('row', 'col')), may hold values from -6 to 6
- block_cluster: int32 [256], replicated, may hold values from 0 to 7, never falling along the last dimension, each value on 1 to 160 neighbouring positions
Outputs:
- nearest: float32 [65536], P(('row', 'col'))
The draws below stay inside these ranges and needn't reach their ends.
Inputs may be any that keep to these rules, and one draw needn't show every extreme that they name: block_cluster never falls along the blocks; each cluster covers 1 to 160 consecutive blocks and one covers exactly 160.
All inputs are finite; a program needn't handle non-finite values.
Results may differ from the reference program's by a relative error of at most 0.0012.
Values may be sent and summed in bfloat16 or wider, within the bound.
No kernel may reach another device: no remote copies, remote signals or barrier semaphores. Data moves between devices by JAX's collectives and lax.ppermute only.
A program may use at most 128 MiB of HBM per device.

```python
import math
import jax
import jax.numpy as jnp
import numpy as np
from jax import lax

D = 384
BLK = 256
NCLUST = 8
NBLK = 256
MOSTB = 160
NDOC = 65536


def level_of(rng, shape, pieces, least, largest):
    factor_of = 1.0
    for position, shards_of in pieces:
        steps = jax.random.uniform(jax.random.fold_in(jax.random.fold_in(rng, 6), position), (shards_of,), jnp.float32, least / len(pieces), largest / len(pieces))
        factor_of = factor_of * jnp.repeat(jnp.exp(steps), shape[position] // shards_of).reshape((-1,) + (1,) * (len(shape) - 1 - position))
    return factor_of


def profile(amount, total, reach, slope):
    weights = [(1 << 20) // math.isqrt(grade ** slope) + 1 for grade in range(2, amount + 1)]
    rest, holding = total - reach - (amount - 1), [1] * (amount - 1)
    while rest > 0:
        free = [i for i in range(amount - 1) if holding[i] < reach]
        pool, budget = sum([weights[i] for i in free]), rest
        for i in free:
            addition = min(reach - holding[i], max(1, budget * weights[i] // pool), rest)
            holding[i] = holding[i] + addition
            rest = rest - addition
    return np.array([reach] + holding)


def ragged(stream_key, count, total, reach, slope):
    if count == 2:
        one = jax.random.randint(stream_key, (), max(1, total - reach), min(reach, total - 1) + 1)
        return jnp.stack([one, total - one])
    tallies = jnp.asarray(profile(count, total, reach, slope), jnp.int32)
    twos = (count - 1) // 2
    giver, receiver = tallies[1:1 + 2 * twos:2], tallies[2:2 + 2 * twos:2]
    margin = jnp.minimum(giver - 1, reach - receiver)
    passed = jax.random.randint(jax.random.fold_in(stream_key, 1), (twos,), 0, 1 << 20) % (margin + 1)
    tallies = tallies.at[1:1 + 2 * twos:2].set(giver - passed).at[2:2 + 2 * twos:2].set(receiver + passed)
    return tallies[jax.random.permutation(jax.random.fold_in(stream_key, 2), count)]


def bell_draw(stream_key, dims, scale, reach, pieces=(), kind=jnp.bfloat16):
    factor_of = level_of(stream_key, dims, pieces, -0.22, 0.18) if pieces else 1.0
    drawn = jax.random.normal(stream_key, dims, jnp.float32) * scale * factor_of
    return jnp.minimum(jnp.maximum(drawn, -reach), reach).astype(kind)


def setup_inputs(seed: int = 0) -> dict:
    keys = jax.random.split(jax.random.key(seed), 3)
    embeddings = bell_draw(keys[0], (NDOC, D), 1.0, 6.0, ((0, 128),))
    block_cluster = jnp.searchsorted(jnp.cumsum(ragged(keys[1], NCLUST, NBLK, MOSTB, 2)), jnp.arange(NBLK), side="right").astype(jnp.int32)
    return {"embeddings": embeddings, "block_cluster": block_cluster}


def reference(embeddings, block_cluster):
    values = embeddings.astype(jnp.float32)
    squares = lax.optimization_barrier(jnp.sum(values * values, axis=1, keepdims=True))
    unit = (values * lax.rsqrt(squares + 1e-06)).astype(jnp.bfloat16)
    label = jnp.repeat(block_cluster, BLK)
    total = label.shape[0]
    step = math.gcd(512, total)
    index_all = jnp.arange(total, dtype=jnp.int32)

    def one_block(offset):
        block_rows = lax.dynamic_slice_in_dim(unit, offset, step, 0)
        block_label = lax.dynamic_slice_in_dim(label, offset, step, 0)
        block_index = lax.dynamic_slice_in_dim(index_all, offset, step, 0)
        scores = lax.dot_general(block_rows, unit, (((1,), (1,)), ((), ())), preferred_element_type=jnp.float32)
        keep = (block_label[:, None] == label[None, :]) & (block_index[:, None] != index_all[None, :])
        return lax.optimization_barrier(jnp.max(jnp.where(keep, scores, jnp.float32(-2.0)), axis=1))
    starts = jnp.arange(total // step, dtype=jnp.int32) * step
    return lax.map(one_block, starts).reshape(total)
```

```python
import functools

import jax
import jax.numpy as jnp
import numpy as np
from jax import lax
from jax.experimental import pallas as pl
from jax.experimental.pallas import tpu as pltpu
from jax.sharding import PartitionSpec as P

BLK = 256
SHARD = 512
D = 384
VMEM_LIMIT = 40 * 1024 * 1024

CORE = 16
X1, X3, Y1, Y3, Z1, Z3 = 32, 96, 4, 12, 1, 3
R_MASKS = (0, X1, X3, Y1, X1 ^ X3, X3 ^ Y1, Y1 ^ X1, X1 ^ X3 ^ Y1)
C_MASKS = (0, Y3, Z1, Z3, Y3 ^ Z1, Z1 ^ Z3, Z3 ^ Y3, Y3 ^ Z1 ^ Z3)
R_SENDS = ((0, X1), (0, X3), (0, Y1), (1, X3), (2, Y1), (3, X1), (5, X1))
C_SENDS = ((0, Y3), (0, Z1), (0, Z3), (1, Z1), (2, Z3), (3, Y3), (5, Y3))
STEP_OF = (0, 0, 0, 0, 1, 1, 1, 2)


def make_table():
    phases = [[], [], []]
    flips = {}
    for i, a in enumerate(R_MASKS):
        for j in range(16):
            b = C_MASKS[j % 8] ^ (CORE if j >= 8 else 0)
            w = a ^ b
            if w == 0:
                continue
            bit = CORE if j >= 8 else w & -w
            phase = max(STEP_OF[i], STEP_OF[j % 8])
            key = (bit, phase)
            flips[key] = flips.get(key, 0) ^ 1
            phases[phase].append((i | j << 4, a, b, bit, bit if flips[key] else 0))
    return [np.array(p, np.int32) for p in phases]


TABLES = make_table()
STARTS = np.cumsum([0] + [len(t) for t in TABLES])
TABLE = np.concatenate(TABLES).reshape(-1)
LIST = len(TABLE) // 5 + 8
VMEM = pltpu.VMEM
SMEM = pltpu.SMEM


def spec(space):
    return pl.BlockSpec(memory_space=space)


def unit_kernel(x_ref, unit_ref, flat_ref):
    values = x_ref[...].astype(jnp.float32)
    squares = jnp.sum(values * values, axis=1, keepdims=True)
    unit = values * lax.rsqrt(squares + 1e-06)
    unit_ref[...] = unit.astype(jnp.bfloat16)
    flat_ref[...] = unit.T.astype(jnp.bfloat16)


def unit_call(x):
    return pl.pallas_call(
        unit_kernel,
        out_shape=(
            jax.ShapeDtypeStruct((SHARD, D), jnp.bfloat16),
            jax.ShapeDtypeStruct((D, SHARD), jnp.bfloat16),
        ),
        in_specs=[spec(VMEM)],
        out_specs=(spec(VMEM), spec(VMEM)),
        compiler_params=pltpu.CompilerParams(vmem_limit_bytes=VMEM_LIMIT),
        cost_estimate=pl.CostEstimate(flops=1000000, bytes_accessed=1200000, transcendentals=512),
    )(x)


def self_kernel(here_ref, cluster_ref, table_ref, unit_ref, flat_ref, own_ref, list_ref, count_ref):
    here = here_ref[0]
    for phase in range(3):
        first = int(STARTS[phase])

        def candidate(n, count):
            code = table_ref[5 * n]
            a = 2 * (here ^ table_ref[5 * n + 1])
            b = 2 * (here ^ table_ref[5 * n + 2])
            mine = (here & table_ref[5 * n + 3]) == table_ref[5 * n + 4]
            a0, a1 = cluster_ref[a], cluster_ref[a + 1]
            b0, b1 = cluster_ref[b], cluster_ref[b + 1]
            quads = (
                jnp.where(a0 == b0, 1, 0)
                + jnp.where(a0 == b1, 2, 0)
                + jnp.where(a1 == b0, 4, 0)
                + jnp.where(a1 == b1, 8, 0)
            )
            list_ref[first + count] = code | (quads << 8)
            return count + jnp.where(mine & (quads != 0), 1, 0)

        count_ref[phase] = lax.fori_loop(first, int(STARTS[phase + 1]), candidate, jnp.int32(0))

    same = cluster_ref[2 * here] == cluster_ref[2 * here + 1]
    for half in range(2):
        rows = slice(half * BLK, half * BLK + BLK)
        scores = jnp.dot(unit_ref[rows, :], flat_ref[...], preferred_element_type=jnp.float32)
        row = lax.broadcasted_iota(jnp.int32, scores.shape, 0) + half * BLK
        col = lax.broadcasted_iota(jnp.int32, scores.shape, 1)
        keep = (row != col) & (same | ((row // BLK) == (col // BLK)))
        best = jnp.max(jnp.where(keep, scores, jnp.float32(-2.0)), axis=0, keepdims=True)
        if half == 0:
            own_ref[...] = best
        else:
            own_ref[...] = jnp.maximum(own_ref[...], best)


def self_call(here, cluster, table, unit, flat):
    return pl.pallas_call(
        self_kernel,
        out_shape=(
            jax.ShapeDtypeStruct((1, SHARD), jnp.float32),
            jax.ShapeDtypeStruct((LIST,), jnp.int32),
            jax.ShapeDtypeStruct((3,), jnp.int32),
        ),
        in_specs=[spec(SMEM), spec(SMEM), spec(SMEM), spec(VMEM), spec(VMEM)],
        out_specs=(spec(VMEM), spec(SMEM), spec(SMEM)),
        compiler_params=pltpu.CompilerParams(vmem_limit_bytes=VMEM_LIMIT),
        cost_estimate=pl.CostEstimate(flops=4000000000, bytes_accessed=1000000, transcendentals=0),
    )(here, cluster, table, unit, flat)


def score_kernel(phase, slots, list_ref, count_ref, *refs):
    a_in, refs = refs[:slots], refs[slots:]
    b_in, refs = refs[: 2 * slots], refs[2 * slots :]
    if phase:
        row_in, col_in, refs = refs[0], refs[1], refs[2:]
    if phase < 2:
        row_ref, col_ref, a_buf, b_buf = refs
    else:
        row_lo, row_hi, col_lo, col_hi, other, row_ref, col_ref, a_buf, b_buf = refs

    if phase:
        row_ref[...] = row_in[...]
        col_ref[...] = col_in[...]
    else:
        row_ref[...] = jnp.full(row_ref.shape, -2.0, jnp.float32)
        col_ref[...] = jnp.full(col_ref.shape, -2.0, jnp.float32)
    for n in range(slots):
        a_buf[n] = a_in[n][...]
        b_buf[n] = b_in[n][...]
        b_buf[8 + n] = b_in[slots + n][...]

    first = int(STARTS[phase])

    def fold(i, j, rows, cols, scores):
        best = scores[:, :128]
        for k in range(1, scores.shape[1] // 128):
            best = jnp.maximum(best, scores[:, 128 * k : 128 * k + 128])
        row_ref[i, rows, :] = jnp.maximum(row_ref[i, rows, :], best)
        down = jnp.max(scores.reshape(scores.shape[0] // 8, 8, scores.shape[1]), axis=0)
        col_ref[j, :, cols] = jnp.maximum(col_ref[j, :, cols], down)

    @pl.loop(0, count_ref[phase])
    def _(n):
        word = list_ref[first + n]
        i = word & 15
        j = (word >> 4) & 15
        quads = word >> 8

        @pl.when(quads == 15)
        def _():
            for half in range(2):
                rows = pl.ds(half * BLK, BLK)
                scores = jnp.dot(
                    a_buf[i, rows, :], b_buf[j], preferred_element_type=jnp.float32
                )
                fold(i, j, rows, slice(None), scores)

        @pl.when(quads != 15)
        def _():
            for quad in range(4):

                @pl.when(((quads >> quad) & 1) == 1)
                def _():
                    rows = pl.ds((quad // 2) * BLK, BLK)
                    cols = pl.ds((quad % 2) * BLK, BLK)
                    scores = jnp.dot(
                        a_buf[i, rows, :], b_buf[j, :, cols], preferred_element_type=jnp.float32
                    )
                    fold(i, j, rows, cols, scores)

    if phase == 2:
        for place, (low, high) in enumerate(((0, 3), (1, 6), (2, 5), (4, 7))):
            for out, slot in ((row_lo, low), (row_hi, high)):
                for k in range(4):
                    part = row_ref[slot, 128 * k : 128 * k + 128, :].T
                    out[place : place + 1, 128 * k : 128 * k + 128] = jnp.max(
                        part, axis=0, keepdims=True
                    )
        for place, (low, high) in enumerate(((0, 2), (1, 4), (3, 5), (6, 7))):
            for out, slot in ((col_lo, low), (col_hi, high)):
                out[place : place + 1, :] = jnp.max(col_ref[slot], axis=0, keepdims=True)
            other[place : place + 1, :] = jnp.max(col_ref[8 + low], axis=0, keepdims=True)
            other[4 + place : 5 + place, :] = jnp.max(col_ref[8 + high], axis=0, keepdims=True)


def score_call(phase, plan, count, a_list, b_list, state):
    slots = len(a_list)
    row_type = jax.ShapeDtypeStruct((8, SHARD, 128), jnp.float32)
    col_type = jax.ShapeDtypeStruct((16, 8, SHARD), jnp.float32)
    quarter = jax.ShapeDtypeStruct((4, SHARD), jnp.float32)
    scratch = [VMEM((8, SHARD, D), jnp.bfloat16), VMEM((16, D, SHARD), jnp.bfloat16)]
    if phase < 2:
        outs = (row_type, col_type)
    else:
        outs = (quarter,) * 4 + (jax.ShapeDtypeStruct((8, SHARD), jnp.float32),)
        scratch = [VMEM(row_type.shape, jnp.float32), VMEM(col_type.shape, jnp.float32)] + scratch
    operands = list(a_list) + list(b_list) + list(state)
    flops = (len(TABLES[phase]) // 4) * 2 * SHARD * SHARD * D
    return pl.pallas_call(
        functools.partial(score_kernel, phase, slots),
        out_shape=outs,
        in_specs=[spec(SMEM), spec(SMEM)] + [spec(VMEM)] * len(operands),
        out_specs=(spec(VMEM),) * len(outs),
        scratch_shapes=scratch,
        compiler_params=pltpu.CompilerParams(vmem_limit_bytes=VMEM_LIMIT),
        cost_estimate=pl.CostEstimate(flops=flops, bytes_accessed=8000000, transcendentals=0),
    )(plan, count, *operands)


def exchange(x, mask):
    return lax.ppermute(x, ("row", "col"), [(s, s ^ mask) for s in range(128)])


def body(embeddings, block_cluster):
    here = (lax.axis_index("row") * 16 + lax.axis_index("col")).astype(jnp.int32).reshape(1)
    unit, flat = unit_call(embeddings)
    own, plan, count = self_call(here, block_cluster, jnp.asarray(TABLE), unit, flat)
    rows, cols, others = [unit], [flat], [exchange(flat, CORE)]
    state = ()
    for phase, slots in enumerate(((1, 2, 3), (4, 5, 6), (7,))):
        for slot in slots:
            source, mask = R_SENDS[slot - 1]
            rows.append(exchange(rows[source], mask))
            source, mask = C_SENDS[slot - 1]
            cols.append(exchange(cols[source], mask))
        for slot in slots:
            others.append(exchange(cols[slot], CORE))
        state = score_call(phase, plan, count, rows, cols + others, state)
    row_lo, row_hi, col_lo, col_hi, other = state
    other = exchange(other, CORE)
    col_lo = jnp.maximum(col_lo, other[:4])
    col_hi = jnp.maximum(col_hi, other[4:])
    row_lo = jnp.maximum(row_lo, exchange(row_hi, Y1))
    col_lo = jnp.maximum(col_lo, exchange(col_hi, Z1))
    row_lo = jnp.maximum(row_lo[:2], exchange(row_lo[2:], X3))
    col_lo = jnp.maximum(col_lo[:2], exchange(col_lo[2:], Z3))
    row_lo = jnp.maximum(row_lo[:1], exchange(row_lo[1:], X1))
    col_lo = jnp.maximum(col_lo[:1], exchange(col_lo[1:], Y3))
    return jnp.maximum(own, jnp.maximum(row_lo, col_lo)).reshape(SHARD)


def solution(mesh):
    placed = (P(("row", "col"), None), P())
    return jax.shard_map(
        body, mesh=mesh, in_specs=placed, out_specs=P(("row", "col")), check_vma=False
    )
```

```python
import functools

import jax
import jax.numpy as jnp
import numpy as np
from jax import lax
from jax.experimental import pallas as pl
from jax.experimental.pallas import tpu as pltpu
from jax.sharding import PartitionSpec as P

BLK = 256
SHARD = 512
D = 384
GROUP = 4
VMEM_LIMIT = 40 * 1024 * 1024

CORE = 16
X1, X3, Y1, Y3, Z1, Z3 = 32, 96, 4, 12, 1, 3
GENERATORS = ((X1, X3, Y1), (Y3, Z1, Z3))
SLOTS = ((), (0,), (1,), (2,), (0, 1), (1, 2), (2, 0), (0, 1, 2))
SENDS = ((0, 0), (0, 1), (0, 2), (1, 1), (2, 2), (3, 0), (5, 0))
PHASES = ((1, 2, 3), (4, 5, 6), (7,))


def mask_of(core, slot):
    mask = 0
    for generator in SLOTS[slot]:
        mask ^= GENERATORS[core][generator]
    return mask


def make_table():
    tables = []
    for core in range(2):
        for slots in PHASES:
            for i in slots:
                for j in range(i + 1):
                    a, b = mask_of(core, i), mask_of(1 - core, j)
                    code = 2 * (i - slots[0]) | (2 * j) << 4
                    bit = (a ^ b) & -(a ^ b)
                    if j < i or core == 0:
                        tables.append((code, a, b, 0, core, 1))
                    if j < i or core == 1:
                        tables.append((code, a, b, bit, (i + j) % 2, 0))
    return np.array(tables, np.int32).reshape(2, -1, 6)


TABLE = make_table()
COUNTS = [sum(2 * i + 1 for i in slots) for slots in PHASES]
STARTS = [0, COUNTS[0], COUNTS[0] + COUNTS[1], sum(COUNTS)]
ITEMS = STARTS[3]
STRIDE = ITEMS + GROUP
VMEM = pltpu.VMEM
SMEM = pltpu.SMEM


def spec(space):
    return pl.BlockSpec(memory_space=space)


def params():
    return pltpu.CompilerParams(vmem_limit_bytes=VMEM_LIMIT)


def unit_kernel(here_ref, own_ref, other_ref, out_ref):
    core = (here_ref[0] >> 4) & 1
    for ref, half in ((own_ref, core), (other_ref, 1 - core)):
        values = ref[...].astype(jnp.float32)
        squares = jnp.sum(values * values, axis=1, keepdims=True)
        out_ref[half] = (values * lax.rsqrt(squares + 1e-06)).astype(jnp.bfloat16)


def unit_call(here, own, other):
    return pl.pallas_call(
        unit_kernel,
        out_shape=jax.ShapeDtypeStruct((2, SHARD, D), jnp.bfloat16),
        in_specs=[spec(SMEM), spec(VMEM), spec(VMEM)],
        out_specs=spec(VMEM),
        compiler_params=params(),
        cost_estimate=pl.CostEstimate(flops=1000000, bytes_accessed=1600000, transcendentals=1024),
    )(here, own, other)


def dot(a, b):
    return lax.dot_general(a, b, (((1,), (1,)), ((), ())), preferred_element_type=jnp.float32)


def self_kernel(here_ref, cluster_ref, table_ref, unit_ref, own_ref, full_ref, part_ref, count_ref):
    here = here_ref[0]
    core = (here >> 4) & 1
    for phase in range(3):
        first = STARTS[phase] + GROUP * phase

        def candidate(n, counts):
            full, part = counts
            entry = 6 * (core * ITEMS + n)
            side = jnp.where((here & table_ref[entry + 3]) != 0, 1, 0) ^ table_ref[entry + 4]
            far = side ^ table_ref[entry + 5]
            a = 2 * (((here ^ table_ref[entry + 1]) & ~CORE) | (side << 4))
            b = 2 * (((here ^ table_ref[entry + 2]) & ~CORE) | (far << 4))
            code = table_ref[entry] + side + (far << 4)
            a0, a1 = cluster_ref[a], cluster_ref[a + 1]
            b0, b1 = cluster_ref[b], cluster_ref[b + 1]
            quads = (
                jnp.where(a0 == b0, 1, 0)
                + jnp.where(a0 == b1, 2, 0)
                + jnp.where(a1 == b0, 4, 0)
                + jnp.where(a1 == b1, 8, 0)
            )
            full_ref[first + full] = code
            part_ref[first + part] = code | (quads << 8)
            return (
                full + jnp.where(quads == 15, 1, 0),
                part + jnp.where((quads != 0) & (quads != 15), 1, 0),
            )

        end = STARTS[phase + 1] - (1 if phase == 2 else 0)
        full, part = lax.fori_loop(STARTS[phase], end, candidate, (jnp.int32(0), jnp.int32(0)))
        last = full_ref[first + jnp.maximum(full - 1, 0)]
        for n in range(GROUP - 1):
            full_ref[first + full + n] = last
        count_ref[2 * phase] = full
        count_ref[2 * phase + 1] = part
        if phase == 2:
            first = STARTS[3] + 3 * GROUP
            full, part = candidate(STARTS[3] - 1, (jnp.int32(0), jnp.int32(0)))
            count_ref[6] = full
            count_ref[7] = part

    first0 = cluster_ref[2 * here]
    first1 = cluster_ref[2 * here + 1]
    there = here ^ CORE
    second0 = cluster_ref[2 * there]
    second1 = cluster_ref[2 * there + 1]
    mine = unit_ref[core]
    best = jnp.full((8, SHARD), -2.0, jnp.float32)
    col = lax.broadcasted_iota(jnp.int32, (BLK, SHARD), 1)
    row = lax.broadcasted_iota(jnp.int32, (BLK, SHARD), 0)
    label = jnp.where(col[:1] < BLK, first0, first1)
    for half, name in ((0, first0), (1, first1)):
        scores = dot(unit_ref[core, half * BLK : half * BLK + BLK, :], mine)
        keep = (row + half * BLK != col) & (label == name)
        scores = jnp.where(keep, scores, jnp.float32(-2.0))
        best = jnp.maximum(best, jnp.max(scores.reshape(BLK // 8, 8, SHARD), axis=0))
    for half, name in ((0, second0), (1, second1)):
        scores = dot(unit_ref[1 - core, half * BLK : half * BLK + BLK, :], mine)
        scores = jnp.where(label == name, scores, jnp.float32(-2.0))
        best = jnp.maximum(best, jnp.max(scores.reshape(BLK // 8, 8, SHARD), axis=0))
    own_ref[...] = jnp.max(best, axis=0, keepdims=True)


def self_call(here, cluster, table, unit):
    lists = jax.ShapeDtypeStruct((ITEMS + 4 * GROUP,), jnp.int32)
    return pl.pallas_call(
        self_kernel,
        out_shape=(
            jax.ShapeDtypeStruct((1, SHARD), jnp.float32),
            lists,
            lists,
            jax.ShapeDtypeStruct((8,), jnp.int32),
        ),
        in_specs=[spec(SMEM), spec(SMEM), spec(SMEM), spec(VMEM)],
        out_specs=(spec(VMEM), spec(SMEM), spec(SMEM), spec(SMEM)),
        compiler_params=params(),
        cost_estimate=pl.CostEstimate(flops=4000000000, bytes_accessed=1000000, transcendentals=0),
    )(here, cluster, table, unit)


def fold(row_ref, col_ref, i, j, rows, cols, scores):
    best = scores[:, :128]
    for k in range(1, scores.shape[1] // 128):
        best = jnp.maximum(best, scores[:, 128 * k : 128 * k + 128])
    row_ref[i, rows, :] = jnp.maximum(row_ref[i, rows, :], best)
    down = jnp.max(scores.reshape(scores.shape[0] // 8, 8, scores.shape[1]), axis=0)
    col_ref[j, :, cols] = jnp.maximum(col_ref[j, :, cols], down)


def score_full(a_ref, b_ref, row_ref, col_ref, word):
    i = word & 15
    j = (word >> 4) & 15
    scores = dot(a_ref[i], b_ref[j])
    fold(row_ref, col_ref, i, j, slice(None), slice(None), scores)


def score_part(a_ref, b_ref, row_ref, col_ref, word):
    i = word & 15
    j = (word >> 4) & 15
    for quad in range(4):

        @pl.when(((word >> (8 + quad)) & 1) == 1)
        def _():
            rows = pl.ds((quad // 2) * BLK, BLK)
            cols = pl.ds((quad % 2) * BLK, BLK)
            scores = dot(a_ref[i, rows, :], b_ref[j, cols, :])
            fold(row_ref, col_ref, i, j, rows, cols, scores)


def score_lists(phase, full_ref, part_ref, count_ref, *refs):
    first = STARTS[phase] + GROUP * phase

    @pl.loop(0, count_ref[2 * phase], step=GROUP)
    def _(n):
        for k in range(GROUP):
            score_full(*refs, full_ref[first + n + k])

    @pl.loop(0, count_ref[2 * phase + 1])
    def _(n):
        score_part(*refs, part_ref[first + n])


def put_rows(out_ref, places, row_ref):
    for n, place in enumerate(places):
        for k in range(SHARD // 128):
            part = row_ref[n, 128 * k : 128 * k + 128, :].T
            out_ref[place : place + 1, 128 * k : 128 * k + 128] = jnp.max(
                part, axis=0, keepdims=True
            )


def score_kernel(phase, full_ref, part_ref, count_ref, *refs):
    slots = PHASES[phase]
    mine, refs = refs[: len(slots)], refs[len(slots) :]
    if phase == 0:
        theirs, refs = refs[:4], refs[4:]
        rows_out, col_ref, a_buf, b_buf, row_ref = refs
        col_ref[...] = jnp.full(col_ref.shape, -2.0, jnp.float32)
    else:
        theirs, refs = refs[:7], refs[7:]
        col_in, rows_out, col_ref, b_buf, a_buf, row_ref = refs
        col_ref[...] = col_in[...]
    row_ref[...] = jnp.full(row_ref.shape, -2.0, jnp.float32)
    for n, ref in enumerate(mine):
        a_buf[2 * n : 2 * n + 2] = ref[...]
    for n, ref in enumerate(theirs):
        b_buf[2 * n : 2 * n + 2] = ref[...]
    score_lists(phase, full_ref, part_ref, count_ref, a_buf, b_buf, row_ref, col_ref)
    put_rows(rows_out, range(2 * len(slots)), row_ref)


def score_call(phase, plan, mine, theirs, state):
    rows = 2 * len(PHASES[phase])
    col_type = jax.ShapeDtypeStruct((16, 8, SHARD), jnp.float32)
    row_type = jax.ShapeDtypeStruct((rows, SHARD), jnp.float32)
    b_type = jax.ShapeDtypeStruct((2 * len(theirs), SHARD, D), jnp.bfloat16)
    outs = (row_type, col_type)
    scratch = [VMEM((rows, SHARD, D), jnp.bfloat16)]
    if phase == 0:
        scratch = scratch + [VMEM(b_type.shape, jnp.bfloat16)]
    else:
        outs = outs + (b_type,)
    scratch = scratch + [VMEM((rows, SHARD, 128), jnp.float32)]
    operands = list(mine) + list(theirs) + list(state)
    flops = (COUNTS[phase] // 2) * 2 * SHARD * SHARD * D
    return pl.pallas_call(
        functools.partial(score_kernel, phase),
        out_shape=outs,
        in_specs=[spec(SMEM)] * 3 + [spec(VMEM)] * len(operands),
        out_specs=(spec(VMEM),) * len(outs),
        scratch_shapes=scratch,
        compiler_params=params(),
        cost_estimate=pl.CostEstimate(flops=flops, bytes_accessed=8000000, transcendentals=0),
    )(*plan, *operands)


def late_kernel(full_ref, part_ref, count_ref, mine, b_ref, col_in, row_ref, col_ref):
    row_ref[...] = jnp.full(row_ref.shape, -2.0, jnp.float32)
    col_ref[...] = col_in[...]
    score_lists(2, full_ref, part_ref, count_ref, mine, b_ref, row_ref, col_ref)


def late_call(plan, mine, b_buf, cols):
    outs = (
        jax.ShapeDtypeStruct((2, SHARD, 128), jnp.float32),
        jax.ShapeDtypeStruct((16, 8, SHARD), jnp.float32),
    )
    return pl.pallas_call(
        late_kernel,
        out_shape=outs,
        in_specs=[spec(SMEM)] * 3 + [spec(VMEM)] * 3,
        out_specs=(spec(VMEM),) * 2,
        compiler_params=params(),
        cost_estimate=pl.CostEstimate(
            flops=(COUNTS[2] // 2) * 2 * SHARD * SHARD * D, bytes_accessed=8000000, transcendentals=0
        ),
    )(*plan, mine, b_buf, cols)


KEPT = (0, 1, 2, 4)
SENT = (3, 6, 5, 7)


def last_kernel(
    full_ref, part_ref, count_ref, mine, theirs, row_in, col_in, rows0, rows1, keep_ref, send_ref, other_ref, row_ref, col_ref
):
    row_ref[...] = row_in[...]
    col_ref[...] = col_in[14:16]
    first = STARTS[3] + 3 * GROUP

    @pl.when(count_ref[6] != 0)
    def _():
        score_full(mine, theirs, row_ref, col_ref, full_ref[first] & 31)

    @pl.when(count_ref[7] != 0)
    def _():
        score_part(mine, theirs, row_ref, col_ref, part_ref[first] & ~224)

    keep_ref[0:2] = jnp.full((2, SHARD), -2.0, jnp.float32)
    for out_ref, slots in ((keep_ref, KEPT), (send_ref, SENT)):
        for place, slot in enumerate(slots):
            if slot in PHASES[0]:
                n = 2 * (slot - PHASES[0][0])
                out_ref[2 * place : 2 * place + 2] = rows0[n : n + 2]
            elif slot in PHASES[1]:
                n = 2 * (slot - PHASES[1][0])
                out_ref[2 * place : 2 * place + 2] = rows1[n : n + 2]
    put_rows(send_ref, (6, 7), row_ref)
    for place, slot in enumerate(KEPT + SENT):
        for half in range(2):
            ref, n = (col_ref, half) if slot == 7 else (col_in, 2 * slot + half)
            at = 2 * place + half
            other_ref[at : at + 1, :] = jnp.max(ref[n], axis=0, keepdims=True)


def last_call(plan, mine, theirs, rows2, cols, rows0, rows1):
    eight = jax.ShapeDtypeStruct((8, SHARD), jnp.float32)
    outs = (eight, eight, jax.ShapeDtypeStruct((16, SHARD), jnp.float32))
    return pl.pallas_call(
        last_kernel,
        out_shape=outs,
        in_specs=[spec(SMEM)] * 3 + [spec(VMEM)] * 6,
        out_specs=(spec(VMEM),) * 3,
        scratch_shapes=[VMEM((2, SHARD, 128), jnp.float32), VMEM((2, 8, SHARD), jnp.float32)],
        compiler_params=params(),
        cost_estimate=pl.CostEstimate(
            flops=2 * SHARD * SHARD * D, bytes_accessed=8000000, transcendentals=0
        ),
    )(*plan, mine, theirs, rows2, cols, rows0, rows1)


def swap(x):
    return lax.ppermute(x, ("row", "col"), [(s, s ^ CORE) for s in range(128)])


def exchange(x, generator):
    pairs = [(s, s ^ GENERATORS[(s >> 4) & 1][generator]) for s in range(128)]
    return lax.ppermute(x, ("row", "col"), pairs)


def body(embeddings, block_cluster):
    here = (lax.axis_index("row") * 16 + lax.axis_index("col")).astype(jnp.int32).reshape(1)
    unit = unit_call(here, embeddings, swap(embeddings))
    own, *plan = self_call(here, block_cluster, jnp.asarray(TABLE.reshape(-1)), unit)
    mine, theirs = [unit], [unit]
    for slot, (source, generator) in enumerate(SENDS, 1):
        mine.append(exchange(mine[source], generator))
        theirs.append(swap(mine[slot]))
    rows0, cols = score_call(0, plan, mine[1:4], theirs[:4], ())
    rows1, cols, b_buf = score_call(1, plan, mine[4:7], theirs[:7], (cols,))
    rows2, cols = late_call(plan, mine[7], b_buf, cols)
    keep, send, other = last_call(plan, mine[7], theirs[7], rows2, cols, rows0, rows1)
    other = swap(other)
    keep = jnp.maximum(keep, other[:8])
    send = jnp.maximum(send, other[8:])
    keep = jnp.maximum(keep, exchange(send, 2))
    keep = jnp.maximum(keep[:4], exchange(keep[4:], 1))
    keep = jnp.maximum(keep[:2], exchange(keep[2:], 0))
    second = (here & CORE) != 0
    ours = jnp.where(second, keep[1], keep[0])
    other = swap(jnp.where(second, keep[0], keep[1]))
    return jnp.maximum(own.reshape(SHARD), jnp.maximum(ours, other))


def solution(mesh):
    placed = (P(("row", "col"), None), P())
    return jax.shard_map(
        body, mesh=mesh, in_specs=placed, out_specs=P(("row", "col")), check_vma=False
    )
```

```python
import functools

import jax
import jax.numpy as jnp
import numpy as np
from jax import lax
from jax.experimental import pallas as pl
from jax.experimental.pallas import tpu as pltpu
from jax.sharding import PartitionSpec as P

BLK = 256
SHARD = 512
D = 384
GROUP = 4
VMEM_LIMIT = 40 * 1024 * 1024

CORE = 16
X1, X3, Y1, Y3, Z1, Z3 = 32, 96, 4, 12, 1, 3
GENERATORS = ((X1, X3, Y1), (Y3, Z1, Z3))
SLOTS = ((), (0,), (1,), (2,), (0, 1), (1, 2), (2, 0), (0, 1, 2))
SENDS = ((0, 0), (0, 1), (0, 2), (1, 1), (2, 2), (3, 0))
HALVES = ((5, 0), (6, 1))
PHASES = (((1, 2, 3), 0, 4, 4), ((4, 5, 6), 0, 4, 4), ((4, 5, 6), 4, 7, 4), ((7,), 0, 7, 4), ((7,), 7, 8, 1))


def mask_of(core, slot):
    mask = 0
    for generator in SLOTS[slot]:
        mask ^= GENERATORS[core][generator]
    return mask


def make_table():
    tables = []
    for core in range(2):
        for slots, low, high, _ in PHASES:
            for i in slots:
                for j in range(low, min(i + 1, high)):
                    a, b = mask_of(core, i), mask_of(1 - core, j)
                    code = 2 * (i - slots[0]) | (2 * (j if low < 7 else 0)) << 4
                    bit = (a ^ b) & -(a ^ b)
                    if j < i or core == 0:
                        tables.append((code, a, b, 0, core, 1))
                    if j < i or core == 1:
                        tables.append((code, a, b, bit, (i + j) % 2, 0))
    return np.array(tables, np.int32).reshape(2, -1, 6)


TABLE = make_table()
COUNTS = [
    sum(2 if j < i else 1 for i in slots for j in range(low, min(i + 1, high)))
    for slots, low, high, _ in PHASES
]
STARTS = [sum(COUNTS[:n]) for n in range(len(PHASES) + 1)]
ITEMS = STARTS[-1]
LISTS = ITEMS + GROUP * len(PHASES)
VMEM = pltpu.VMEM
SMEM = pltpu.SMEM


def spec(space):
    return pl.BlockSpec(memory_space=space)


def params():
    return pltpu.CompilerParams(vmem_limit_bytes=VMEM_LIMIT)


def unit_of(x):
    values = x.astype(jnp.float32)
    squares = jnp.sum(values * values, axis=1, keepdims=True)
    return (values * lax.rsqrt(squares + 1e-06)).astype(jnp.bfloat16)


def own_kernel(x_ref, out_ref):
    out_ref[...] = unit_of(x_ref[...])


def pair_kernel(here_ref, own_ref, other_ref, out_ref):
    core = (here_ref[0] >> 4) & 1
    out_ref[core] = own_ref[...]
    out_ref[1 - core] = unit_of(other_ref[...])


def unit_call(here, x, other):
    cost = pl.CostEstimate(flops=1000000, bytes_accessed=1600000, transcendentals=512)
    own = pl.pallas_call(
        own_kernel,
        out_shape=jax.ShapeDtypeStruct((SHARD, D), jnp.bfloat16),
        in_specs=[spec(VMEM)],
        out_specs=spec(VMEM),
        compiler_params=params(),
        cost_estimate=cost,
    )(x)
    return pl.pallas_call(
        pair_kernel,
        out_shape=jax.ShapeDtypeStruct((2, SHARD, D), jnp.bfloat16),
        in_specs=[spec(SMEM), spec(VMEM), spec(VMEM)],
        out_specs=spec(VMEM),
        compiler_params=params(),
        cost_estimate=cost,
    )(here, own, other)


def dot(a, b):
    return lax.dot_general(a, b, (((1,), (1,)), ((), ())), preferred_element_type=jnp.float32)


def self_kernel(here_ref, cluster_ref, table_ref, unit_ref, own_ref, full_ref, part_ref, count_ref):
    here = here_ref[0]
    core = (here >> 4) & 1
    for phase in range(len(PHASES)):
        first = STARTS[phase] + GROUP * phase

        def candidate(n, counts):
            full, part = counts
            entry = 6 * (core * ITEMS + n)
            side = jnp.where((here & table_ref[entry + 3]) != 0, 1, 0) ^ table_ref[entry + 4]
            far = side ^ table_ref[entry + 5]
            a = 2 * (((here ^ table_ref[entry + 1]) & ~CORE) | (side << 4))
            b = 2 * (((here ^ table_ref[entry + 2]) & ~CORE) | (far << 4))
            code = table_ref[entry] + side + (far << 4)
            a0, a1 = cluster_ref[a], cluster_ref[a + 1]
            b0, b1 = cluster_ref[b], cluster_ref[b + 1]
            quads = (
                jnp.where(a0 == b0, 1, 0)
                + jnp.where(a0 == b1, 2, 0)
                + jnp.where(a1 == b0, 4, 0)
                + jnp.where(a1 == b1, 8, 0)
            )
            full_ref[first + full] = code
            part_ref[first + part] = code | (quads << 8)
            return (
                full + jnp.where(quads == 15, 1, 0),
                part + jnp.where((quads != 0) & (quads != 15), 1, 0),
            )

        full, part = lax.fori_loop(
            STARTS[phase], STARTS[phase + 1], candidate, (jnp.int32(0), jnp.int32(0))
        )
        last = full_ref[first + jnp.maximum(full - 1, 0)]
        for n in range(GROUP - 1):
            full_ref[first + full + n] = last
        count_ref[2 * phase] = full
        count_ref[2 * phase + 1] = part

    first0 = cluster_ref[2 * here]
    first1 = cluster_ref[2 * here + 1]
    there = here ^ CORE
    second0 = cluster_ref[2 * there]
    second1 = cluster_ref[2 * there + 1]
    mine = unit_ref[core]
    best = jnp.full((8, SHARD), -2.0, jnp.float32)
    col = lax.broadcasted_iota(jnp.int32, (BLK, SHARD), 1)
    row = lax.broadcasted_iota(jnp.int32, (BLK, SHARD), 0)
    label = jnp.where(col[:1] < BLK, first0, first1)
    for half, name in ((0, first0), (1, first1)):
        scores = dot(unit_ref[core, half * BLK : half * BLK + BLK, :], mine)
        keep = (row + half * BLK != col) & (label == name)
        scores = jnp.where(keep, scores, jnp.float32(-2.0))
        best = jnp.maximum(best, jnp.max(scores.reshape(BLK // 8, 8, SHARD), axis=0))
    for half, name in ((0, second0), (1, second1)):
        scores = dot(unit_ref[1 - core, half * BLK : half * BLK + BLK, :], mine)
        scores = jnp.where(label == name, scores, jnp.float32(-2.0))
        best = jnp.maximum(best, jnp.max(scores.reshape(BLK // 8, 8, SHARD), axis=0))
    own_ref[...] = jnp.max(best, axis=0, keepdims=True)


def self_call(here, cluster, table, unit):
    lists = jax.ShapeDtypeStruct((LISTS,), jnp.int32)
    return pl.pallas_call(
        self_kernel,
        out_shape=(
            jax.ShapeDtypeStruct((1, SHARD), jnp.float32),
            lists,
            lists,
            jax.ShapeDtypeStruct((2 * len(PHASES),), jnp.int32),
        ),
        in_specs=[spec(SMEM), spec(SMEM), spec(SMEM), spec(VMEM)],
        out_specs=(spec(VMEM), spec(SMEM), spec(SMEM), spec(SMEM)),
        compiler_params=params(),
        cost_estimate=pl.CostEstimate(flops=4000000000, bytes_accessed=1000000, transcendentals=0),
    )(here, cluster, table, unit)


def fold(row_ref, col_ref, i, j, rows, cols, scores):
    best = scores[:, :128]
    for k in range(1, scores.shape[1] // 128):
        best = jnp.maximum(best, scores[:, 128 * k : 128 * k + 128])
    row_ref[i, rows, :] = jnp.maximum(row_ref[i, rows, :], best)
    down = jnp.max(scores.reshape(scores.shape[0] // 8, 8, scores.shape[1]), axis=0)
    col_ref[j, :, cols] = jnp.maximum(col_ref[j, :, cols], down)


def score_full(a_ref, b_ref, row_ref, col_ref, word):
    i = word & 15
    j = (word >> 4) & 15
    scores = dot(a_ref[i], b_ref[j])
    fold(row_ref, col_ref, i, j, slice(None), slice(None), scores)


def score_part(a_ref, b_ref, row_ref, col_ref, word):
    i = word & 15
    j = (word >> 4) & 15
    for quad in range(4):

        @pl.when(((word >> (8 + quad)) & 1) == 1)
        def _():
            rows = pl.ds((quad // 2) * BLK, BLK)
            cols = pl.ds((quad % 2) * BLK, BLK)
            scores = dot(a_ref[i, rows, :], b_ref[j, cols, :])
            fold(row_ref, col_ref, i, j, rows, cols, scores)


def score_lists(phase, full_ref, part_ref, count_ref, *refs):
    first = STARTS[phase] + GROUP * phase
    group = PHASES[phase][3]

    @pl.loop(0, count_ref[2 * phase], step=group)
    def _(n):
        for k in range(group):
            score_full(*refs, full_ref[first + n + k])

    @pl.loop(0, count_ref[2 * phase + 1])
    def _(n):
        score_part(*refs, part_ref[first + n])


def put_rows(out_ref, place, row_ref, first):
    for half in range(2):
        at = place + half
        for k in range(SHARD // 128):
            part = row_ref[first + half, 128 * k : 128 * k + 128, :].T
            out_ref[at : at + 1, 128 * k : 128 * k + 128] = jnp.max(part, axis=0, keepdims=True)


def score_kernel(phase, full_ref, part_ref, count_ref, *refs):
    slots, low, high, _ = PHASES[phase]
    mine, refs = refs[: len(slots)], refs[len(slots) :]
    if phase == 0:
        theirs, refs = refs[:high], refs[high:]
        row_ref, col_ref, b_buf, a_buf = refs
        row_ref[...] = jnp.full(row_ref.shape, -2.0, jnp.float32)
        col_ref[...] = jnp.full(col_ref.shape, -2.0, jnp.float32)
    elif phase == 1:
        b_buf, col_in, row_ref, col_ref, a_buf = refs
        theirs = ()
        row_ref[...] = jnp.full(row_ref.shape, -2.0, jnp.float32)
        col_ref[...] = col_in[...]
    else:
        theirs, refs = refs[: high - low], refs[high - low :]
        b_in, col_in, row_in, row_ref, col_ref, b_buf, a_buf = refs
        b_buf[: 2 * low] = b_in[...]
        row_ref[...] = row_in[...]
        col_ref[...] = col_in[...]
    for n, ref in enumerate(mine):
        a_buf[2 * n : 2 * n + 2] = ref[...]
    for n, ref in enumerate(theirs, low):
        b_buf[2 * n : 2 * n + 2] = ref[...]
    score_lists(phase, full_ref, part_ref, count_ref, a_buf, b_buf, row_ref, col_ref)


ROWS = jax.ShapeDtypeStruct((6, SHARD, 128), jnp.float32)
COLS = jax.ShapeDtypeStruct((14, 8, SHARD), jnp.float32)


def score_call(phase, plan, mine, theirs, state):
    outs = (ROWS, COLS)
    if phase != 1:
        outs = outs + (jax.ShapeDtypeStruct((2 * PHASES[phase][2], SHARD, D), jnp.bfloat16),)
    operands = list(plan) + list(mine) + list(theirs) + list(state)
    return pl.pallas_call(
        functools.partial(score_kernel, phase),
        out_shape=outs,
        in_specs=[spec(SMEM)] * 3 + [spec(VMEM)] * (len(operands) - 3),
        out_specs=(spec(VMEM),) * len(outs),
        scratch_shapes=[VMEM((6, SHARD, D), jnp.bfloat16)],
        compiler_params=params(),
        cost_estimate=pl.CostEstimate(
            flops=COUNTS[phase] * SHARD * SHARD * D, bytes_accessed=8000000, transcendentals=0
        ),
    )(*operands)


KEPT = (0, 1, 2, 4)
SENT = (3, 6, 5, 7)


def last_kernel(full_ref, part_ref, count_ref, *refs):
    plan, mine, theirs, refs = (full_ref, part_ref, count_ref), refs[:2], refs[2:4], refs[4:]
    b_buf, col_in, rows0, rows1, keep_ref, send_ref, other_ref, refs = *refs[:7], refs[7:]
    a_buf, b_last, row_ref, col_ref, col_last = refs
    row_ref[...] = jnp.full(row_ref.shape, -2.0, jnp.float32)
    col_ref[...] = col_in[...]
    col_last[...] = jnp.full(col_last.shape, -2.0, jnp.float32)
    for half in range(2):
        a_buf[half] = mine[half][...]
        b_last[half] = theirs[half][...]
    score_lists(3, *plan, a_buf, b_buf, row_ref, col_ref)
    score_lists(4, *plan, a_buf, b_last, row_ref, col_last)
    keep_ref[0:2] = jnp.full((2, SHARD), -2.0, jnp.float32)
    for out_ref, slots in ((keep_ref, KEPT), (send_ref, SENT)):
        for place, slot in enumerate(slots):
            if slot == 7:
                put_rows(out_ref, 2 * place, row_ref, 0)
            elif slot > 3:
                put_rows(out_ref, 2 * place, rows1, 2 * slot - 8)
            elif slot > 0:
                put_rows(out_ref, 2 * place, rows0, 2 * slot - 2)
    for place, slot in enumerate(KEPT + SENT):
        for half in range(2):
            at = 2 * place + half
            down = col_last[half] if slot == 7 else col_ref[2 * slot + half]
            other_ref[at : at + 1, :] = jnp.max(down, axis=0, keepdims=True)


def last_call(plan, mine, theirs, state):
    eight = jax.ShapeDtypeStruct((8, SHARD), jnp.float32)
    outs = (eight, eight, jax.ShapeDtypeStruct((16, SHARD), jnp.float32))
    operands = list(plan) + list(mine) + list(theirs) + list(state)
    return pl.pallas_call(
        last_kernel,
        out_shape=outs,
        in_specs=[spec(SMEM)] * 3 + [spec(VMEM)] * (len(operands) - 3),
        out_specs=(spec(VMEM),) * 3,
        scratch_shapes=[
            VMEM((2, SHARD, D), jnp.bfloat16),
            VMEM((2, SHARD, D), jnp.bfloat16),
            VMEM((2, SHARD, 128), jnp.float32),
            VMEM(COLS.shape, jnp.float32),
            VMEM((2, 8, SHARD), jnp.float32),
        ],
        compiler_params=params(),
        cost_estimate=pl.CostEstimate(
            flops=COUNTS[3] * SHARD * SHARD * D, bytes_accessed=8000000, transcendentals=0
        ),
    )(*operands)


def swap(x):
    return lax.ppermute(x, ("row", "col"), [(s, s ^ CORE) for s in range(128)])


def exchange(x, generator):
    pairs = [(s, s ^ GENERATORS[(s >> 4) & 1][generator]) for s in range(128)]
    return lax.ppermute(x, ("row", "col"), pairs)


def after(x, *done):
    return lax.optimization_barrier((x, *done))[0]


def body(embeddings, block_cluster):
    here = (lax.axis_index("row") * 16 + lax.axis_index("col")).astype(jnp.int32).reshape(1)
    unit = unit_call(here, embeddings, swap(embeddings))
    own, *plan = self_call(here, block_cluster, jnp.asarray(TABLE.reshape(-1)), unit)
    mine, theirs = [unit], [unit]
    for slot in (1, 2, 3):
        source, generator = SENDS[slot - 1]
        mine.append(after(exchange(mine[source], generator), own))
        theirs.append(swap(mine[slot]))
    rows0, cols, b_buf = score_call(0, plan, mine[1:4], theirs[:4], ())
    for slot in (4, 5, 6):
        source, generator = SENDS[slot - 1]
        mine.append(after(exchange(mine[source], generator), cols))
        theirs.append(swap(mine[slot]))
    rows1, cols = score_call(1, plan, mine[4:7], (), (b_buf, cols))
    halves = [
        after(exchange(mine[source][half], generator), cols)
        for half, (source, generator) in enumerate(HALVES)
    ]
    swapped = [swap(x) for x in halves]
    rows1, cols, b_buf = score_call(2, plan, mine[4:7], theirs[4:7], (b_buf, cols, rows1))
    keep, send, other = last_call(plan, halves, swapped, (b_buf, cols, rows0, rows1))
    other = swap(other)
    keep = jnp.maximum(keep, other[:8])
    send = jnp.maximum(send, other[8:])
    keep = jnp.maximum(keep, exchange(send, 2))
    keep = jnp.maximum(keep[:4], exchange(keep[4:], 1))
    keep = jnp.maximum(keep[:2], exchange(keep[2:], 0))
    second = (here & CORE) != 0
    ours = jnp.where(second, keep[1], keep[0])
    other = swap(jnp.where(second, keep[0], keep[1]))
    return jnp.maximum(own.reshape(SHARD), jnp.maximum(ours, other))


def solution(mesh):
    placed = (P(("row", "col"), None), P())
    return jax.shard_map(
        body, mesh=mesh, in_specs=placed, out_specs=P(("row", "col")), check_vma=False
    )
```

```python
import functools

import jax
import jax.numpy as jnp
import numpy as np
from jax import lax
from jax.experimental import pallas as pl
from jax.experimental.pallas import tpu as pltpu
from jax.sharding import PartitionSpec as P

BLK = 256
SHARD = 512
D = 384
GROUP = 4
VMEM_LIMIT = 20 * 1024 * 1024

CORE = 16
X1, X3, Y1, Y3, Z1, Z3 = 32, 96, 4, 12, 1, 3
GENERATORS = ((X1, X3, Y1), (Y3, Z1, Z3))
SLOTS = ((), (0,), (1,), (2,), (0, 1), (1, 2), (2, 0), (0, 1, 2))
SENDS = ((0, 0), (0, 1), (0, 2), (1, 1), (2, 2), (3, 0))
HALVES = ((5, 0), (6, 1))
PHASES = (
    ((1, 2, 3), 0, 4, 4),
    ((4, 5, 6), 0, 4, 4),
    ((4, 5, 6), 4, 7, 4),
    ((7,), 0, 4, 4),
    ((7,), 4, 7, 4),
    ((7,), 7, 8, 1),
)


def mask_of(core, slot):
    mask = 0
    for generator in SLOTS[slot]:
        mask ^= GENERATORS[core][generator]
    return mask


def make_table():
    tables = []
    for core in range(2):
        for slots, low, high, _ in PHASES:
            for i in slots:
                for j in range(low, min(i + 1, high)):
                    a, b = mask_of(core, i), mask_of(1 - core, j)
                    code = 2 * (i - slots[0]) | (2 * (j - low)) << 4
                    bit = (a ^ b) & -(a ^ b)
                    if j < i or core == 0:
                        tables.append((code, a, b, 0, core, 1))
                    if j < i or core == 1:
                        tables.append((code, a, b, bit, (i + j) % 2, 0))
    return np.array(tables, np.int32).reshape(2, -1, 6)


TABLE = make_table()
COUNTS = [
    sum(2 if j < i else 1 for i in slots for j in range(low, min(i + 1, high)))
    for slots, low, high, _ in PHASES
]
STARTS = [sum(COUNTS[:n]) for n in range(len(PHASES) + 1)]
ITEMS = STARTS[-1]
LISTS = ITEMS + GROUP * len(PHASES)
VMEM = pltpu.VMEM
SMEM = pltpu.SMEM


def spec(space):
    return pl.BlockSpec(memory_space=space)


def params():
    return pltpu.CompilerParams(vmem_limit_bytes=VMEM_LIMIT)


def unit_of(x):
    values = x.astype(jnp.float32)
    squares = jnp.sum(values * values, axis=1, keepdims=True)
    return (values * lax.rsqrt(squares + 1e-06)).astype(jnp.bfloat16)


def first_kernel(x_ref, out_ref):
    out_ref[...] = unit_of(x_ref[...])


def pair_kernel(here_ref, own_ref, other_ref, out_ref):
    core = (here_ref[0] >> 4) & 1
    out_ref[core] = own_ref[...]
    out_ref[1 - core] = unit_of(other_ref[...])


def unit_call(here, x, other):
    cost = pl.CostEstimate(flops=1000000, bytes_accessed=1600000, transcendentals=512)
    own = pl.pallas_call(
        first_kernel,
        out_shape=jax.ShapeDtypeStruct((SHARD, D), jnp.bfloat16),
        in_specs=[spec(VMEM)],
        out_specs=spec(VMEM),
        compiler_params=params(),
        cost_estimate=cost,
    )(x)
    return pl.pallas_call(
        pair_kernel,
        out_shape=jax.ShapeDtypeStruct((2, SHARD, D), jnp.bfloat16),
        in_specs=[spec(SMEM), spec(VMEM), spec(VMEM)],
        out_specs=spec(VMEM),
        compiler_params=params(),
        cost_estimate=cost,
    )(here, own, other)


def dot(a, b):
    return lax.dot_general(a, b, (((1,), (1,)), ((), ())), preferred_element_type=jnp.float32)


def plan_kernel(here_ref, cluster_ref, table_ref, full_ref, part_ref, count_ref):
    here = here_ref[0]
    core = (here >> 4) & 1
    for phase in range(len(PHASES)):
        first = STARTS[phase] + GROUP * phase

        def candidate(n, counts):
            full, part = counts
            entry = 6 * (core * ITEMS + n)
            side = jnp.where((here & table_ref[entry + 3]) != 0, 1, 0) ^ table_ref[entry + 4]
            far = side ^ table_ref[entry + 5]
            a = 2 * (((here ^ table_ref[entry + 1]) & ~CORE) | (side << 4))
            b = 2 * (((here ^ table_ref[entry + 2]) & ~CORE) | (far << 4))
            code = table_ref[entry] + side + (far << 4)
            a0, a1 = cluster_ref[a], cluster_ref[a + 1]
            b0, b1 = cluster_ref[b], cluster_ref[b + 1]
            quads = (
                jnp.where(a0 == b0, 1, 0)
                + jnp.where(a0 == b1, 2, 0)
                + jnp.where(a1 == b0, 4, 0)
                + jnp.where(a1 == b1, 8, 0)
            )
            full_ref[first + full] = code
            part_ref[first + part] = code | (quads << 8)
            return (
                full + jnp.where(quads == 15, 1, 0),
                part + jnp.where((quads != 0) & (quads != 15), 1, 0),
            )

        full, part = lax.fori_loop(
            STARTS[phase], STARTS[phase + 1], candidate, (jnp.int32(0), jnp.int32(0))
        )
        last = full_ref[first + jnp.maximum(full - 1, 0)]
        for n in range(GROUP - 1):
            full_ref[first + full + n] = last
        count_ref[2 * phase] = full
        count_ref[2 * phase + 1] = part


def own_kernel(here_ref, cluster_ref, unit_ref, own_ref):
    here = here_ref[0]
    core = (here >> 4) & 1
    first0 = cluster_ref[2 * here]
    first1 = cluster_ref[2 * here + 1]
    there = here ^ CORE
    second0 = cluster_ref[2 * there]
    second1 = cluster_ref[2 * there + 1]
    mine = unit_ref[core]
    best = jnp.full((8, SHARD), -2.0, jnp.float32)
    col = lax.broadcasted_iota(jnp.int32, (BLK, SHARD), 1)
    row = lax.broadcasted_iota(jnp.int32, (BLK, SHARD), 0)
    label = jnp.where(col[:1] < BLK, first0, first1)
    for half, name in ((0, first0), (1, first1)):
        scores = dot(unit_ref[core, half * BLK : half * BLK + BLK, :], mine)
        keep = (row + half * BLK != col) & (label == name)
        scores = jnp.where(keep, scores, jnp.float32(-2.0))
        best = jnp.maximum(best, jnp.max(scores.reshape(BLK // 8, 8, SHARD), axis=0))
    for half, name in ((0, second0), (1, second1)):
        scores = dot(unit_ref[1 - core, half * BLK : half * BLK + BLK, :], mine)
        scores = jnp.where(label == name, scores, jnp.float32(-2.0))
        best = jnp.maximum(best, jnp.max(scores.reshape(BLK // 8, 8, SHARD), axis=0))
    own_ref[...] = jnp.max(best, axis=0, keepdims=True)


def plan_call(here, cluster, table):
    lists = jax.ShapeDtypeStruct((LISTS,), jnp.int32)
    return pl.pallas_call(
        plan_kernel,
        out_shape=(lists, lists, jax.ShapeDtypeStruct((2 * len(PHASES),), jnp.int32)),
        in_specs=[spec(SMEM)] * 3,
        out_specs=(spec(SMEM),) * 3,
        compiler_params=params(),
        cost_estimate=pl.CostEstimate(flops=3000000000, bytes_accessed=10000, transcendentals=0),
    )(here, cluster, table)


def own_call(here, cluster, unit):
    return pl.pallas_call(
        own_kernel,
        out_shape=jax.ShapeDtypeStruct((1, SHARD), jnp.float32),
        in_specs=[spec(SMEM), spec(SMEM), spec(VMEM)],
        out_specs=spec(VMEM),
        compiler_params=params(),
        cost_estimate=pl.CostEstimate(flops=1000000000, bytes_accessed=1000000, transcendentals=0),
    )(here, cluster, unit)


def fold(row_ref, col_ref, i, j, rows, cols, scores):
    best = scores[:, :128]
    for k in range(1, scores.shape[1] // 128):
        best = jnp.maximum(best, scores[:, 128 * k : 128 * k + 128])
    row_ref[i, rows, :] = jnp.maximum(row_ref[i, rows, :], best)
    down = jnp.max(scores.reshape(scores.shape[0] // 8, 8, scores.shape[1]), axis=0)
    col_ref[j, :, cols] = jnp.maximum(col_ref[j, :, cols], down)


def score_full(a_ref, b_ref, row_ref, col_ref, word):
    i = word & 15
    j = (word >> 4) & 15
    scores = dot(a_ref[i], b_ref[j])
    fold(row_ref, col_ref, i, j, slice(None), slice(None), scores)


def score_part(a_ref, b_ref, row_ref, col_ref, word):
    i = word & 15
    j = (word >> 4) & 15
    for quad in range(4):

        @pl.when(((word >> (8 + quad)) & 1) == 1)
        def _():
            rows = pl.ds((quad // 2) * BLK, BLK)
            cols = pl.ds((quad % 2) * BLK, BLK)
            scores = dot(a_ref[i, rows, :], b_ref[j, cols, :])
            fold(row_ref, col_ref, i, j, rows, cols, scores)


def score_lists(phase, full_ref, part_ref, count_ref, *refs):
    first = STARTS[phase] + GROUP * phase
    group = PHASES[phase][3]

    @pl.loop(0, count_ref[2 * phase], step=group)
    def _(n):
        for k in range(group):
            score_full(*refs, full_ref[first + n + k])

    @pl.loop(0, count_ref[2 * phase + 1])
    def _(n):
        score_part(*refs, part_ref[first + n])


def put_rows(out_ref, place, row_ref, first):
    for half in range(2):
        at = place + half
        for k in range(SHARD // 128):
            part = row_ref[first + half, 128 * k : 128 * k + 128, :].T
            out_ref[at : at + 1, 128 * k : 128 * k + 128] = jnp.max(part, axis=0, keepdims=True)


def clear(*refs):
    for ref in refs:
        ref[...] = jnp.full(ref.shape, -2.0, jnp.float32)


def put(buf, refs):
    for n, ref in enumerate(refs):
        buf[2 * n : 2 * n + 2] = ref[...]


def early_kernel(full_ref, part_ref, count_ref, *refs):
    mine, theirs, (rows_out, col_ref, b_buf, a_buf, row_ref) = refs[:3], refs[3:7], refs[7:]
    clear(row_ref, col_ref)
    put(a_buf, mine)
    put(b_buf, theirs)
    score_lists(0, full_ref, part_ref, count_ref, a_buf, b_buf, row_ref, col_ref)
    for slot in (1, 2, 3):
        put_rows(rows_out, 2 * slot - 2, row_ref, 2 * slot - 2)


def middle_kernel(full_ref, part_ref, count_ref, *refs):
    mine, (b_buf, col_in, row_ref, col_ref, a_buf) = refs[:3], refs[3:]
    clear(row_ref)
    col_ref[...] = col_in[...]
    put(a_buf, mine)
    score_lists(1, full_ref, part_ref, count_ref, a_buf, b_buf, row_ref, col_ref)


ROWS = jax.ShapeDtypeStruct((6, SHARD, 128), jnp.float32)
COLS = jax.ShapeDtypeStruct((8, 8, SHARD), jnp.float32)
PACK = jax.ShapeDtypeStruct((6, SHARD, D), jnp.bfloat16)


def kernel_call(kernel, operands, outs, scratch, flops, smem=3):
    return pl.pallas_call(
        kernel,
        out_shape=outs,
        in_specs=[spec(SMEM)] * smem + [spec(VMEM)] * (len(operands) - smem),
        out_specs=jax.tree.map(lambda _: spec(VMEM), outs),
        scratch_shapes=[VMEM(x.shape, x.dtype) for x in scratch],
        compiler_params=params(),
        cost_estimate=pl.CostEstimate(flops=flops, bytes_accessed=8000000, transcendentals=0),
    )(*operands)


def early_call(plan, mine, theirs):
    buf = jax.ShapeDtypeStruct((8, SHARD, D), jnp.bfloat16)
    outs = (jax.ShapeDtypeStruct((6, SHARD), jnp.float32), COLS, buf)
    return kernel_call(early_kernel, [*plan, *mine, *theirs], outs, [PACK, ROWS], 4000000000)


def middle_call(plan, *operands):
    return kernel_call(middle_kernel, [*plan, *operands], (ROWS, COLS, PACK), [], 5000000000)


KEPT = (0, 1, 2, 4)
SENT = (3, 6, 5, 7)


def last_kernel(full_ref, part_ref, count_ref, *refs):
    plan = (full_ref, part_ref, count_ref)
    theirs, mine7, theirs7, refs = refs[:3], refs[3:5], refs[5:7], refs[7:]
    a_mid, b_low, col_low_in, rows0, row_in, keep_ref, send_ref, other_ref, *refs = refs
    b_mid, a_last, b_last, row_mid, row_last, col_low, col_mid, col_last = refs
    clear(row_last, col_mid, col_last)
    row_mid[...] = row_in[...]
    col_low[...] = col_low_in[...]
    put(b_mid, theirs)
    for half in range(2):
        a_last[half] = mine7[half][...]
        b_last[half] = theirs7[half][...]
    score_lists(2, *plan, a_mid, b_mid, row_mid, col_mid)
    score_lists(3, *plan, a_last, b_low, row_last, col_low)
    score_lists(4, *plan, a_last, b_mid, row_last, col_mid)
    score_lists(5, *plan, a_last, b_last, row_last, col_last)
    keep_ref[0:2] = jnp.full((2, SHARD), -2.0, jnp.float32)
    for out_ref, slots in ((keep_ref, KEPT), (send_ref, SENT)):
        for place, slot in enumerate(slots):
            if slot == 7:
                put_rows(out_ref, 2 * place, row_last, 0)
            elif slot > 3:
                put_rows(out_ref, 2 * place, row_mid, 2 * slot - 8)
            elif slot > 0:
                out_ref[2 * place : 2 * place + 2] = rows0[2 * slot - 2 : 2 * slot]
    for place, slot in enumerate(KEPT + SENT):
        for half in range(2):
            at = 2 * place + half
            if slot == 7:
                down = col_last[half]
            elif slot > 3:
                down = col_mid[2 * slot - 8 + half]
            else:
                down = col_low[2 * slot + half]
            other_ref[at : at + 1, :] = jnp.max(down, axis=0, keepdims=True)


def last_call(plan, *operands):
    def f32(*shape):
        return jax.ShapeDtypeStruct(shape, jnp.float32)

    two = jax.ShapeDtypeStruct((2, SHARD, D), jnp.bfloat16)
    outs = (f32(8, SHARD), f32(8, SHARD), f32(16, SHARD))
    scratch = [PACK, two, two, ROWS, f32(2, SHARD, 128), COLS, f32(6, 8, SHARD), f32(2, 8, SHARD)]
    return kernel_call(last_kernel, [*plan, *operands], outs, scratch, 5000000000)


def swap(x):
    return lax.ppermute(x, ("row", "col"), [(s, s ^ CORE) for s in range(128)])


def exchange(x, generator):
    pairs = [(s, s ^ GENERATORS[(s >> 4) & 1][generator]) for s in range(128)]
    return lax.ppermute(x, ("row", "col"), pairs)


def after(x, *done):
    return lax.optimization_barrier((x, *done))[0]


def body(embeddings, block_cluster):
    here = (lax.axis_index("row") * 16 + lax.axis_index("col")).astype(jnp.int32).reshape(1)
    unit = unit_call(here, embeddings, swap(embeddings))
    plan = plan_call(here, block_cluster, jnp.asarray(TABLE.reshape(-1)))
    mine, theirs = [unit], [unit]

    def step(slots):
        return [exchange(mine[SENDS[k - 1][0]], SENDS[k - 1][1]) for k in slots]

    own = own_call(here, block_cluster, unit)
    mine.extend(after(x, plan[2], own) for x in step((1, 2, 3)))
    theirs.extend(swap(x) for x in mine[1:4])
    rows0, cols, b_low = early_call(plan, mine[1:4], theirs)
    mine.extend(after(x, cols) for x in step((4, 5, 6)))
    halves = [
        exchange(mine[source][half], generator) for half, (source, generator) in enumerate(HALVES)
    ]
    theirs.extend(swap(x) for x in mine[4:7])
    rows1, cols, a_mid = middle_call(plan, *mine[4:7], b_low, cols)
    halves = [after(x, cols) for x in halves]
    swapped = [swap(x) for x in halves]
    keep, send, other = last_call(
        plan, *theirs[4:7], *halves, *swapped, a_mid, b_low, cols, rows0, rows1
    )
    other = swap(other)
    keep = jnp.maximum(keep, other[:8])
    send = jnp.maximum(send, other[8:])
    keep = jnp.maximum(keep, exchange(send, 2))
    keep = jnp.maximum(keep[:4], exchange(keep[4:], 1))
    keep = jnp.maximum(keep[:2], exchange(keep[2:], 0))
    second = (here & CORE) != 0
    ours = jnp.where(second, keep[1], keep[0])
    other = swap(jnp.where(second, keep[0], keep[1]))
    return jnp.maximum(own.reshape(SHARD), jnp.maximum(ours, other))


def solution(mesh):
    placed = (P(("row", "col"), None), P())
    return jax.shard_map(
        body, mesh=mesh, in_specs=placed, out_specs=P(("row", "col")), check_vma=False
    )
```

```python
import functools

import jax
import jax.numpy as jnp
import numpy as np
from jax import lax
from jax.experimental import pallas as pl
from jax.experimental.pallas import tpu as pltpu
from jax.sharding import PartitionSpec as P

BLK = 256
SHARD = 512
D = 384
GROUP = 4
VMEM_LIMIT = 20 * 1024 * 1024

CORE = 16
X1, X3, Y1, Y3, Z1, Z3 = 32, 96, 4, 12, 1, 3
GENERATORS = ((X1, X3, Y1), (Y3, Z1, Z3))
SLOTS = ((), (0,), (1,), (2,), (0, 1), (1, 2), (2, 0), (0, 1, 2))
SENDS = ((0, 0), (0, 1), (0, 2), (1, 1), (2, 2), (3, 0))
HALVES = ((5, 0), (6, 1))
PHASES = (
    ((1, 2, 3), 0, 1, 4),
    ((4, 5, 6), 0, 1, 4),
    ((4, 5, 6), 1, 4, 4),
    ((1, 2, 3), 1, 4, 4),
    ((4, 5, 6), 4, 7, 4),
    ((7,), 0, 1, 1),
    ((7,), 1, 4, 4),
    ((7,), 4, 7, 4),
    ((7,), 7, 8, 1),
)


def mask_of(core, slot):
    mask = 0
    for generator in SLOTS[slot]:
        mask ^= GENERATORS[core][generator]
    return mask


def make_table():
    tables = []
    for core in range(2):
        for slots, low, high, _ in PHASES:
            for i in slots:
                for j in range(low, min(i + 1, high)):
                    a, b = mask_of(core, i), mask_of(1 - core, j)
                    code = 2 * (i - slots[0]) | (2 * (j - low)) << 4
                    bit = (a ^ b) & -(a ^ b)
                    if j < i or core == 0:
                        tables.append((code, a, b, 0, core, 1))
                    if j < i or core == 1:
                        tables.append((code, a, b, bit, (i + j) % 2, 0))
    return np.array(tables, np.int32).reshape(2, -1, 6)


TABLE = make_table()
COUNTS = [
    sum(2 if j < i else 1 for i in slots for j in range(low, min(i + 1, high)))
    for slots, low, high, _ in PHASES
]
STARTS = [sum(COUNTS[:n]) for n in range(len(PHASES) + 1)]
ITEMS = STARTS[-1]
LISTS = ITEMS + GROUP * len(PHASES)
VMEM = pltpu.VMEM
SMEM = pltpu.SMEM


def spec(space):
    return pl.BlockSpec(memory_space=space)


def params():
    return pltpu.CompilerParams(vmem_limit_bytes=VMEM_LIMIT)


def unit_of(x):
    values = x.astype(jnp.float32)
    squares = jnp.sum(values * values, axis=1, keepdims=True)
    return (values * lax.rsqrt(squares + 1e-06)).astype(jnp.bfloat16)


def first_kernel(x_ref, out_ref):
    out_ref[...] = unit_of(x_ref[...])


def pair_kernel(here_ref, own_ref, other_ref, out_ref):
    core = (here_ref[0] >> 4) & 1
    out_ref[core] = own_ref[...]
    out_ref[1 - core] = unit_of(other_ref[...])


def unit_call(here, x, other):
    cost = pl.CostEstimate(flops=1000000, bytes_accessed=1600000, transcendentals=512)
    own = pl.pallas_call(
        first_kernel,
        out_shape=jax.ShapeDtypeStruct((SHARD, D), jnp.bfloat16),
        in_specs=[spec(VMEM)],
        out_specs=spec(VMEM),
        compiler_params=params(),
        cost_estimate=cost,
    )(x)
    return pl.pallas_call(
        pair_kernel,
        out_shape=jax.ShapeDtypeStruct((2, SHARD, D), jnp.bfloat16),
        in_specs=[spec(SMEM), spec(VMEM), spec(VMEM)],
        out_specs=spec(VMEM),
        compiler_params=params(),
        cost_estimate=cost,
    )(here, own, other)


def dot(a, b):
    return lax.dot_general(a, b, (((1,), (1,)), ((), ())), preferred_element_type=jnp.float32)


def plan_kernel(here_ref, cluster_ref, table_ref, full_ref, part_ref, count_ref):
    here = here_ref[0]
    core = (here >> 4) & 1
    for phase in range(len(PHASES)):
        first = STARTS[phase] + GROUP * phase

        def candidate(n, counts):
            full, part = counts
            entry = 6 * (core * ITEMS + n)
            side = jnp.where((here & table_ref[entry + 3]) != 0, 1, 0) ^ table_ref[entry + 4]
            far = side ^ table_ref[entry + 5]
            a = 2 * (((here ^ table_ref[entry + 1]) & ~CORE) | (side << 4))
            b = 2 * (((here ^ table_ref[entry + 2]) & ~CORE) | (far << 4))
            code = table_ref[entry] + side + (far << 4)
            a0, a1 = cluster_ref[a], cluster_ref[a + 1]
            b0, b1 = cluster_ref[b], cluster_ref[b + 1]
            quads = (
                jnp.where(a0 == b0, 1, 0)
                + jnp.where(a0 == b1, 2, 0)
                + jnp.where(a1 == b0, 4, 0)
                + jnp.where(a1 == b1, 8, 0)
            )
            full_ref[first + full] = code
            part_ref[first + part] = code | (quads << 8)
            return (
                full + jnp.where(quads == 15, 1, 0),
                part + jnp.where((quads != 0) & (quads != 15), 1, 0),
            )

        full, part = lax.fori_loop(
            STARTS[phase], STARTS[phase + 1], candidate, (jnp.int32(0), jnp.int32(0))
        )
        last = full_ref[first + jnp.maximum(full - 1, 0)]
        for n in range(GROUP - 1):
            full_ref[first + full + n] = last
        count_ref[2 * phase] = full
        count_ref[2 * phase + 1] = part


def own_kernel(here_ref, cluster_ref, unit_ref, own_ref):
    here = here_ref[0]
    core = (here >> 4) & 1
    first0 = cluster_ref[2 * here]
    first1 = cluster_ref[2 * here + 1]
    there = here ^ CORE
    second0 = cluster_ref[2 * there]
    second1 = cluster_ref[2 * there + 1]
    mine = unit_ref[core]
    best = jnp.full((8, SHARD), -2.0, jnp.float32)
    col = lax.broadcasted_iota(jnp.int32, (BLK, SHARD), 1)
    row = lax.broadcasted_iota(jnp.int32, (BLK, SHARD), 0)
    label = jnp.where(col[:1] < BLK, first0, first1)
    for half, name in ((0, first0), (1, first1)):
        scores = dot(unit_ref[core, half * BLK : half * BLK + BLK, :], mine)
        keep = (row + half * BLK != col) & (label == name)
        scores = jnp.where(keep, scores, jnp.float32(-2.0))
        best = jnp.maximum(best, jnp.max(scores.reshape(BLK // 8, 8, SHARD), axis=0))
    for half, name in ((0, second0), (1, second1)):
        scores = dot(unit_ref[1 - core, half * BLK : half * BLK + BLK, :], mine)
        scores = jnp.where(label == name, scores, jnp.float32(-2.0))
        best = jnp.maximum(best, jnp.max(scores.reshape(BLK // 8, 8, SHARD), axis=0))
    own_ref[...] = jnp.max(best, axis=0, keepdims=True)


def plan_call(here, cluster, table):
    lists = jax.ShapeDtypeStruct((LISTS,), jnp.int32)
    return pl.pallas_call(
        plan_kernel,
        out_shape=(lists, lists, jax.ShapeDtypeStruct((2 * len(PHASES),), jnp.int32)),
        in_specs=[spec(SMEM)] * 3,
        out_specs=(spec(SMEM),) * 3,
        compiler_params=params(),
        cost_estimate=pl.CostEstimate(flops=3000000000, bytes_accessed=10000, transcendentals=0),
    )(here, cluster, table)


def own_call(here, cluster, unit):
    return pl.pallas_call(
        own_kernel,
        out_shape=jax.ShapeDtypeStruct((1, SHARD), jnp.float32),
        in_specs=[spec(SMEM), spec(SMEM), spec(VMEM)],
        out_specs=spec(VMEM),
        compiler_params=params(),
        cost_estimate=pl.CostEstimate(flops=1000000000, bytes_accessed=1000000, transcendentals=0),
    )(here, cluster, unit)


def fold(row_ref, col_ref, i, j, rows, cols, scores):
    best = scores[:, :128]
    for k in range(1, scores.shape[1] // 128):
        best = jnp.maximum(best, scores[:, 128 * k : 128 * k + 128])
    row_ref[i, rows, :] = jnp.maximum(row_ref[i, rows, :], best)
    down = jnp.max(scores.reshape(scores.shape[0] // 8, 8, scores.shape[1]), axis=0)
    col_ref[j, :, cols] = jnp.maximum(col_ref[j, :, cols], down)


def score_full(a_ref, b_ref, row_ref, col_ref, word):
    i = word & 15
    j = (word >> 4) & 15
    scores = dot(a_ref[i], b_ref[j])
    fold(row_ref, col_ref, i, j, slice(None), slice(None), scores)


def score_part(a_ref, b_ref, row_ref, col_ref, word):
    i = word & 15
    j = (word >> 4) & 15
    for quad in range(4):

        @pl.when(((word >> (8 + quad)) & 1) == 1)
        def _():
            rows = pl.ds((quad // 2) * BLK, BLK)
            cols = pl.ds((quad % 2) * BLK, BLK)
            scores = dot(a_ref[i, rows, :], b_ref[j, cols, :])
            fold(row_ref, col_ref, i, j, rows, cols, scores)


def score_lists(phase, full_ref, part_ref, count_ref, *refs):
    first = STARTS[phase] + GROUP * phase
    group = PHASES[phase][3]

    @pl.loop(0, count_ref[2 * phase], step=group)
    def _(n):
        for k in range(group):
            score_full(*refs, full_ref[first + n + k])

    @pl.loop(0, count_ref[2 * phase + 1])
    def _(n):
        score_part(*refs, part_ref[first + n])


def put_rows(out_ref, place, row_ref, first):
    for half in range(2):
        at = place + half
        for k in range(SHARD // 128):
            part = row_ref[first + half, 128 * k : 128 * k + 128, :].T
            out_ref[at : at + 1, 128 * k : 128 * k + 128] = jnp.max(part, axis=0, keepdims=True)


def clear(*refs):
    for ref in refs:
        ref[...] = jnp.full(ref.shape, -2.0, jnp.float32)


def put(buf, refs):
    for n, ref in enumerate(refs):
        buf[2 * n : 2 * n + 2] = ref[...]


def early_kernel(*refs):
    plan, mine, (unit, pack_ref, row_ref, col_ref) = refs[:3], refs[3:6], refs[6:]
    clear(row_ref, col_ref)
    put(pack_ref, mine)
    score_lists(0, *plan, pack_ref, unit, row_ref, col_ref)


def pack_kernel(a_ref, b_ref, c_ref, out_ref):
    put(out_ref, (a_ref, b_ref, c_ref))


def middle_kernel(*refs):
    plan, (a_low, a_mid, b_own, b_low, row_in, col_in), outs = refs[:3], refs[3:9], refs[9:]
    rows_out, row_mid, col_own, col_low, row_low = outs
    clear(row_mid, col_low)
    row_low[...] = row_in[...]
    col_own[...] = col_in[...]
    score_lists(1, *plan, a_mid, b_own, row_mid, col_own)
    score_lists(2, *plan, a_mid, b_low, row_mid, col_low)
    score_lists(3, *plan, a_low, b_low, row_low, col_low)
    for n in range(0, 6, 2):
        put_rows(rows_out, n, row_low, n)


def f32(*shape):
    return jax.ShapeDtypeStruct(shape, jnp.float32)


ROWS = f32(6, SHARD, 128)
COLS = f32(6, 8, SHARD)
COLS2 = f32(2, 8, SHARD)
PACK = jax.ShapeDtypeStruct((6, SHARD, D), jnp.bfloat16)


def kernel_call(kernel, operands, outs, scratch, flops, smem=3):
    return pl.pallas_call(
        kernel,
        out_shape=outs,
        in_specs=[spec(SMEM)] * smem + [spec(VMEM)] * (len(operands) - smem),
        out_specs=jax.tree.map(lambda _: spec(VMEM), outs),
        scratch_shapes=[VMEM(x.shape, x.dtype) for x in scratch],
        compiler_params=params(),
        cost_estimate=pl.CostEstimate(flops=flops, bytes_accessed=8000000, transcendentals=0),
    )(*operands)


def early_call(plan, *operands):
    return kernel_call(early_kernel, [*plan, *operands], (PACK, ROWS, COLS2), [], 3000000000)


def middle_call(plan, *operands):
    outs = (f32(6, SHARD), ROWS, COLS2, COLS)
    return kernel_call(middle_kernel, [*plan, *operands], outs, [ROWS], 5000000000)


KEPT = (0, 1, 2, 4)
SENT = (3, 6, 5, 7)


def last_kernel(*refs):
    plan, mine, theirs, refs = refs[:3], refs[3:5], refs[5:7], refs[7:]
    (a_mid, b_own, b_low, b_mid, rows0, row_in, own_in, low_in), refs = refs[:8], refs[8:]
    keep_ref, send_ref, other_ref, *refs = refs
    a_last, b_last, row_mid, row_last, col_own, col_low, col_mid, col_last = refs
    clear(row_last, col_mid, col_last)
    row_mid[...] = row_in[...]
    col_own[...] = own_in[...]
    col_low[...] = low_in[...]
    for half in range(2):
        a_last[half] = mine[half][...]
        b_last[half] = theirs[half][...]
    score_lists(4, *plan, a_mid, b_mid, row_mid, col_mid)
    score_lists(5, *plan, a_last, b_own, row_last, col_own)
    score_lists(6, *plan, a_last, b_low, row_last, col_low)
    score_lists(7, *plan, a_last, b_mid, row_last, col_mid)
    score_lists(8, *plan, a_last, b_last, row_last, col_last)
    keep_ref[0:2] = jnp.full((2, SHARD), -2.0, jnp.float32)
    for out_ref, slots in ((keep_ref, KEPT), (send_ref, SENT)):
        for place, slot in enumerate(slots):
            if slot == 7:
                put_rows(out_ref, 2 * place, row_last, 0)
            elif slot > 3:
                put_rows(out_ref, 2 * place, row_mid, 2 * slot - 8)
            elif slot > 0:
                out_ref[2 * place : 2 * place + 2] = rows0[2 * slot - 2 : 2 * slot]
    for place, slot in enumerate(KEPT + SENT):
        for half in range(2):
            at = 2 * place + half
            col_ref, n = ((col_own, 0), (col_low, 2), (col_mid, 8), (col_last, 14))[(slot + 2) // 3]
            down = col_ref[2 * slot + half - n]
            other_ref[at : at + 1, :] = jnp.max(down, axis=0, keepdims=True)


def last_call(plan, *operands):
    two = jax.ShapeDtypeStruct((2, SHARD, D), jnp.bfloat16)
    outs = (f32(8, SHARD), f32(8, SHARD), f32(16, SHARD))
    scratch = [two, two, ROWS, f32(2, SHARD, 128), COLS2, COLS, COLS, COLS2]
    return kernel_call(last_kernel, [*plan, *operands], outs, scratch, 5000000000)


def swap(x):
    return lax.ppermute(x, ("row", "col"), [(s, s ^ CORE) for s in range(128)])


def exchange(x, generator):
    pairs = [(s, s ^ GENERATORS[(s >> 4) & 1][generator]) for s in range(128)]
    return lax.ppermute(x, ("row", "col"), pairs)


def after(x, *done):
    return lax.optimization_barrier((x, *done))[0]


def body(embeddings, block_cluster):
    here = (lax.axis_index("row") * 16 + lax.axis_index("col")).astype(jnp.int32).reshape(1)
    unit = unit_call(here, embeddings, swap(embeddings))
    plan = plan_call(here, block_cluster, jnp.asarray(TABLE.reshape(-1)))
    mine = [unit]

    def step(slots):
        return [exchange(mine[SENDS[k - 1][0]], SENDS[k - 1][1]) for k in slots]

    own = own_call(here, block_cluster, unit)
    mine.extend(after(x, plan[2], own) for x in step((1, 2, 3)))
    a_low, rows0, col_own = early_call(plan, *mine[1:4], unit)
    b_low = swap(a_low)
    mine.extend(after(x, a_low) for x in step((4, 5, 6)))
    halves = [
        exchange(mine[source][half], generator) for half, (source, generator) in enumerate(HALVES)
    ]
    a_mid = kernel_call(pack_kernel, mine[4:7], PACK, [], 1000000000, 0)
    b_mid = swap(a_mid)
    rows0, rows1, col_own, col_low = middle_call(
        plan, a_low, a_mid, unit, b_low, rows0, col_own
    )
    halves = [after(x, col_low) for x in halves]
    swapped = [swap(x) for x in halves]
    keep, send, other = last_call(
        plan, *halves, *swapped, a_mid, unit, b_low, b_mid, rows0, rows1, col_own, col_low
    )
    other = swap(other)
    keep = jnp.maximum(keep, other[:8])
    send = jnp.maximum(send, other[8:])
    keep = jnp.maximum(keep, exchange(send, 2))
    keep = jnp.maximum(keep[:4], exchange(keep[4:], 1))
    keep = jnp.maximum(keep[:2], exchange(keep[2:], 0))
    second = (here & CORE) != 0
    ours = jnp.where(second, keep[1], keep[0])
    other = swap(jnp.where(second, keep[0], keep[1]))
    return jnp.maximum(own.reshape(SHARD), jnp.maximum(ours, other))


def solution(mesh):
    placed = (P(("row", "col"), None), P())
    return jax.shard_map(
        body, mesh=mesh, in_specs=placed, out_specs=P(("row", "col")), check_vma=False
    )
```

```python
import jax
import jax.numpy as jnp
from jax import lax
from jax.experimental import pallas as pl
from jax.experimental.pallas import tpu as pltpu
from jax.sharding import PartitionSpec as P

BLK = 256
SHARD = 512
D = 384
VMEM_LIMIT = 20 * 1024 * 1024

CORE = 16
X1, X3, Y1, Y3, Z1, Z3 = 32, 96, 4, 12, 1, 3
GENERATORS = ((X1, Y1, Y3), (X3, Z1, Z3))
SLOTS = ((), (0,), (1,), (2,), (0, 1), (1, 2), (2, 0), (0, 1, 2))
SENDS = ((0, 0), (0, 1), (0, 2), (1, 1), (2, 2), (3, 0))
HALVES = ((5, 0), (6, 1))


def mask_of(core, slot):
    mask = 0
    for generator in SLOTS[slot]:
        mask ^= GENERATORS[core][generator]
    return mask


EARLY = [(g, 0) for g in (1, 2, 3)]
MIDDLE = [(g, h) for g in (1, 2, 3) for h in range(1, g + 1)]
MIDDLE += [(g, h) for g in (4, 5, 6) for h in range(4)]
LAST = [(g, h) for g in (4, 5, 6, 7) for h in range(4, 8)] + [(7, h) for h in range(4)]
PHASES = ((EARLY, 1), (MIDDLE, 1), (LAST, 4))


def shared(g, h):
    return g == h or (g >= 4 and h >= 4)


COUNTS = [sum(2 if shared(g, h) else 4 for g, h in pairs) for pairs, _ in PHASES]
STARTS = [0, COUNTS[0] + 1, COUNTS[0] + COUNTS[1] + 2]
LISTS = sum(COUNTS) + 3
MARGIN = 24
MOST = 160
VMEM = pltpu.VMEM
SMEM = pltpu.SMEM


def spec(space):
    return pl.BlockSpec(memory_space=space)


def params():
    return pltpu.CompilerParams(vmem_limit_bytes=VMEM_LIMIT)


def unit_of(x):
    values = x.astype(jnp.float32)
    squares = jnp.sum(values * values, axis=1, keepdims=True)
    return (values * lax.rsqrt(squares + 1e-06)).astype(jnp.bfloat16)


def first_kernel(x_ref, out_ref):
    out_ref[...] = unit_of(x_ref[...])


def pair_kernel(here_ref, own_ref, other_ref, out_ref):
    core = (here_ref[0] >> 4) & 1
    out_ref[core] = own_ref[...]
    out_ref[1 - core] = unit_of(other_ref[...])


def unit_call(here, x, other):
    cost = pl.CostEstimate(flops=1000000, bytes_accessed=1600000, transcendentals=512)
    own = pl.pallas_call(
        first_kernel,
        out_shape=jax.ShapeDtypeStruct((SHARD, D), jnp.bfloat16),
        in_specs=[spec(VMEM)],
        out_specs=spec(VMEM),
        compiler_params=params(),
        cost_estimate=cost,
    )(x)
    return pl.pallas_call(
        pair_kernel,
        out_shape=jax.ShapeDtypeStruct((2, SHARD, D), jnp.bfloat16),
        in_specs=[spec(SMEM), spec(VMEM), spec(VMEM)],
        out_specs=spec(VMEM),
        compiler_params=params(),
        cost_estimate=cost,
    )(here, own, other)


def dot(a, b):
    return lax.dot_general(a, b, (((1,), (1,)), ((), ())), preferred_element_type=jnp.float32)


def plan_kernel(here_ref, cluster_ref, blocks_ref, full_ref, part_ref, count_ref, mine, theirs, share):
    here = here_ref[0]
    core = (here >> 4) & 1
    masks = [[mask_of(c, slot) for slot in range(8)] for c in range(2)]
    for slot in range(8):
        for ref, one, two in ((mine, 0, 1), (theirs, 1, 0)):
            chip = (here ^ jnp.where(core == 0, masks[one][slot], masks[two][slot])) & ~CORE
            for half in range(2):
                block = 2 * (chip | (half * CORE))
                ref[2 * slot + half] = cluster_ref[block] | (cluster_ref[block + 1] << 4)

    first = jnp.sum(jnp.where(blocks_ref[...] < cluster_ref[128], 1, 0))

    def held(slab):
        low, high = slab * 64, slab * 64 + 64
        return jnp.maximum(jnp.minimum(high, first + MOST) - jnp.maximum(low, first), 0)

    slab = here >> 5
    ours = held(slab)
    share[0] = 0
    for other in range(1, 4):
        there = held(slab ^ other)
        share[other] = jnp.where(
            ours + MARGIN <= there, 1, jnp.where(there + MARGIN <= ours, 2, 0)
        )

    for phase, (pairs, base) in enumerate(PHASES):
        full = jnp.int32(STARTS[phase])
        part = jnp.int32(STARTS[phase])

        def candidate(full, part, wanted, g, side, h, far):
            a, b = mine[2 * g + side], theirs[2 * h + far]
            same = a ^ b
            left, right = (a >> 4) ^ b, a ^ (b >> 4)
            quads = (
                jnp.where((same & 15) == 0, 1, 0)
                | jnp.where((right & 15) == 0, 2, 0)
                | jnp.where((left & 15) == 0, 4, 0)
                | jnp.where((same & 240) == 0, 8, 0)
            )
            code = (2 * (g - base) + side) | ((2 * h + far) << 4)
            full_ref[full] = code
            part_ref[part] = code | (quads << 8)
            whole = quads == 15
            full = full + jnp.where(wanted & whole, 1, 0)
            part = part + jnp.where(wanted & (quads != 0) & jnp.logical_not(whole), 1, 0)
            return full, part

        for g, h in pairs:
            w = jnp.where(
                core == 0, masks[0][g] ^ masks[1][h], masks[1][g] ^ masks[0][h]
            )
            kind = share[(w >> 5) & 3]
            bit = jnp.where((here & (w & -w)) != 0, 1, 0) ^ ((g + h) % 2)
            whole, half = kind == 1, kind == 0
            mixed = ((whole | half, core, 1 - core), (whole, 1 - core, core))
            plain = ((whole | (half & (bit == 0)), 0, 0), (whole | (half & (bit == 1)), 1, 1))
            if shared(g, h):
                for (one, side, far), (two, _, _), n in zip(mixed, plain, (0, 1)):
                    wanted = ((core == 0) & one) | ((core == 1) & two)
                    side = jnp.where(core == 0, side, n)
                    far = jnp.where(core == 0, far, n)
                    full, part = candidate(full, part, wanted, g, side, h, far)
            else:
                for wanted, side, far in mixed + plain:
                    full, part = candidate(full, part, wanted, g, side, h, far)
        count_ref[2 * phase] = full - STARTS[phase]
        count_ref[2 * phase + 1] = part - STARTS[phase]


def own_kernel(here_ref, cluster_ref, unit_ref, own_ref):
    here = here_ref[0]
    core = (here >> 4) & 1
    first0 = cluster_ref[2 * here]
    first1 = cluster_ref[2 * here + 1]
    there = here ^ CORE
    second0 = cluster_ref[2 * there]
    second1 = cluster_ref[2 * there + 1]
    mine = unit_ref[core]
    best = jnp.full((8, SHARD), -2.0, jnp.float32)
    col = lax.broadcasted_iota(jnp.int32, (BLK, SHARD), 1)
    row = lax.broadcasted_iota(jnp.int32, (BLK, SHARD), 0)
    label = jnp.where(col[:1] < BLK, first0, first1)
    for half, name in ((0, first0), (1, first1)):
        scores = dot(unit_ref[core, half * BLK : half * BLK + BLK, :], mine)
        keep = (row + half * BLK != col) & (label == name)
        scores = jnp.where(keep, scores, jnp.float32(-2.0))
        best = jnp.maximum(best, jnp.max(scores.reshape(BLK // 8, 8, SHARD), axis=0))
    for half, name in ((0, second0), (1, second1)):
        scores = dot(unit_ref[1 - core, half * BLK : half * BLK + BLK, :], mine)
        scores = jnp.where(label == name, scores, jnp.float32(-2.0))
        best = jnp.maximum(best, jnp.max(scores.reshape(BLK // 8, 8, SHARD), axis=0))
    own_ref[...] = jnp.max(best, axis=0, keepdims=True)


def plan_call(here, cluster):
    lists = jax.ShapeDtypeStruct((LISTS,), jnp.int32)
    return pl.pallas_call(
        plan_kernel,
        out_shape=(lists, lists, jax.ShapeDtypeStruct((2 * len(PHASES),), jnp.int32)),
        in_specs=[spec(SMEM), spec(SMEM), spec(VMEM)],
        out_specs=(spec(SMEM),) * 3,
        scratch_shapes=[SMEM((16,), jnp.int32), SMEM((16,), jnp.int32), SMEM((4,), jnp.int32)],
        compiler_params=params(),
        cost_estimate=pl.CostEstimate(flops=3000000000, bytes_accessed=10000, transcendentals=0),
    )(here, cluster, cluster.reshape(2, 128))


def own_call(here, cluster, unit):
    return pl.pallas_call(
        own_kernel,
        out_shape=jax.ShapeDtypeStruct((1, SHARD), jnp.float32),
        in_specs=[spec(SMEM), spec(SMEM), spec(VMEM)],
        out_specs=spec(VMEM),
        compiler_params=params(),
        cost_estimate=pl.CostEstimate(flops=1000000000, bytes_accessed=1000000, transcendentals=0),
    )(here, cluster, unit)


def fold(row_ref, col_ref, i, j, rows, cols, scores):
    best = scores[:, :128]
    for k in range(1, scores.shape[1] // 128):
        best = jnp.maximum(best, scores[:, 128 * k : 128 * k + 128])
    row_ref[i, rows, :] = jnp.maximum(row_ref[i, rows, :], best)
    down = jnp.max(scores.reshape(scores.shape[0] // 8, 8, scores.shape[1]), axis=0)
    col_ref[j, :, cols] = jnp.maximum(col_ref[j, :, cols], down)


def score_full(a_ref, b_ref, row_ref, col_ref, word):
    i = word & 15
    j = (word >> 4) & 15
    scores = dot(a_ref[i], b_ref[j])
    fold(row_ref, col_ref, i, j, slice(None), slice(None), scores)


def score_part(a_ref, b_ref, row_ref, col_ref, word):
    i = word & 15
    j = (word >> 4) & 15
    for quad in range(4):

        @pl.when(((word >> (8 + quad)) & 1) == 1)
        def _():
            rows = pl.ds((quad // 2) * BLK, BLK)
            cols = pl.ds((quad % 2) * BLK, BLK)
            scores = dot(a_ref[i, rows, :], b_ref[j, cols, :])
            fold(row_ref, col_ref, i, j, rows, cols, scores)


def score_lists(phase, full_ref, part_ref, count_ref, *refs):
    first = STARTS[phase]
    full = count_ref[2 * phase]
    fours = full & ~3

    def items(n, count):
        for k in range(count):
            score_full(*refs, full_ref[first + n + k])

    @pl.loop(0, fours, step=4)
    def _(n):
        items(n, 4)

    @pl.when((full & 2) != 0)
    def _():
        items(fours, 2)

    @pl.when((full & 1) != 0)
    def _():
        items(full - 1, 1)

    @pl.loop(0, count_ref[2 * phase + 1])
    def _(n):
        score_part(*refs, part_ref[first + n])


def put_rows(out_ref, place, row_ref, first):
    for half in range(2):
        at = place + half
        for k in range(SHARD // 128):
            part = row_ref[first + half, 128 * k : 128 * k + 128, :].T
            out_ref[at : at + 1, 128 * k : 128 * k + 128] = jnp.max(part, axis=0, keepdims=True)


def clear(*refs):
    for ref in refs:
        ref[...] = jnp.full(ref.shape, -2.0, jnp.float32)


def put(buf, refs):
    for n, ref in enumerate(refs):
        buf[2 * n : 2 * n + 2] = ref[...]


def early_kernel(*refs):
    plan, unit, mine, (pack_ref, row_ref, col_ref) = refs[:3], refs[3], refs[4:7], refs[7:]
    clear(row_ref, col_ref)
    put(pack_ref, mine)
    score_lists(0, *plan, pack_ref, unit, row_ref, col_ref)


def pack_kernel(a_ref, b_ref, c_ref, out_ref):
    put(out_ref, (a_ref, b_ref, c_ref))


def middle_kernel(*refs):
    plan, (unit, a_low, a_mid, b_low, row_in, col_in), outs = refs[:3], refs[3:9], refs[9:]
    rows_out, row_mid, col_ref, a_buf, b_buf, row_ref = outs
    row_ref[:6] = row_in[...]
    row_ref[6:] = jnp.full(row_mid.shape, -2.0, jnp.float32)
    col_ref[:2] = col_in[...]
    col_ref[2:] = jnp.full((6, 8, SHARD), -2.0, jnp.float32)
    a_buf[:6] = a_low[...]
    a_buf[6:] = a_mid[...]
    b_buf[:2] = unit[...]
    b_buf[2:] = b_low[...]
    score_lists(1, *plan, a_buf, b_buf, row_ref, col_ref)
    for n in range(0, 6, 2):
        put_rows(rows_out, n, row_ref, n)
    row_mid[...] = row_ref[6:]


def f32(*shape):
    return jax.ShapeDtypeStruct(shape, jnp.float32)


def shards(n):
    return jax.ShapeDtypeStruct((n, SHARD, D), jnp.bfloat16)


def rows_of(n):
    return f32(n, SHARD, 128)


def cols_of(n):
    return f32(n, 8, SHARD)


def kernel_call(kernel, operands, outs, scratch, flops, smem=3):
    return pl.pallas_call(
        kernel,
        out_shape=outs,
        in_specs=[spec(SMEM)] * smem + [spec(VMEM)] * (len(operands) - smem),
        out_specs=jax.tree.map(lambda _: spec(VMEM), outs),
        scratch_shapes=[VMEM(x.shape, x.dtype) for x in scratch],
        compiler_params=params(),
        cost_estimate=pl.CostEstimate(flops=flops, bytes_accessed=8000000, transcendentals=0),
    )(*operands)


def early_call(plan, *operands):
    outs = (shards(6), rows_of(6), cols_of(2))
    return kernel_call(early_kernel, [*plan, *operands], outs, [], 3000000000)


def middle_call(plan, *operands):
    outs = (f32(6, SHARD), rows_of(6), cols_of(8))
    scratch = [shards(12), shards(8), rows_of(12)]
    return kernel_call(middle_kernel, [*plan, *operands], outs, scratch, 5000000000)


KEPT = (0, 1, 2, 4)
SENT = (3, 6, 5, 7)


def last_kernel(*refs):
    plan, mine, theirs, refs = refs[:3], refs[3:5], refs[5:7], refs[7:]
    unit, a_mid, b_low, b_mid, rows0, row_in, col_in, keep_ref, send_ref, other_ref, *refs = refs
    a_buf, b_buf, row_ref, col_ref = refs
    a_buf[:6] = a_mid[...]
    b_buf[:2] = unit[...]
    b_buf[2:8] = b_low[...]
    b_buf[8:14] = b_mid[...]
    for half in range(2):
        a_buf[6 + half] = mine[half][...]
        b_buf[14 + half] = theirs[half][...]
    row_ref[:6] = row_in[...]
    row_ref[6:] = jnp.full((2, SHARD, 128), -2.0, jnp.float32)
    col_ref[:8] = col_in[...]
    col_ref[8:] = jnp.full(col_in.shape, -2.0, jnp.float32)
    score_lists(2, *plan, a_buf, b_buf, row_ref, col_ref)
    keep_ref[0:2] = jnp.full((2, SHARD), -2.0, jnp.float32)
    for out_ref, slots in ((keep_ref, KEPT), (send_ref, SENT)):
        for place, slot in enumerate(slots):
            if slot > 3:
                put_rows(out_ref, 2 * place, row_ref, 2 * slot - 8)
            elif slot > 0:
                out_ref[2 * place : 2 * place + 2] = rows0[2 * slot - 2 : 2 * slot]
    for place, slot in enumerate(KEPT + SENT):
        for half in range(2):
            at = 2 * place + half
            down = col_ref[2 * slot + half]
            other_ref[at : at + 1, :] = jnp.max(down, axis=0, keepdims=True)


def last_call(plan, *operands):
    outs = (f32(8, SHARD), f32(8, SHARD), f32(16, SHARD))
    scratch = [shards(8), shards(16), rows_of(8), cols_of(16)]
    return kernel_call(last_kernel, [*plan, *operands], outs, scratch, 5000000000)


def swap(x):
    return lax.ppermute(x, ("row", "col"), [(s, s ^ CORE) for s in range(128)])


def exchange(x, generator):
    pairs = [(s, s ^ GENERATORS[(s >> 4) & 1][generator]) for s in range(128)]
    return lax.ppermute(x, ("row", "col"), pairs)


def after(x, *done):
    return lax.optimization_barrier((x, *done))[0]


def body(embeddings, block_cluster):
    here = (lax.axis_index("row") * 16 + lax.axis_index("col")).astype(jnp.int32).reshape(1)
    unit = unit_call(here, embeddings, swap(embeddings))
    plan = plan_call(here, block_cluster)
    mine = [unit]

    def step(slots):
        return [exchange(mine[SENDS[k - 1][0]], SENDS[k - 1][1]) for k in slots]

    own = own_call(here, block_cluster, unit)
    mine.extend(after(x, plan[2], own) for x in step((1, 2, 3)))
    a_low, rows0, cols = early_call(plan, *mine)
    b_low = swap(a_low)
    mine.extend(after(x, a_low) for x in step((4, 5, 6)))
    halves = [
        exchange(mine[source][half], generator) for half, (source, generator) in enumerate(HALVES)
    ]
    a_mid = kernel_call(pack_kernel, mine[4:7], shards(6), [], 1000000000, 0)
    b_mid = swap(a_mid)
    rows0, rows1, cols = middle_call(plan, unit, a_low, a_mid, b_low, rows0, cols)
    halves = [after(x, cols) for x in halves]
    swapped = [swap(x) for x in halves]
    keep, send, other = last_call(
        plan, *halves, *swapped, unit, a_mid, b_low, b_mid, rows0, rows1, cols
    )
    other = swap(other)
    keep = jnp.maximum(keep, other[:8])
    send = jnp.maximum(send, other[8:])
    keep = jnp.maximum(keep, exchange(send, 2))
    keep = jnp.maximum(keep[:4], exchange(keep[4:], 1))
    keep = jnp.maximum(keep[:2], exchange(keep[2:], 0))
    second = (here & CORE) != 0
    ours = jnp.where(second, keep[1], keep[0])
    other = swap(jnp.where(second, keep[0], keep[1]))
    return jnp.maximum(own.reshape(SHARD), jnp.maximum(ours, other))


def solution(mesh):
    placed = (P(("row", "col"), None), P())
    return jax.shard_map(
        body, mesh=mesh, in_specs=placed, out_specs=P(("row", "col")), check_vma=False
    )
```

```python
import jax
import jax.numpy as jnp
from jax import lax
from jax.experimental import pallas as pl
from jax.experimental.pallas import tpu as pltpu
from jax.sharding import PartitionSpec as P

BLK = 256
SHARD = 512
D = 384
VMEM_LIMIT = 20 * 1024 * 1024

CORE = 16
X1, X3, Y1, Y3, Z1, Z3 = 32, 96, 4, 12, 1, 3
GENERATORS = ((X1, Y1, Y3), (X3, Z1, Z3))
SLOTS = ((), (0,), (1,), (2,), (0, 1), (1, 2), (2, 0), (0, 1, 2))
SENDS = ((0, 0), (0, 1), (0, 2), (1, 1), (2, 2), (3, 0))
HALVES = ((5, 0), (6, 1))


def mask_of(core, slot):
    mask = 0
    for generator in SLOTS[slot]:
        mask ^= GENERATORS[core][generator]
    return mask


EARLY = [(g, 0) for g in (1, 2, 3)]
SECOND = [(g, h) for g in (1, 2, 3) for h in range(1, g + 1)]
MIDDLE = [(g, h) for g in (4, 5, 6) for h in range(4)]
LAST = [(g, h) for g in (4, 5, 6) for h in (4, 5, 6)] + [(7, h) for h in range(7)]
FINAL = [(7, 7)]
PHASES = ((EARLY, 1, 0), (SECOND, 1, 1), (MIDDLE, 4, 0), (LAST, 4, 0), (FINAL, 7, 7))


def shared(g, h):
    return g == h or 4 <= min(g, h) <= max(g, h) <= 6


COUNTS = [sum(2 if shared(g, h) else 4 for g, h in phase[0]) for phase in PHASES]
STARTS = [sum(COUNTS[:n]) + n for n in range(len(PHASES))]
LISTS = sum(COUNTS) + len(PHASES)
MARGIN = 24
MOST = 160
VMEM = pltpu.VMEM
SMEM = pltpu.SMEM


def spec(space):
    return pl.BlockSpec(memory_space=space)


def params():
    return pltpu.CompilerParams(vmem_limit_bytes=VMEM_LIMIT)


def unit_of(x):
    values = x.astype(jnp.float32)
    squares = jnp.sum(values * values, axis=1, keepdims=True)
    return (values * lax.rsqrt(squares + 1e-06)).astype(jnp.bfloat16)


def first_kernel(x_ref, out_ref):
    out_ref[...] = unit_of(x_ref[...])


def pair_kernel(here_ref, own_ref, other_ref, out_ref):
    core = (here_ref[0] >> 4) & 1
    out_ref[core] = own_ref[...]
    out_ref[1 - core] = unit_of(other_ref[...])


def unit_call(here, x, other):
    cost = pl.CostEstimate(flops=1000000, bytes_accessed=1600000, transcendentals=512)
    own = pl.pallas_call(
        first_kernel,
        out_shape=jax.ShapeDtypeStruct((SHARD, D), jnp.bfloat16),
        in_specs=[spec(VMEM)],
        out_specs=spec(VMEM),
        compiler_params=params(),
        cost_estimate=cost,
    )(x)
    return pl.pallas_call(
        pair_kernel,
        out_shape=jax.ShapeDtypeStruct((2, SHARD, D), jnp.bfloat16),
        in_specs=[spec(SMEM), spec(VMEM), spec(VMEM)],
        out_specs=spec(VMEM),
        compiler_params=params(),
        cost_estimate=cost,
    )(here, own, other)


def dot(a, b):
    return lax.dot_general(a, b, (((1,), (1,)), ((), ())), preferred_element_type=jnp.float32)


def plan_kernel(here_ref, cluster_ref, blocks_ref, full_ref, part_ref, count_ref, mine, theirs, share):
    here = here_ref[0]
    core = (here >> 4) & 1
    masks = [[mask_of(c, slot) for slot in range(8)] for c in range(2)]
    for slot in range(8):
        for ref, one, two in ((mine, 0, 1), (theirs, 1, 0)):
            chip = (here ^ jnp.where(core == 0, masks[one][slot], masks[two][slot])) & ~CORE
            for half in range(2):
                block = 2 * (chip | (half * CORE))
                ref[2 * slot + half] = cluster_ref[block] | (cluster_ref[block + 1] << 4)

    first = jnp.sum(jnp.where(blocks_ref[...] < cluster_ref[128], 1, 0))

    def held(slab):
        low, high = slab * 64, slab * 64 + 64
        return jnp.maximum(jnp.minimum(high, first + MOST) - jnp.maximum(low, first), 0)

    slab = here >> 5
    ours = held(slab)
    share[0] = 0
    for other in range(1, 4):
        there = held(slab ^ other)
        share[other] = jnp.where(
            ours + MARGIN <= there, 1, jnp.where(there + MARGIN <= ours, 2, 0)
        )

    for phase, (pairs, base_a, base_b) in enumerate(PHASES):
        full = jnp.int32(STARTS[phase])
        part = jnp.int32(STARTS[phase])

        def candidate(full, part, wanted, g, side, h, far):
            a, b = mine[2 * g + side], theirs[2 * h + far]
            same = a ^ b
            left, right = (a >> 4) ^ b, a ^ (b >> 4)
            quads = (
                jnp.where((same & 15) == 0, 1, 0)
                | jnp.where((right & 15) == 0, 2, 0)
                | jnp.where((left & 15) == 0, 4, 0)
                | jnp.where((same & 240) == 0, 8, 0)
            )
            code = (2 * (g - base_a) + side) | ((2 * (h - base_b) + far) << 4)
            full_ref[full] = code
            part_ref[part] = code | (quads << 8)
            whole = quads == 15
            full = full + jnp.where(wanted & whole, 1, 0)
            part = part + jnp.where(wanted & (quads != 0) & jnp.logical_not(whole), 1, 0)
            return full, part

        for g, h in pairs:
            w = jnp.where(
                core == 0, masks[0][g] ^ masks[1][h], masks[1][g] ^ masks[0][h]
            )
            kind = share[(w >> 5) & 3]
            bit = jnp.where((here & (w & -w)) != 0, 1, 0) ^ ((g + h) % 2)
            whole, half = kind == 1, kind == 0
            mixed = ((whole | half, core, 1 - core), (whole, 1 - core, core))
            plain = ((whole | (half & (bit == 0)), 0, 0), (whole | (half & (bit == 1)), 1, 1))
            if shared(g, h):
                for (one, side, far), (two, _, _), n in zip(mixed, plain, (0, 1)):
                    wanted = ((core == 0) & one) | ((core == 1) & two)
                    side = jnp.where(core == 0, side, n)
                    far = jnp.where(core == 0, far, n)
                    full, part = candidate(full, part, wanted, g, side, h, far)
            else:
                for wanted, side, far in mixed + plain:
                    full, part = candidate(full, part, wanted, g, side, h, far)
        count_ref[2 * phase] = full - STARTS[phase]
        count_ref[2 * phase + 1] = part - STARTS[phase]


def own_kernel(here_ref, cluster_ref, unit_ref, own_ref):
    here = here_ref[0]
    core = (here >> 4) & 1
    first0 = cluster_ref[2 * here]
    first1 = cluster_ref[2 * here + 1]
    there = here ^ CORE
    second0 = cluster_ref[2 * there]
    second1 = cluster_ref[2 * there + 1]
    mine = unit_ref[core]
    best = jnp.full((8, SHARD), -2.0, jnp.float32)
    col = lax.broadcasted_iota(jnp.int32, (BLK, SHARD), 1)
    row = lax.broadcasted_iota(jnp.int32, (BLK, SHARD), 0)
    label = jnp.where(col[:1] < BLK, first0, first1)
    for half, name in ((0, first0), (1, first1)):
        scores = dot(unit_ref[core, half * BLK : half * BLK + BLK, :], mine)
        keep = (row + half * BLK != col) & (label == name)
        scores = jnp.where(keep, scores, jnp.float32(-2.0))
        best = jnp.maximum(best, jnp.max(scores.reshape(BLK // 8, 8, SHARD), axis=0))
    for half, name in ((0, second0), (1, second1)):
        scores = dot(unit_ref[1 - core, half * BLK : half * BLK + BLK, :], mine)
        scores = jnp.where(label == name, scores, jnp.float32(-2.0))
        best = jnp.maximum(best, jnp.max(scores.reshape(BLK // 8, 8, SHARD), axis=0))
    own_ref[...] = jnp.max(best, axis=0, keepdims=True)


def plan_call(here, cluster):
    lists = jax.ShapeDtypeStruct((LISTS,), jnp.int32)
    return pl.pallas_call(
        plan_kernel,
        out_shape=(lists, lists, jax.ShapeDtypeStruct((2 * len(PHASES),), jnp.int32)),
        in_specs=[spec(SMEM), spec(SMEM), spec(VMEM)],
        out_specs=(spec(SMEM),) * 3,
        scratch_shapes=[SMEM((16,), jnp.int32), SMEM((16,), jnp.int32), SMEM((4,), jnp.int32)],
        compiler_params=params(),
        cost_estimate=pl.CostEstimate(flops=3000000000, bytes_accessed=10000, transcendentals=0),
    )(here, cluster, cluster.reshape(2, 128))


def own_call(here, cluster, unit):
    return pl.pallas_call(
        own_kernel,
        out_shape=jax.ShapeDtypeStruct((1, SHARD), jnp.float32),
        in_specs=[spec(SMEM), spec(SMEM), spec(VMEM)],
        out_specs=spec(VMEM),
        compiler_params=params(),
        cost_estimate=pl.CostEstimate(flops=1000000000, bytes_accessed=1000000, transcendentals=0),
    )(here, cluster, unit)


def fold(row_ref, col_ref, i, j, rows, cols, scores):
    best = scores[:, :128]
    for k in range(1, scores.shape[1] // 128):
        best = jnp.maximum(best, scores[:, 128 * k : 128 * k + 128])
    row_ref[i, rows, :] = jnp.maximum(row_ref[i, rows, :], best)
    down = jnp.max(scores.reshape(scores.shape[0] // 8, 8, scores.shape[1]), axis=0)
    col_ref[j, :, cols] = jnp.maximum(col_ref[j, :, cols], down)


def score_full(a_ref, b_ref, row_ref, col_ref, word):
    i = word & 15
    j = (word >> 4) & 15
    scores = dot(a_ref[i], b_ref[j])
    fold(row_ref, col_ref, i, j, slice(None), slice(None), scores)


def score_part(a_ref, b_ref, row_ref, col_ref, word):
    i = word & 15
    j = (word >> 4) & 15
    for quad in range(4):

        @pl.when(((word >> (8 + quad)) & 1) == 1)
        def _():
            rows = pl.ds((quad // 2) * BLK, BLK)
            cols = pl.ds((quad % 2) * BLK, BLK)
            scores = dot(a_ref[i, rows, :], b_ref[j, cols, :])
            fold(row_ref, col_ref, i, j, rows, cols, scores)


def score_lists(phase, full_ref, part_ref, count_ref, *refs):
    first = STARTS[phase]
    full = count_ref[2 * phase]
    fours = full & ~3

    def items(n, count):
        for k in range(count):
            score_full(*refs, full_ref[first + n + k])

    @pl.loop(0, fours, step=4)
    def _(n):
        items(n, 4)

    @pl.when((full & 2) != 0)
    def _():
        items(fours, 2)

    @pl.when((full & 1) != 0)
    def _():
        items(full - 1, 1)

    @pl.loop(0, count_ref[2 * phase + 1])
    def _(n):
        score_part(*refs, part_ref[first + n])


def put_rows(out_ref, place, row_ref, first):
    for half in range(2):
        at = place + half
        for k in range(SHARD // 128):
            part = row_ref[first + half, 128 * k : 128 * k + 128, :].T
            out_ref[at : at + 1, 128 * k : 128 * k + 128] = jnp.max(part, axis=0, keepdims=True)


def clear(*refs):
    for ref in refs:
        ref[...] = jnp.full(ref.shape, -2.0, jnp.float32)


def put(buf, refs):
    for n, ref in enumerate(refs):
        buf[2 * n : 2 * n + 2] = ref[...]


def pack_kernel(a_ref, b_ref, c_ref, out_ref):
    put(out_ref, (a_ref, b_ref, c_ref))


def early_kernel(*refs):
    plan, (a_low, unit, row_ref, col_ref) = refs[:3], refs[3:]
    clear(row_ref, col_ref)
    score_lists(0, *plan, a_low, unit, row_ref, col_ref)


def second_kernel(*refs):
    plan, (a_low, unit, b_in, row_in, col_in), outs = refs[:3], refs[3:8], refs[8:]
    rows_out, col_ref, b_low, row_ref, col_low = outs
    b_low[:2] = unit[...]
    b_low[2:] = b_in[...]
    row_ref[...] = row_in[...]
    clear(col_low)
    score_lists(1, *plan, a_low, b_in, row_ref, col_low)
    col_ref[:2] = col_in[...]
    col_ref[2:] = col_low[...]
    for n in range(0, 6, 2):
        put_rows(rows_out, n, row_ref, n)


def middle_kernel(*refs):
    plan, (a_mid, b_low, col_in, row_ref, col_ref) = refs[:3], refs[3:]
    clear(row_ref)
    col_ref[...] = col_in[...]
    score_lists(2, *plan, a_mid, b_low, row_ref, col_ref)


def f32(*shape):
    return jax.ShapeDtypeStruct(shape, jnp.float32)


def shards(n):
    return jax.ShapeDtypeStruct((n, SHARD, D), jnp.bfloat16)


def rows_of(n):
    return f32(n, SHARD, 128)


def cols_of(n):
    return f32(n, 8, SHARD)


def kernel_call(kernel, operands, outs, scratch, flops, smem=3):
    return pl.pallas_call(
        kernel,
        out_shape=outs,
        in_specs=[spec(SMEM)] * smem + [spec(VMEM)] * (len(operands) - smem),
        out_specs=jax.tree.map(lambda _: spec(VMEM), outs),
        scratch_shapes=[VMEM(x.shape, x.dtype) for x in scratch],
        compiler_params=params(),
        cost_estimate=pl.CostEstimate(flops=flops, bytes_accessed=8000000, transcendentals=0),
    )(*operands)


def early_call(plan, *operands):
    outs = (rows_of(6), cols_of(2))
    return kernel_call(early_kernel, [*plan, *operands], outs, [], 3000000000)


def second_call(plan, *operands):
    outs = (f32(6, SHARD), cols_of(8), shards(8))
    scratch = [rows_of(6), cols_of(6)]
    return kernel_call(second_kernel, [*plan, *operands], outs, scratch, 3000000000)


def middle_call(plan, *operands):
    outs = (rows_of(6), cols_of(8))
    return kernel_call(middle_kernel, [*plan, *operands], outs, [], 5000000000)


KEPT = (0, 1, 2, 4)
SENT = (3, 6, 5, 7)


def last_kernel(*refs):
    plan, mine, refs = refs[:3], refs[3:5], refs[5:]
    a_mid, b_low, b_mid, row_in, col_in, row_ref, col_ref, a_buf, b_buf = refs
    a_buf[:6] = a_mid[...]
    b_buf[:8] = b_low[...]
    b_buf[8:] = b_mid[...]
    for half in range(2):
        a_buf[6 + half] = mine[half][...]
    row_ref[:6] = row_in[...]
    row_ref[6:] = jnp.full((2, SHARD, 128), -2.0, jnp.float32)
    col_ref[:8] = col_in[...]
    col_ref[8:] = jnp.full((6, 8, SHARD), -2.0, jnp.float32)
    score_lists(3, *plan, a_buf, b_buf, row_ref, col_ref)


def last_call(plan, *operands):
    outs = (rows_of(8), cols_of(14))
    return kernel_call(last_kernel, [*plan, *operands], outs, [shards(8), shards(14)], 5000000000)


def final_kernel(*refs):
    plan, mine, theirs, refs = refs[:3], refs[3:5], refs[5:7], refs[7:]
    rows0, row_in, col_in, keep_ref, send_ref, other_ref, a_buf, b_buf, row_ref, col_ref = refs
    for half in range(2):
        a_buf[half] = mine[half][...]
        b_buf[half] = theirs[half][...]
    row_ref[...] = row_in[6:]
    clear(col_ref)
    score_lists(4, *plan, a_buf, b_buf, row_ref, col_ref)
    keep_ref[0:2] = jnp.full((2, SHARD), -2.0, jnp.float32)
    for out_ref, slots in ((keep_ref, KEPT), (send_ref, SENT)):
        for place, slot in enumerate(slots):
            if slot == 7:
                put_rows(out_ref, 2 * place, row_ref, 0)
            elif slot > 3:
                put_rows(out_ref, 2 * place, row_in, 2 * slot - 8)
            elif slot > 0:
                out_ref[2 * place : 2 * place + 2] = rows0[2 * slot - 2 : 2 * slot]
    for place, slot in enumerate(KEPT + SENT):
        for half in range(2):
            at = 2 * place + half
            down = col_ref[half] if slot == 7 else col_in[2 * slot + half]
            other_ref[at : at + 1, :] = jnp.max(down, axis=0, keepdims=True)


def final_call(plan, *operands):
    outs = (f32(8, SHARD), f32(8, SHARD), f32(16, SHARD))
    scratch = [shards(2), shards(2), rows_of(2), cols_of(2)]
    return kernel_call(final_kernel, [*plan, *operands], outs, scratch, 500000000)


def swap(x):
    return lax.ppermute(x, ("row", "col"), [(s, s ^ CORE) for s in range(128)])


def exchange(x, generator):
    pairs = [(s, s ^ GENERATORS[(s >> 4) & 1][generator]) for s in range(128)]
    return lax.ppermute(x, ("row", "col"), pairs)


def after(x, *done):
    return lax.optimization_barrier((x, *done))[0]


def body(embeddings, block_cluster):
    here = (lax.axis_index("row") * 16 + lax.axis_index("col")).astype(jnp.int32).reshape(1)
    unit = unit_call(here, embeddings, swap(embeddings))
    plan = plan_call(here, block_cluster)
    mine = [unit]

    def step(slots):
        return [exchange(mine[SENDS[k - 1][0]], SENDS[k - 1][1]) for k in slots]

    own = own_call(here, block_cluster, unit)
    mine.extend(after(x, plan[2], own) for x in step((1, 2, 3)))
    a_low = kernel_call(pack_kernel, mine[1:4], shards(6), [], 1000000000, 0)
    b_low = swap(a_low)
    rows0, cols = early_call(plan, a_low, unit)
    rows0, cols, b_low = second_call(plan, a_low, unit, b_low, rows0, cols)
    mine.extend(after(x, cols) for x in step((4, 5, 6)))
    halves = [
        exchange(mine[source][half], generator) for half, (source, generator) in enumerate(HALVES)
    ]
    a_mid = kernel_call(pack_kernel, mine[4:7], shards(6), [], 1000000000, 0)
    b_mid = swap(a_mid)
    rows1, cols = middle_call(plan, a_mid, b_low, cols)
    halves = [after(x, cols) for x in halves]
    swapped = [swap(x) for x in halves]
    rows1, cols = last_call(plan, *halves, a_mid, b_low, b_mid, rows1, cols)
    keep, send, other = final_call(plan, *halves, *swapped, rows0, rows1, cols)
    other = swap(other)
    keep = jnp.maximum(keep, other[:8])
    send = jnp.maximum(send, other[8:])
    keep = jnp.maximum(keep, exchange(send, 2))
    keep = jnp.maximum(keep[:4], exchange(keep[4:], 1))
    keep = jnp.maximum(keep[:2], exchange(keep[2:], 0))
    second = (here & CORE) != 0
    ours = jnp.where(second, keep[1], keep[0])
    other = swap(jnp.where(second, keep[0], keep[1]))
    return jnp.maximum(own.reshape(SHARD), jnp.maximum(ours, other))


def solution(mesh):
    placed = (P(("row", "col"), None), P())
    return jax.shard_map(
        body, mesh=mesh, in_specs=placed, out_specs=P(("row", "col")), check_vma=False
    )
```

```python
import jax
import jax.numpy as jnp
from jax import lax
from jax.experimental import pallas as pl
from jax.experimental.pallas import tpu as pltpu
from jax.sharding import PartitionSpec as P

BLK = 256
SHARD = 512
D = 384
VMEM_LIMIT = 20 * 1024 * 1024

CORE = 16
X1, X3, Y1, Y3, Z1, Z3 = 32, 96, 4, 12, 1, 3
GENERATORS = ((X1, Y1, Y3), (X3, Z1, Z3))
SLOTS = ((), (0,), (1,), (2,), (0, 1), (1, 2), (2, 0), (0, 1, 2))
SENDS = ((0, 0), (0, 1), (0, 2), (1, 1), (2, 2), (3, 0))
HALVES = ((5, 0), (6, 1))


def mask_of(core, slot):
    mask = 0
    for generator in SLOTS[slot]:
        mask ^= GENERATORS[core][generator]
    return mask


EARLY = [(g, 0) for g in (1, 2, 3)]
SECOND = [(g, h) for g in (1, 2, 3) for h in range(1, g + 1)]
MIDDLE = [(g, h) for g in (4, 5, 6) for h in range(4)]
LAST = [(g, h) for g in (4, 5, 6) for h in (4, 5, 6)] + [(7, h) for h in range(7)]
FINAL = [(7, 7)]
PHASES = ((EARLY, 1, 0), (SECOND, 1, 1), (MIDDLE, 4, 0), (LAST, 4, 0), (FINAL, 7, 7))


def shared(g, h):
    return g == h or 4 <= min(g, h) <= max(g, h) <= 6


COUNTS = [sum(2 if shared(g, h) else 4 for g, h in phase[0]) for phase in PHASES]
STARTS = [sum(COUNTS[:n]) + n for n in range(len(PHASES))]
LISTS = sum(COUNTS) + len(PHASES)
MARGIN = 24
MOST = 160
VMEM = pltpu.VMEM
SMEM = pltpu.SMEM


def spec(space):
    return pl.BlockSpec(memory_space=space)


def params():
    return pltpu.CompilerParams(vmem_limit_bytes=VMEM_LIMIT)


def unit_of(x):
    values = x.astype(jnp.float32)
    squares = jnp.sum(values * values, axis=1, keepdims=True)
    return (values * lax.rsqrt(squares + 1e-06)).astype(jnp.bfloat16)


def first_kernel(x_ref, out_ref):
    out_ref[...] = unit_of(x_ref[...])


def pair_kernel(here_ref, own_ref, other_ref, out_ref):
    core = (here_ref[0] >> 4) & 1
    out_ref[core] = own_ref[...]
    out_ref[1 - core] = unit_of(other_ref[...])


def unit_call(here, x, other):
    cost = pl.CostEstimate(flops=1000000, bytes_accessed=1600000, transcendentals=512)
    own = pl.pallas_call(
        first_kernel,
        out_shape=jax.ShapeDtypeStruct((SHARD, D), jnp.bfloat16),
        in_specs=[spec(VMEM)],
        out_specs=spec(VMEM),
        compiler_params=params(),
        cost_estimate=cost,
    )(x)
    return pl.pallas_call(
        pair_kernel,
        out_shape=jax.ShapeDtypeStruct((2, SHARD, D), jnp.bfloat16),
        in_specs=[spec(SMEM), spec(VMEM), spec(VMEM)],
        out_specs=spec(VMEM),
        compiler_params=params(),
        cost_estimate=cost,
    )(here, own, other)


def dot(a, b):
    return lax.dot_general(a, b, (((1,), (1,)), ((), ())), preferred_element_type=jnp.float32)


def plan_kernel(here_ref, cluster_ref, blocks_ref, full_ref, part_ref, count_ref, mine, theirs, share):
    here = here_ref[0]
    core = (here >> 4) & 1
    masks = [[mask_of(c, slot) for slot in range(8)] for c in range(2)]
    for slot in range(8):
        for ref, one, two in ((mine, 0, 1), (theirs, 1, 0)):
            chip = (here ^ jnp.where(core == 0, masks[one][slot], masks[two][slot])) & ~CORE
            for half in range(2):
                block = 2 * (chip | (half * CORE))
                ref[2 * slot + half] = cluster_ref[block] | (cluster_ref[block + 1] << 4)

    first = jnp.sum(jnp.where(blocks_ref[...] < cluster_ref[128], 1, 0))

    def held(slab):
        low, high = slab * 64, slab * 64 + 64
        return jnp.maximum(jnp.minimum(high, first + MOST) - jnp.maximum(low, first), 0)

    slab = here >> 5
    ours = held(slab)
    share[0] = 0
    for other in range(1, 4):
        there = held(slab ^ other)
        share[other] = jnp.where(
            ours + MARGIN <= there, 1, jnp.where(there + MARGIN <= ours, 2, 0)
        )

    for phase, (pairs, base_a, base_b) in enumerate(PHASES):
        full = jnp.int32(STARTS[phase])
        part = jnp.int32(STARTS[phase])

        def candidate(full, part, wanted, g, side, h, far):
            a, b = mine[2 * g + side], theirs[2 * h + far]
            same = a ^ b
            left, right = (a >> 4) ^ b, a ^ (b >> 4)
            quads = (
                jnp.where((same & 15) == 0, 1, 0)
                | jnp.where((right & 15) == 0, 2, 0)
                | jnp.where((left & 15) == 0, 4, 0)
                | jnp.where((same & 240) == 0, 8, 0)
            )
            code = (2 * (g - base_a) + side) | ((2 * (h - base_b) + far) << 4)
            full_ref[full] = code
            part_ref[part] = code | (quads << 8)
            whole = quads == 15
            full = full + jnp.where(wanted & whole, 1, 0)
            part = part + jnp.where(wanted & (quads != 0) & jnp.logical_not(whole), 1, 0)
            return full, part

        for g, h in pairs:
            w = jnp.where(
                core == 0, masks[0][g] ^ masks[1][h], masks[1][g] ^ masks[0][h]
            )
            kind = share[(w >> 5) & 3]
            bit = jnp.where((here & (w & -w)) != 0, 1, 0) ^ ((g + h) % 2)
            whole, half = kind == 1, kind == 0
            mixed = ((whole | half, core, 1 - core), (whole, 1 - core, core))
            plain = ((whole | (half & (bit == 0)), 0, 0), (whole | (half & (bit == 1)), 1, 1))
            if shared(g, h):
                for (one, side, far), (two, _, _), n in zip(mixed, plain, (0, 1)):
                    wanted = ((core == 0) & one) | ((core == 1) & two)
                    side = jnp.where(core == 0, side, n)
                    far = jnp.where(core == 0, far, n)
                    full, part = candidate(full, part, wanted, g, side, h, far)
            else:
                for wanted, side, far in mixed + plain:
                    full, part = candidate(full, part, wanted, g, side, h, far)
        count_ref[2 * phase] = full - STARTS[phase]
        count_ref[2 * phase + 1] = part - STARTS[phase]


def own_kernel(here_ref, cluster_ref, unit_ref, own_ref):
    here = here_ref[0]
    core = (here >> 4) & 1
    first0 = cluster_ref[2 * here]
    first1 = cluster_ref[2 * here + 1]
    there = here ^ CORE
    second0 = cluster_ref[2 * there]
    second1 = cluster_ref[2 * there + 1]
    mine = unit_ref[core]
    best = jnp.full((8, SHARD), -2.0, jnp.float32)
    col = lax.broadcasted_iota(jnp.int32, (BLK, SHARD), 1)
    row = lax.broadcasted_iota(jnp.int32, (BLK, SHARD), 0)
    label = jnp.where(col[:1] < BLK, first0, first1)
    for half, name in ((0, first0), (1, first1)):
        scores = dot(unit_ref[core, half * BLK : half * BLK + BLK, :], mine)
        keep = (row + half * BLK != col) & (label == name)
        scores = jnp.where(keep, scores, jnp.float32(-2.0))
        best = jnp.maximum(best, jnp.max(scores.reshape(BLK // 8, 8, SHARD), axis=0))
    for half, name in ((0, second0), (1, second1)):
        scores = dot(unit_ref[1 - core, half * BLK : half * BLK + BLK, :], mine)
        scores = jnp.where(label == name, scores, jnp.float32(-2.0))
        best = jnp.maximum(best, jnp.max(scores.reshape(BLK // 8, 8, SHARD), axis=0))
    own_ref[...] = jnp.max(best, axis=0, keepdims=True)


def plan_call(here, cluster):
    lists = jax.ShapeDtypeStruct((LISTS,), jnp.int32)
    return pl.pallas_call(
        plan_kernel,
        out_shape=(lists, lists, jax.ShapeDtypeStruct((2 * len(PHASES),), jnp.int32)),
        in_specs=[spec(SMEM), spec(SMEM), spec(VMEM)],
        out_specs=(spec(SMEM),) * 3,
        scratch_shapes=[SMEM((16,), jnp.int32), SMEM((16,), jnp.int32), SMEM((4,), jnp.int32)],
        compiler_params=params(),
        cost_estimate=pl.CostEstimate(flops=3000000000, bytes_accessed=10000, transcendentals=0),
    )(here, cluster, cluster.reshape(2, 128))


def own_call(here, cluster, unit):
    return pl.pallas_call(
        own_kernel,
        out_shape=jax.ShapeDtypeStruct((1, SHARD), jnp.float32),
        in_specs=[spec(SMEM), spec(SMEM), spec(VMEM)],
        out_specs=spec(VMEM),
        compiler_params=params(),
        cost_estimate=pl.CostEstimate(flops=1000000000, bytes_accessed=1000000, transcendentals=0),
    )(here, cluster, unit)


def fold(row_ref, col_ref, i, j, rows, cols, scores):
    best = scores[:, :128]
    for k in range(1, scores.shape[1] // 128):
        best = jnp.maximum(best, scores[:, 128 * k : 128 * k + 128])
    row_ref[i, rows, :] = jnp.maximum(row_ref[i, rows, :], best)
    down = jnp.max(scores.reshape(scores.shape[0] // 8, 8, scores.shape[1]), axis=0)
    col_ref[j, :, cols] = jnp.maximum(col_ref[j, :, cols], down)


def score_full(a_ref, b_ref, row_ref, col_ref, word):
    i = word & 15
    j = (word >> 4) & 15
    scores = dot(a_ref[i], b_ref[j])
    fold(row_ref, col_ref, i, j, slice(None), slice(None), scores)


def score_part(a_ref, b_ref, row_ref, col_ref, word):
    i = word & 15
    j = (word >> 4) & 15
    for quad in range(4):

        @pl.when(((word >> (8 + quad)) & 1) == 1)
        def _():
            rows = pl.ds((quad // 2) * BLK, BLK)
            cols = pl.ds((quad % 2) * BLK, BLK)
            scores = dot(a_ref[i, rows, :], b_ref[j, cols, :])
            fold(row_ref, col_ref, i, j, rows, cols, scores)


def score_lists(phase, full_ref, part_ref, count_ref, *refs):
    first = STARTS[phase]
    full = count_ref[2 * phase]
    fours = full & ~3

    def items(n, count):
        for k in range(count):
            score_full(*refs, full_ref[first + n + k])

    @pl.loop(0, fours, step=4)
    def _(n):
        items(n, 4)

    @pl.when((full & 2) != 0)
    def _():
        items(fours, 2)

    @pl.when((full & 1) != 0)
    def _():
        items(full - 1, 1)

    @pl.loop(0, count_ref[2 * phase + 1])
    def _(n):
        score_part(*refs, part_ref[first + n])


def put_rows(out_ref, place, row_ref, first):
    for half in range(2):
        at = place + half
        for k in range(SHARD // 128):
            part = row_ref[first + half, 128 * k : 128 * k + 128, :].T
            out_ref[at : at + 1, 128 * k : 128 * k + 128] = jnp.max(part, axis=0, keepdims=True)


def clear(*refs):
    for ref in refs:
        ref[...] = jnp.full(ref.shape, -2.0, jnp.float32)


def put(buf, refs):
    for n, ref in enumerate(refs):
        buf[2 * n : 2 * n + 2] = ref[...]


def pack_kernel(a_ref, b_ref, c_ref, out_ref):
    put(out_ref, (a_ref, b_ref, c_ref))


def early_kernel(*refs):
    plan, (a_low, unit, row_ref, col_ref) = refs[:3], refs[3:]
    clear(row_ref, col_ref)
    score_lists(0, *plan, a_low, unit, row_ref, col_ref)


def second_kernel(*refs):
    plan, mine, refs = refs[:3], refs[3:6], refs[6:]
    a_low, unit, b_in, row_in, col_in, rows_out, col_ref, a_mid, b_low, row_ref, col_low = refs
    put(a_mid, mine)
    b_low[:2] = unit[...]
    b_low[2:] = b_in[...]
    row_ref[...] = row_in[...]
    clear(col_low)
    score_lists(1, *plan, a_low, b_in, row_ref, col_low)
    col_ref[:2] = col_in[...]
    col_ref[2:] = col_low[...]
    for n in range(0, 6, 2):
        put_rows(rows_out, n, row_ref, n)


def middle_kernel(*refs):
    plan, (a_mid, b_low, col_in, row_ref, col_ref) = refs[:3], refs[3:]
    clear(row_ref)
    col_ref[...] = col_in[...]
    score_lists(2, *plan, a_mid, b_low, row_ref, col_ref)


def f32(*shape):
    return jax.ShapeDtypeStruct(shape, jnp.float32)


def shards(n):
    return jax.ShapeDtypeStruct((n, SHARD, D), jnp.bfloat16)


def rows_of(n):
    return f32(n, SHARD, 128)


def cols_of(n):
    return f32(n, 8, SHARD)


def kernel_call(kernel, operands, outs, scratch, flops, smem=3):
    return pl.pallas_call(
        kernel,
        out_shape=outs,
        in_specs=[spec(SMEM)] * smem + [spec(VMEM)] * (len(operands) - smem),
        out_specs=jax.tree.map(lambda _: spec(VMEM), outs),
        scratch_shapes=[VMEM(x.shape, x.dtype) for x in scratch],
        compiler_params=params(),
        cost_estimate=pl.CostEstimate(flops=flops, bytes_accessed=8000000, transcendentals=0),
    )(*operands)


def early_call(plan, *operands):
    outs = (rows_of(6), cols_of(2))
    return kernel_call(early_kernel, [*plan, *operands], outs, [], 30000000000)


def second_call(plan, *operands):
    outs = (f32(6, SHARD), cols_of(8), shards(6), shards(8))
    scratch = [rows_of(6), cols_of(6)]
    return kernel_call(second_kernel, [*plan, *operands], outs, scratch, 3000000000)


def middle_call(plan, *operands):
    outs = (rows_of(6), cols_of(8))
    return kernel_call(middle_kernel, [*plan, *operands], outs, [], 30000000000)


KEPT = (0, 1, 2, 4)
SENT = (3, 6, 5, 7)


def last_kernel(*refs):
    plan, mine, refs = refs[:3], refs[3:5], refs[5:]
    a_mid, b_low, b_mid, row_in, col_in, row_ref, col_ref, a_buf, b_buf = refs
    a_buf[:6] = a_mid[...]
    b_buf[:8] = b_low[...]
    b_buf[8:] = b_mid[...]
    for half in range(2):
        a_buf[6 + half] = mine[half][...]
    row_ref[:6] = row_in[...]
    row_ref[6:] = jnp.full((2, SHARD, 128), -2.0, jnp.float32)
    col_ref[:8] = col_in[...]
    col_ref[8:] = jnp.full((6, 8, SHARD), -2.0, jnp.float32)
    score_lists(3, *plan, a_buf, b_buf, row_ref, col_ref)


def last_call(plan, *operands):
    outs = (rows_of(8), cols_of(14))
    return kernel_call(last_kernel, [*plan, *operands], outs, [shards(8), shards(14)], 5000000000)


def final_kernel(*refs):
    plan, mine, theirs, refs = refs[:3], refs[3:5], refs[5:7], refs[7:]
    rows0, row_in, col_in, keep_ref, send_ref, other_ref, a_buf, b_buf, row_ref, col_ref = refs
    for half in range(2):
        a_buf[half] = mine[half][...]
        b_buf[half] = theirs[half][...]
    row_ref[...] = row_in[6:]
    clear(col_ref)
    score_lists(4, *plan, a_buf, b_buf, row_ref, col_ref)
    keep_ref[0:2] = jnp.full((2, SHARD), -2.0, jnp.float32)
    for out_ref, slots in ((keep_ref, KEPT), (send_ref, SENT)):
        for place, slot in enumerate(slots):
            if slot == 7:
                put_rows(out_ref, 2 * place, row_ref, 0)
            elif slot > 3:
                put_rows(out_ref, 2 * place, row_in, 2 * slot - 8)
            elif slot > 0:
                out_ref[2 * place : 2 * place + 2] = rows0[2 * slot - 2 : 2 * slot]
    for place, slot in enumerate(KEPT + SENT):
        for half in range(2):
            at = 2 * place + half
            down = col_ref[half] if slot == 7 else col_in[2 * slot + half]
            other_ref[at : at + 1, :] = jnp.max(down, axis=0, keepdims=True)


def final_call(plan, *operands):
    outs = (f32(8, SHARD), f32(8, SHARD), f32(16, SHARD))
    scratch = [shards(2), shards(2), rows_of(2), cols_of(2)]
    return kernel_call(final_kernel, [*plan, *operands], outs, scratch, 500000000)


def swap(x):
    return lax.ppermute(x, ("row", "col"), [(s, s ^ CORE) for s in range(128)])


def exchange(x, generator):
    pairs = [(s, s ^ GENERATORS[(s >> 4) & 1][generator]) for s in range(128)]
    return lax.ppermute(x, ("row", "col"), pairs)


def after(x, *done):
    return lax.optimization_barrier((x, *done))[0]


def body(embeddings, block_cluster):
    here = (lax.axis_index("row") * 16 + lax.axis_index("col")).astype(jnp.int32).reshape(1)
    unit = unit_call(here, embeddings, swap(embeddings))
    plan = plan_call(here, block_cluster)
    mine = [unit]

    def step(slots):
        return [exchange(mine[SENDS[k - 1][0]], SENDS[k - 1][1]) for k in slots]

    own = own_call(here, block_cluster, unit)
    mine.extend(after(x, plan[2], own) for x in step((1, 2, 3)))
    a_low = kernel_call(pack_kernel, mine[1:4], shards(6), [], 1000000000, 0)
    b_low = swap(a_low)
    rows0, cols = early_call(plan, a_low, unit)
    mine.extend(after(x, rows0) for x in step((4, 5, 6)))
    halves = [
        exchange(mine[source][half], generator) for half, (source, generator) in enumerate(HALVES)
    ]
    rows0, cols, a_mid, b_low = second_call(plan, *mine[4:7], a_low, unit, b_low, rows0, cols)
    b_mid = swap(a_mid)
    rows1, cols = middle_call(plan, a_mid, b_low, cols)
    halves = [after(x, cols) for x in halves]
    swapped = [swap(x) for x in halves]
    rows1, cols = last_call(plan, *halves, a_mid, b_low, b_mid, rows1, cols)
    keep, send, other = final_call(plan, *halves, *swapped, rows0, rows1, cols)
    other = swap(other)
    keep = jnp.maximum(keep, other[:8])
    send = jnp.maximum(send, other[8:])
    keep = jnp.maximum(keep, exchange(send, 2))
    keep = jnp.maximum(keep[:4], exchange(keep[4:], 1))
    keep = jnp.maximum(keep[:2], exchange(keep[2:], 0))
    second = (here & CORE) != 0
    ours = jnp.where(second, keep[1], keep[0])
    other = swap(jnp.where(second, keep[0], keep[1]))
    return jnp.maximum(own.reshape(SHARD), jnp.maximum(ours, other))


def solution(mesh):
    placed = (P(("row", "col"), None), P())
    return jax.shard_map(
        body, mesh=mesh, in_specs=placed, out_specs=P(("row", "col")), check_vma=False
    )
```

```python
import jax
import jax.numpy as jnp
from jax import lax
from jax.experimental import pallas as pl
from jax.experimental.pallas import tpu as pltpu
from jax.sharding import PartitionSpec as P

BLK = 256
SHARD = 512
D = 384
VMEM_LIMIT = 20 * 1024 * 1024

CORE = 16
X1, X3, Y1, Y3, Z1, Z3 = 32, 96, 4, 12, 1, 3
GENERATORS = ((X1, Y1, Y3), (X3, Z1, Z3))
SLOTS = ((), (0,), (1,), (2,), (0, 1), (1, 2), (2, 0), (0, 1, 2))
SENDS = ((0, 0), (0, 1), (0, 2), (1, 1), (2, 2), (3, 0))
HALVES = ((5, 0), (6, 1))


def mask_of(core, slot):
    mask = 0
    for generator in SLOTS[slot]:
        mask ^= GENERATORS[core][generator]
    return mask


EARLY = [(g, 0) for g in (1, 2, 3)]
SECOND = [(g, h) for g in (1, 2, 3) for h in range(1, g + 1)]
MIDDLE = [(g, h) for g in (4, 5, 6) for h in range(4)]
LAST = [(g, h) for g in (4, 5, 6) for h in (4, 5, 6)] + [(7, h) for h in range(7)]
FINAL = [(7, 7)]
PHASES = ((EARLY, 1, 0), (SECOND, 1, 1), (MIDDLE, 4, 0), (LAST, 4, 0), (FINAL, 7, 7))


def shared(g, h):
    return g == h or 4 <= min(g, h) <= max(g, h) <= 6


COUNTS = [sum(2 if shared(g, h) else 4 for g, h in phase[0]) for phase in PHASES]
STARTS = [sum(COUNTS[:n]) + n for n in range(len(PHASES))]
LISTS = sum(COUNTS) + len(PHASES)
MARGIN = 24
MOST = 160
VMEM = pltpu.VMEM
SMEM = pltpu.SMEM


def spec(space):
    return pl.BlockSpec(memory_space=space)


def params():
    return pltpu.CompilerParams(vmem_limit_bytes=VMEM_LIMIT)


def unit_of(x):
    values = x.astype(jnp.float32)
    squares = jnp.sum(values * values, axis=1, keepdims=True)
    return (values * lax.rsqrt(squares + 1e-06)).astype(jnp.bfloat16)


def first_kernel(x_ref, out_ref):
    out_ref[...] = unit_of(x_ref[...])


def pair_kernel(here_ref, own_ref, other_ref, out_ref):
    core = (here_ref[0] >> 4) & 1
    out_ref[core] = own_ref[...]
    out_ref[1 - core] = unit_of(other_ref[...])


def unit_call(here, x, other):
    cost = pl.CostEstimate(flops=1000000, bytes_accessed=1600000, transcendentals=512)
    own = pl.pallas_call(
        first_kernel,
        out_shape=jax.ShapeDtypeStruct((SHARD, D), jnp.bfloat16),
        in_specs=[spec(VMEM)],
        out_specs=spec(VMEM),
        compiler_params=params(),
        cost_estimate=cost,
    )(x)
    return pl.pallas_call(
        pair_kernel,
        out_shape=jax.ShapeDtypeStruct((2, SHARD, D), jnp.bfloat16),
        in_specs=[spec(SMEM), spec(VMEM), spec(VMEM)],
        out_specs=spec(VMEM),
        compiler_params=params(),
        cost_estimate=cost,
    )(here, own, other)


def dot(a, b):
    return lax.dot_general(a, b, (((1,), (1,)), ((), ())), preferred_element_type=jnp.float32)


def plan_kernel(here_ref, cluster_ref, blocks_ref, full_ref, part_ref, count_ref, mine, theirs, share):
    here = here_ref[0]
    core = (here >> 4) & 1
    masks = [[mask_of(c, slot) for slot in range(8)] for c in range(2)]
    for slot in range(8):
        for ref, one, two in ((mine, 0, 1), (theirs, 1, 0)):
            chip = (here ^ jnp.where(core == 0, masks[one][slot], masks[two][slot])) & ~CORE
            for half in range(2):
                block = 2 * (chip | (half * CORE))
                ref[2 * slot + half] = cluster_ref[block] | (cluster_ref[block + 1] << 4)

    first = jnp.sum(jnp.where(blocks_ref[...] < cluster_ref[128], 1, 0))

    def held(slab):
        low, high = slab * 64, slab * 64 + 64
        return jnp.maximum(jnp.minimum(high, first + MOST) - jnp.maximum(low, first), 0)

    slab = here >> 5
    ours = held(slab)
    share[0] = 0
    for other in range(1, 4):
        there = held(slab ^ other)
        share[other] = jnp.where(
            ours + MARGIN <= there, 1, jnp.where(there + MARGIN <= ours, 2, 0)
        )

    for phase, (pairs, base_a, base_b) in enumerate(PHASES):
        full = jnp.int32(STARTS[phase])
        part = jnp.int32(STARTS[phase])

        def candidate(full, part, wanted, g, side, h, far):
            a, b = mine[2 * g + side], theirs[2 * h + far]
            same = a ^ b
            left, right = (a >> 4) ^ b, a ^ (b >> 4)
            quads = (
                jnp.where((same & 15) == 0, 1, 0)
                | jnp.where((right & 15) == 0, 2, 0)
                | jnp.where((left & 15) == 0, 4, 0)
                | jnp.where((same & 240) == 0, 8, 0)
            )
            code = (2 * (g - base_a) + side) | ((2 * (h - base_b) + far) << 4)
            full_ref[full] = code
            part_ref[part] = code | (quads << 8)
            whole = quads == 15
            full = full + jnp.where(wanted & whole, 1, 0)
            part = part + jnp.where(wanted & (quads != 0) & jnp.logical_not(whole), 1, 0)
            return full, part

        for g, h in pairs:
            w = jnp.where(
                core == 0, masks[0][g] ^ masks[1][h], masks[1][g] ^ masks[0][h]
            )
            kind = share[(w >> 5) & 3]
            bit = jnp.where((here & (w & -w)) != 0, 1, 0) ^ ((g + h) % 2)
            whole, half = kind == 1, kind == 0
            mixed = ((whole | half, core, 1 - core), (whole, 1 - core, core))
            plain = ((whole | (half & (bit == 0)), 0, 0), (whole | (half & (bit == 1)), 1, 1))
            if shared(g, h):
                for (one, side, far), (two, _, _), n in zip(mixed, plain, (0, 1)):
                    wanted = ((core == 0) & one) | ((core == 1) & two)
                    side = jnp.where(core == 0, side, n)
                    far = jnp.where(core == 0, far, n)
                    full, part = candidate(full, part, wanted, g, side, h, far)
            else:
                for wanted, side, far in mixed + plain:
                    full, part = candidate(full, part, wanted, g, side, h, far)
        count_ref[2 * phase] = full - STARTS[phase]
        count_ref[2 * phase + 1] = part - STARTS[phase]


def own_kernel(here_ref, cluster_ref, unit_ref, own_ref):
    here = here_ref[0]
    core = (here >> 4) & 1
    first0 = cluster_ref[2 * here]
    first1 = cluster_ref[2 * here + 1]
    there = here ^ CORE
    second0 = cluster_ref[2 * there]
    second1 = cluster_ref[2 * there + 1]
    mine = unit_ref[core]
    best = jnp.full((8, SHARD), -2.0, jnp.float32)
    col = lax.broadcasted_iota(jnp.int32, (BLK, SHARD), 1)
    row = lax.broadcasted_iota(jnp.int32, (BLK, SHARD), 0)
    label = jnp.where(col[:1] < BLK, first0, first1)
    for half, name in ((0, first0), (1, first1)):
        scores = dot(unit_ref[core, half * BLK : half * BLK + BLK, :], mine)
        keep = (row + half * BLK != col) & (label == name)
        scores = jnp.where(keep, scores, jnp.float32(-2.0))
        best = jnp.maximum(best, jnp.max(scores.reshape(BLK // 8, 8, SHARD), axis=0))
    for half, name in ((0, second0), (1, second1)):
        scores = dot(unit_ref[1 - core, half * BLK : half * BLK + BLK, :], mine)
        scores = jnp.where(label == name, scores, jnp.float32(-2.0))
        best = jnp.maximum(best, jnp.max(scores.reshape(BLK // 8, 8, SHARD), axis=0))
    own_ref[...] = jnp.max(best, axis=0, keepdims=True)


def plan_call(here, cluster):
    lists = jax.ShapeDtypeStruct((LISTS,), jnp.int32)
    return pl.pallas_call(
        plan_kernel,
        out_shape=(lists, lists, jax.ShapeDtypeStruct((2 * len(PHASES),), jnp.int32)),
        in_specs=[spec(SMEM), spec(SMEM), spec(VMEM)],
        out_specs=(spec(SMEM),) * 3,
        scratch_shapes=[SMEM((16,), jnp.int32), SMEM((16,), jnp.int32), SMEM((4,), jnp.int32)],
        compiler_params=params(),
        cost_estimate=pl.CostEstimate(flops=3000000000, bytes_accessed=10000, transcendentals=0),
    )(here, cluster, cluster.reshape(2, 128))


def own_call(here, cluster, unit):
    return pl.pallas_call(
        own_kernel,
        out_shape=jax.ShapeDtypeStruct((1, SHARD), jnp.float32),
        in_specs=[spec(SMEM), spec(SMEM), spec(VMEM)],
        out_specs=spec(VMEM),
        compiler_params=params(),
        cost_estimate=pl.CostEstimate(flops=1000000000, bytes_accessed=1000000, transcendentals=0),
    )(here, cluster, unit)


def fold(row_ref, col_ref, i, j, rows, cols, scores):
    best = scores[:, :128]
    for k in range(1, scores.shape[1] // 128):
        best = jnp.maximum(best, scores[:, 128 * k : 128 * k + 128])
    row_ref[i, rows, :] = jnp.maximum(row_ref[i, rows, :], best)
    down = jnp.max(scores.reshape(scores.shape[0] // 8, 8, scores.shape[1]), axis=0)
    col_ref[j, :, cols] = jnp.maximum(col_ref[j, :, cols], down)


def score_full(a_ref, b_ref, row_ref, col_ref, word):
    i = word & 15
    j = (word >> 4) & 15
    scores = dot(a_ref[i], b_ref[j])
    fold(row_ref, col_ref, i, j, slice(None), slice(None), scores)


def score_part(a_ref, b_ref, row_ref, col_ref, word):
    i = word & 15
    j = (word >> 4) & 15
    for quad in range(4):

        @pl.when(((word >> (8 + quad)) & 1) == 1)
        def _():
            rows = pl.ds((quad // 2) * BLK, BLK)
            cols = pl.ds((quad % 2) * BLK, BLK)
            scores = dot(a_ref[i, rows, :], b_ref[j, cols, :])
            fold(row_ref, col_ref, i, j, rows, cols, scores)


def score_lists(phase, full_ref, part_ref, count_ref, *refs):
    first = STARTS[phase]
    full = count_ref[2 * phase]
    fours = full & ~3

    def items(n, count):
        for k in range(count):
            score_full(*refs, full_ref[first + n + k])

    @pl.loop(0, fours, step=4)
    def _(n):
        items(n, 4)

    @pl.when((full & 2) != 0)
    def _():
        items(fours, 2)

    @pl.when((full & 1) != 0)
    def _():
        items(full - 1, 1)

    @pl.loop(0, count_ref[2 * phase + 1])
    def _(n):
        score_part(*refs, part_ref[first + n])


def put_rows(out_ref, place, row_ref, first):
    for half in range(2):
        for k in range(SHARD // 128):
            part = row_ref[first + half, 128 * k : 128 * k + 128, :].T
            out_ref[place, pl.ds(4 * half + k, 1), :] = jnp.max(part, axis=0, keepdims=True)


def put_cols(out_ref, place, col_ref, first):
    for half in range(2):
        down = jnp.max(col_ref[first + half], axis=0, keepdims=True)
        for k in range(SHARD // 128):
            out_ref[place, pl.ds(4 * half + k, 1), :] = down[:, 128 * k : 128 * k + 128]


def clear(*refs):
    for ref in refs:
        ref[...] = jnp.full(ref.shape, -2.0, jnp.float32)


def put(buf, refs):
    for n, ref in enumerate(refs):
        buf[2 * n : 2 * n + 2] = ref[...]


def pack_kernel(a_ref, b_ref, c_ref, out_ref):
    put(out_ref, (a_ref, b_ref, c_ref))


def early_kernel(*refs):
    plan, (a_low, unit, row_ref, col_ref) = refs[:3], refs[3:]
    clear(row_ref, col_ref)
    score_lists(0, *plan, a_low, unit, row_ref, col_ref)


def second_kernel(*refs):
    plan, (a_low, unit, b_in, row_in, col_in), outs = refs[:3], refs[3:8], refs[8:]
    rows_out, col_ref, b_low, row_ref, col_low = outs
    b_low[:2] = unit[...]
    b_low[2:] = b_in[...]
    row_ref[...] = row_in[...]
    clear(col_low)
    score_lists(1, *plan, a_low, b_in, row_ref, col_low)
    col_ref[:2] = col_in[...]
    col_ref[2:] = col_low[...]
    for n in range(3):
        put_rows(rows_out, n, row_ref, 2 * n)


def middle_kernel(*refs):
    plan, (a_mid, b_low, col_in, row_ref, col_ref) = refs[:3], refs[3:]
    clear(row_ref)
    col_ref[...] = col_in[...]
    score_lists(2, *plan, a_mid, b_low, row_ref, col_ref)


def f32(*shape):
    return jax.ShapeDtypeStruct(shape, jnp.float32)


def shards(n):
    return jax.ShapeDtypeStruct((n, SHARD, D), jnp.bfloat16)


def rows_of(n):
    return f32(n, SHARD, 128)


def cols_of(n):
    return f32(n, 8, SHARD)


def kernel_call(kernel, operands, outs, scratch, flops, smem=3):
    return pl.pallas_call(
        kernel,
        out_shape=outs,
        in_specs=[spec(SMEM)] * smem + [spec(VMEM)] * (len(operands) - smem),
        out_specs=jax.tree.map(lambda _: spec(VMEM), outs),
        scratch_shapes=[VMEM(x.shape, x.dtype) for x in scratch],
        compiler_params=params(),
        cost_estimate=pl.CostEstimate(flops=flops, bytes_accessed=8000000, transcendentals=0),
    )(*operands)


def early_call(plan, *operands):
    outs = (rows_of(6), cols_of(2))
    return kernel_call(early_kernel, [*plan, *operands], outs, [], 30000000000)


def second_call(plan, *operands):
    outs = (f32(3, 8, 128), cols_of(8), shards(8))
    scratch = [rows_of(6), cols_of(6)]
    return kernel_call(second_kernel, [*plan, *operands], outs, scratch, 3000000000)


def middle_call(plan, *operands):
    outs = (rows_of(6), cols_of(8))
    return kernel_call(middle_kernel, [*plan, *operands], outs, [], 30000000000)


def last_kernel(*refs):
    plan, mine, refs = refs[:3], refs[3:5], refs[5:]
    a_mid, b_low, b_mid, row_in, col_in, row_ref, col_ref, a_buf, b_buf = refs
    a_buf[:6] = a_mid[...]
    b_buf[:8] = b_low[...]
    b_buf[8:] = b_mid[...]
    for half in range(2):
        a_buf[6 + half] = mine[half][...]
    row_ref[:6] = row_in[...]
    row_ref[6:] = jnp.full((2, SHARD, 128), -2.0, jnp.float32)
    col_ref[:8] = col_in[...]
    col_ref[8:] = jnp.full((6, 8, SHARD), -2.0, jnp.float32)
    score_lists(3, *plan, a_buf, b_buf, row_ref, col_ref)


def last_call(plan, *operands):
    outs = (rows_of(8), cols_of(14))
    return kernel_call(last_kernel, [*plan, *operands], outs, [shards(8), shards(14)], 5000000000)


def final_kernel(*refs):
    here_ref, plan, mine, theirs, refs = refs[0], refs[1:4], refs[4:6], refs[6:8], refs[8:]
    rows0, row_in, col_in, part_ref, other_ref, a_buf, b_buf, row_ref, col_ref = refs
    for half in range(2):
        a_buf[half] = mine[half][...]
        b_buf[half] = theirs[half][...]
    row_ref[...] = row_in[6:]
    clear(col_ref)
    score_lists(4, *plan, a_buf, b_buf, row_ref, col_ref)
    here = here_ref[0]
    places = place_of(0, here), place_of(1, here)
    core = (here >> 4) & 1
    ours = jnp.where(core == 0, places[0], places[1])
    others = jnp.where(core == 0, places[1], places[0])
    part_ref[ours] = jnp.full((8, 128), -2.0, jnp.float32)
    for slot in range(8):
        place = ours ^ bits_of(slot)
        if slot == 7:
            put_rows(part_ref, place, row_ref, 0)
            put_cols(other_ref, others ^ bits_of(slot), col_ref, 0)
            continue
        if slot > 3:
            put_rows(part_ref, place, row_in, 2 * slot - 8)
        elif slot > 0:
            part_ref[place] = rows0[slot - 1]
        put_cols(other_ref, others ^ bits_of(slot), col_in, 2 * slot)


def final_call(*operands):
    outs = (f32(8, 8, 128), f32(8, 8, 128))
    scratch = [shards(2), shards(2), rows_of(2), cols_of(2)]
    return kernel_call(final_kernel, operands, outs, scratch, 500000000, 4)


def bits_of(slot):
    return sum(1 << generator for generator in SLOTS[slot])


def place_of(core, here):
    if core == 0:
        one, two, three = here >> 5, (here >> 2) ^ (here >> 3), here >> 3
    else:
        one, two, three = here >> 6, here ^ (here >> 1), here >> 1
    return (one & 1) | ((two & 1) << 1) | ((three & 1) << 2)


def groups():
    found = [[0] * 8 for _ in range(16)]
    firsts = {}
    for here in range(128):
        core = (here >> 4) & 1
        first = here
        place = place_of(core, here)
        for generator in range(3):
            if place >> generator & 1:
                first ^= GENERATORS[core][generator]
        found[firsts.setdefault(first, len(firsts))][place] = here
    return found


def swap(x):
    return lax.ppermute(x, ("row", "col"), [(s, s ^ CORE) for s in range(128)])


def exchange(x, generator):
    pairs = [(s, s ^ GENERATORS[(s >> 4) & 1][generator]) for s in range(128)]
    return lax.ppermute(x, ("row", "col"), pairs)


def after(x, *done):
    return lax.optimization_barrier((x, *done))[0]


def body(embeddings, block_cluster):
    here = (lax.axis_index("row") * 16 + lax.axis_index("col")).astype(jnp.int32).reshape(1)
    unit = unit_call(here, embeddings, swap(embeddings))
    plan = plan_call(here, block_cluster)
    mine = [unit]

    def step(slots):
        return [exchange(mine[SENDS[k - 1][0]], SENDS[k - 1][1]) for k in slots]

    own = own_call(here, block_cluster, unit)
    mine.extend(after(x, plan[2], own) for x in step((1, 2, 3)))
    a_low = kernel_call(pack_kernel, mine[1:4], shards(6), [], 1000000000, 0)
    b_low = swap(a_low)
    rows0, cols = early_call(plan, a_low, unit)
    rows0, cols, b_low = second_call(plan, a_low, unit, b_low, rows0, cols)
    mine.extend(after(x, cols) for x in step((4, 5, 6)))
    halves = [
        exchange(mine[source][half], generator) for half, (source, generator) in enumerate(HALVES)
    ]
    a_mid = kernel_call(pack_kernel, mine[4:7], shards(6), [], 1000000000, 0)
    b_mid = swap(a_mid)
    rows1, cols = middle_call(plan, a_mid, b_low, cols)
    halves = [after(x, cols) for x in halves]
    swapped = [swap(x) for x in halves]
    rows1, cols = last_call(plan, *halves, a_mid, b_low, b_mid, rows1, cols)
    part, other = final_call(here, *plan, *halves, *swapped, rows0, rows1, cols)
    part = jnp.maximum(part, swap(other))
    part = lax.all_to_all(part, ("row", "col"), 0, 0, axis_index_groups=groups())
    both = jnp.max(part, axis=0)
    second = (here & CORE) != 0
    ours = jnp.where(second, both[4:], both[:4])
    other = swap(jnp.where(second, both[:4], both[4:]))
    return jnp.maximum(own.reshape(SHARD), jnp.maximum(ours, other).reshape(SHARD))


def solution(mesh):
    placed = (P(("row", "col"), None), P())
    return jax.shard_map(
        body, mesh=mesh, in_specs=placed, out_specs=P(("row", "col")), check_vma=False
    )
```

```python
import jax
import jax.numpy as jnp
from jax import lax
from jax.experimental import pallas as pl
from jax.experimental.pallas import tpu as pltpu
from jax.sharding import PartitionSpec as P

BLK = 256
SHARD = 512
D = 384
VMEM_LIMIT = 20 * 1024 * 1024

CORE = 16
X1, X3, Y1, Y3, Z1, Z3 = 32, 96, 4, 12, 1, 3
GENERATORS = ((X1, Y1, Y3), (X3, Z1, Z3))
SLOTS = ((), (0,), (1,), (2,), (0, 1), (1, 2), (2, 0), (0, 1, 2))
SENDS = ((0, 0), (0, 1), (0, 2), (1, 1), (2, 2), (3, 0))
HALVES = ((5, 0), (6, 1))


def mask_of(core, slot):
    mask = 0
    for generator in SLOTS[slot]:
        mask ^= GENERATORS[core][generator]
    return mask


EARLY = [(g, 0) for g in (1, 2, 3)]
SECOND = [(g, h) for g in (1, 2, 3) for h in range(1, g + 1)]
MIDDLE = [(g, h) for g in (4, 5, 6) for h in range(4)]
LAST = [(g, h) for g in (4, 5, 6) for h in (4, 5, 6)] + [(7, h) for h in range(7)]
FINAL = [(7, 7)]
PHASES = ((EARLY, 1, 0), (SECOND, 1, 1), (MIDDLE, 4, 0), (LAST, 4, 0), (FINAL, 7, 7))


def shared(g, h):
    return g == h or 4 <= min(g, h) <= max(g, h) <= 6


COUNTS = [sum(2 if shared(g, h) else 4 for g, h in phase[0]) for phase in PHASES]
STARTS = [sum(COUNTS[:n]) + n for n in range(len(PHASES))]
LISTS = sum(COUNTS) + len(PHASES)
MARGIN = 24
MOST = 160
VMEM = pltpu.VMEM
SMEM = pltpu.SMEM


def spec(space):
    return pl.BlockSpec(memory_space=space)


def params():
    return pltpu.CompilerParams(vmem_limit_bytes=VMEM_LIMIT)


def unit_of(x):
    values = x.astype(jnp.float32)
    squares = jnp.sum(values * values, axis=1, keepdims=True)
    return (values * lax.rsqrt(squares + 1e-06)).astype(jnp.bfloat16)


def first_kernel(x_ref, out_ref):
    out_ref[...] = unit_of(x_ref[...])


def pair_kernel(here_ref, own_ref, other_ref, out_ref):
    core = (here_ref[0] >> 4) & 1
    out_ref[core] = own_ref[...]
    out_ref[1 - core] = unit_of(other_ref[...])


def unit_call(here, x, other):
    cost = pl.CostEstimate(flops=1000000, bytes_accessed=1600000, transcendentals=512)
    own = pl.pallas_call(
        first_kernel,
        out_shape=jax.ShapeDtypeStruct((SHARD, D), jnp.bfloat16),
        in_specs=[spec(VMEM)],
        out_specs=spec(VMEM),
        compiler_params=params(),
        cost_estimate=cost,
    )(x)
    return pl.pallas_call(
        pair_kernel,
        out_shape=jax.ShapeDtypeStruct((2, SHARD, D), jnp.bfloat16),
        in_specs=[spec(SMEM), spec(VMEM), spec(VMEM)],
        out_specs=spec(VMEM),
        compiler_params=params(),
        cost_estimate=cost,
    )(here, own, other)


def dot(a, b):
    return lax.dot_general(a, b, (((1,), (1,)), ((), ())), preferred_element_type=jnp.float32)


def plan_kernel(here_ref, cluster_ref, blocks_ref, full_ref, part_ref, count_ref, mine, theirs, share):
    here = here_ref[0]
    core = (here >> 4) & 1
    masks = [[mask_of(c, slot) for slot in range(8)] for c in range(2)]
    for slot in range(8):
        for ref, one, two in ((mine, 0, 1), (theirs, 1, 0)):
            chip = (here ^ jnp.where(core == 0, masks[one][slot], masks[two][slot])) & ~CORE
            for half in range(2):
                block = 2 * (chip | (half * CORE))
                ref[2 * slot + half] = cluster_ref[block] | (cluster_ref[block + 1] << 4)

    first = jnp.sum(jnp.where(blocks_ref[...] < cluster_ref[128], 1, 0))

    def held(slab):
        low, high = slab * 64, slab * 64 + 64
        return jnp.maximum(jnp.minimum(high, first + MOST) - jnp.maximum(low, first), 0)

    slab = here >> 5
    ours = held(slab)
    share[0] = 0
    for other in range(1, 4):
        there = held(slab ^ other)
        share[other] = jnp.where(
            ours + MARGIN <= there, 1, jnp.where(there + MARGIN <= ours, 2, 0)
        )

    for phase, (pairs, base_a, base_b) in enumerate(PHASES):
        full = jnp.int32(STARTS[phase])
        part = jnp.int32(STARTS[phase])

        def candidate(full, part, wanted, g, side, h, far):
            a, b = mine[2 * g + side], theirs[2 * h + far]
            same = a ^ b
            left, right = (a >> 4) ^ b, a ^ (b >> 4)
            quads = (
                jnp.where((same & 15) == 0, 1, 0)
                | jnp.where((right & 15) == 0, 2, 0)
                | jnp.where((left & 15) == 0, 4, 0)
                | jnp.where((same & 240) == 0, 8, 0)
            )
            code = (2 * (g - base_a) + side) | ((2 * (h - base_b) + far) << 4)
            full_ref[full] = code
            part_ref[part] = code | (quads << 8)
            whole = quads == 15
            full = full + jnp.where(wanted & whole, 1, 0)
            part = part + jnp.where(wanted & (quads != 0) & jnp.logical_not(whole), 1, 0)
            return full, part

        for g, h in pairs:
            w = jnp.where(
                core == 0, masks[0][g] ^ masks[1][h], masks[1][g] ^ masks[0][h]
            )
            kind = share[(w >> 5) & 3]
            bit = jnp.where((here & (w & -w)) != 0, 1, 0) ^ ((g + h) % 2)
            whole, half = kind == 1, kind == 0
            mixed = ((whole | half, core, 1 - core), (whole, 1 - core, core))
            plain = ((whole | (half & (bit == 0)), 0, 0), (whole | (half & (bit == 1)), 1, 1))
            if shared(g, h):
                for (one, side, far), (two, _, _), n in zip(mixed, plain, (0, 1)):
                    wanted = ((core == 0) & one) | ((core == 1) & two)
                    side = jnp.where(core == 0, side, n)
                    far = jnp.where(core == 0, far, n)
                    full, part = candidate(full, part, wanted, g, side, h, far)
            else:
                for wanted, side, far in mixed + plain:
                    full, part = candidate(full, part, wanted, g, side, h, far)
        count_ref[2 * phase] = full - STARTS[phase]
        count_ref[2 * phase + 1] = part - STARTS[phase]


def own_kernel(here_ref, cluster_ref, unit_ref, own_ref):
    here = here_ref[0]
    core = (here >> 4) & 1
    first0 = cluster_ref[2 * here]
    first1 = cluster_ref[2 * here + 1]
    there = here ^ CORE
    second0 = cluster_ref[2 * there]
    second1 = cluster_ref[2 * there + 1]
    mine = unit_ref[core]
    best = jnp.full((8, SHARD), -2.0, jnp.float32)
    col = lax.broadcasted_iota(jnp.int32, (BLK, SHARD), 1)
    row = lax.broadcasted_iota(jnp.int32, (BLK, SHARD), 0)
    label = jnp.where(col[:1] < BLK, first0, first1)
    for half, name in ((0, first0), (1, first1)):
        scores = dot(unit_ref[core, half * BLK : half * BLK + BLK, :], mine)
        keep = (row + half * BLK != col) & (label == name)
        scores = jnp.where(keep, scores, jnp.float32(-2.0))
        best = jnp.maximum(best, jnp.max(scores.reshape(BLK // 8, 8, SHARD), axis=0))
    for half, name in ((0, second0), (1, second1)):
        scores = dot(unit_ref[1 - core, half * BLK : half * BLK + BLK, :], mine)
        scores = jnp.where(label == name, scores, jnp.float32(-2.0))
        best = jnp.maximum(best, jnp.max(scores.reshape(BLK // 8, 8, SHARD), axis=0))
    own_ref[...] = jnp.max(best, axis=0, keepdims=True)


def plan_call(here, cluster):
    lists = jax.ShapeDtypeStruct((LISTS,), jnp.int32)
    return pl.pallas_call(
        plan_kernel,
        out_shape=(lists, lists, jax.ShapeDtypeStruct((2 * len(PHASES),), jnp.int32)),
        in_specs=[spec(SMEM), spec(SMEM), spec(VMEM)],
        out_specs=(spec(SMEM),) * 3,
        scratch_shapes=[SMEM((16,), jnp.int32), SMEM((16,), jnp.int32), SMEM((4,), jnp.int32)],
        compiler_params=params(),
        cost_estimate=pl.CostEstimate(flops=3000000000, bytes_accessed=10000, transcendentals=0),
    )(here, cluster, cluster.reshape(2, 128))


def own_call(here, cluster, unit):
    return pl.pallas_call(
        own_kernel,
        out_shape=jax.ShapeDtypeStruct((1, SHARD), jnp.float32),
        in_specs=[spec(SMEM), spec(SMEM), spec(VMEM)],
        out_specs=spec(VMEM),
        compiler_params=params(),
        cost_estimate=pl.CostEstimate(flops=1000000000, bytes_accessed=1000000, transcendentals=0),
    )(here, cluster, unit)


def fold(row_ref, col_ref, i, j, rows, cols, scores):
    best = scores[:, :128]
    for k in range(1, scores.shape[1] // 128):
        best = jnp.maximum(best, scores[:, 128 * k : 128 * k + 128])
    row_ref[i, rows, :] = jnp.maximum(row_ref[i, rows, :], best)
    down = jnp.max(scores.reshape(scores.shape[0] // 8, 8, scores.shape[1]), axis=0)
    col_ref[j, :, cols] = jnp.maximum(col_ref[j, :, cols], down)


def score_full(a_ref, b_ref, row_ref, col_ref, word):
    i = word & 15
    j = (word >> 4) & 15
    scores = dot(a_ref[i], b_ref[j])
    fold(row_ref, col_ref, i, j, slice(None), slice(None), scores)


def score_part(a_ref, b_ref, row_ref, col_ref, word):
    i = word & 15
    j = (word >> 4) & 15
    for quad in range(4):

        @pl.when(((word >> (8 + quad)) & 1) == 1)
        def _():
            rows = pl.ds((quad // 2) * BLK, BLK)
            cols = pl.ds((quad % 2) * BLK, BLK)
            scores = dot(a_ref[i, rows, :], b_ref[j, cols, :])
            fold(row_ref, col_ref, i, j, rows, cols, scores)


def score_lists(phase, full_ref, part_ref, count_ref, *refs):
    first = STARTS[phase]
    full = count_ref[2 * phase]
    fours = full & ~3

    def items(n, count):
        for k in range(count):
            score_full(*refs, full_ref[first + n + k])

    @pl.loop(0, fours, step=4)
    def _(n):
        items(n, 4)

    @pl.when((full & 2) != 0)
    def _():
        items(fours, 2)

    @pl.when((full & 1) != 0)
    def _():
        items(full - 1, 1)

    @pl.loop(0, count_ref[2 * phase + 1])
    def _(n):
        score_part(*refs, part_ref[first + n])


def put_rows(out_ref, place, row_ref, first):
    for half in range(2):
        at = place + half
        for k in range(SHARD // 128):
            part = row_ref[first + half, 128 * k : 128 * k + 128, :].T
            out_ref[at : at + 1, 128 * k : 128 * k + 128] = jnp.max(part, axis=0, keepdims=True)


def clear(*refs):
    for ref in refs:
        ref[...] = jnp.full(ref.shape, -2.0, jnp.float32)


def put(buf, refs):
    for n, ref in enumerate(refs):
        buf[2 * n : 2 * n + 2] = ref[...]


def pack_kernel(a_ref, b_ref, c_ref, out_ref):
    put(out_ref, (a_ref, b_ref, c_ref))


def early_kernel(*refs):
    plan, (a_low, unit, row_ref, col_ref) = refs[:3], refs[3:]
    clear(row_ref, col_ref)
    score_lists(0, *plan, a_low, unit, row_ref, col_ref)


def second_kernel(*refs):
    plan, (a_low, unit, b_in, row_in, col_in), outs = refs[:3], refs[3:8], refs[8:]
    rows_out, col_ref, b_low, row_ref, col_low = outs
    b_low[:2] = unit[...]
    b_low[2:] = b_in[...]
    row_ref[...] = row_in[...]
    clear(col_low)
    score_lists(1, *plan, a_low, b_in, row_ref, col_low)
    col_ref[:2] = col_in[...]
    col_ref[2:] = col_low[...]
    for n in range(0, 6, 2):
        put_rows(rows_out, n, row_ref, n)


def middle_kernel(*refs):
    plan, (a_mid, b_low, col_in, row_ref, col_ref) = refs[:3], refs[3:]
    clear(row_ref)
    col_ref[...] = col_in[...]
    score_lists(2, *plan, a_mid, b_low, row_ref, col_ref)


def f32(*shape):
    return jax.ShapeDtypeStruct(shape, jnp.float32)


def shards(n):
    return jax.ShapeDtypeStruct((n, SHARD, D), jnp.bfloat16)


def rows_of(n):
    return f32(n, SHARD, 128)


def cols_of(n):
    return f32(n, 8, SHARD)


def kernel_call(kernel, operands, outs, scratch, flops, smem=3):
    return pl.pallas_call(
        kernel,
        out_shape=outs,
        in_specs=[spec(SMEM)] * smem + [spec(VMEM)] * (len(operands) - smem),
        out_specs=jax.tree.map(lambda _: spec(VMEM), outs),
        scratch_shapes=[VMEM(x.shape, x.dtype) for x in scratch],
        compiler_params=params(),
        cost_estimate=pl.CostEstimate(flops=flops, bytes_accessed=8000000, transcendentals=0),
    )(*operands)


def early_call(plan, *operands):
    outs = (rows_of(6), cols_of(2))
    return kernel_call(early_kernel, [*plan, *operands], outs, [], 30000000000)


def second_call(plan, *operands):
    outs = (f32(6, SHARD), cols_of(8), shards(8))
    scratch = [rows_of(6), cols_of(6)]
    return kernel_call(second_kernel, [*plan, *operands], outs, scratch, 3000000000)


def middle_call(plan, *operands):
    outs = (rows_of(6), cols_of(8))
    return kernel_call(middle_kernel, [*plan, *operands], outs, [], 30000000000)


KEPT = (0, 1, 2, 4)
SENT = (3, 6, 5, 7)


def last_kernel(*refs):
    plan, mine, refs = refs[:3], refs[3:5], refs[5:]
    a_mid, b_low, b_mid, row_in, col_in, row_ref, col_ref, a_buf, b_buf = refs
    a_buf[:6] = a_mid[...]
    b_buf[:8] = b_low[...]
    b_buf[8:] = b_mid[...]
    for half in range(2):
        a_buf[6 + half] = mine[half][...]
    row_ref[:6] = row_in[...]
    row_ref[6:] = jnp.full((2, SHARD, 128), -2.0, jnp.float32)
    col_ref[:8] = col_in[...]
    col_ref[8:] = jnp.full((6, 8, SHARD), -2.0, jnp.float32)
    score_lists(3, *plan, a_buf, b_buf, row_ref, col_ref)


def last_call(plan, *operands):
    outs = (rows_of(8), cols_of(14))
    return kernel_call(last_kernel, [*plan, *operands], outs, [shards(8), shards(14)], 5000000000)


def final_kernel(*refs):
    plan, mine, theirs, refs = refs[:3], refs[3:5], refs[5:7], refs[7:]
    rows0, row_in, col_in, keep_ref, send_ref, other_ref, a_buf, b_buf, row_ref, col_ref = refs
    for half in range(2):
        a_buf[half] = mine[half][...]
        b_buf[half] = theirs[half][...]
    row_ref[...] = row_in[6:]
    clear(col_ref)
    score_lists(4, *plan, a_buf, b_buf, row_ref, col_ref)
    keep_ref[0:2] = jnp.full((2, SHARD), -2.0, jnp.float32)
    for out_ref, slots in ((keep_ref, KEPT), (send_ref, SENT)):
        for place, slot in enumerate(slots):
            if slot == 7:
                put_rows(out_ref, 2 * place, row_ref, 0)
            elif slot > 3:
                put_rows(out_ref, 2 * place, row_in, 2 * slot - 8)
            elif slot > 0:
                out_ref[2 * place : 2 * place + 2] = rows0[2 * slot - 2 : 2 * slot]
    for place, slot in enumerate(KEPT + SENT):
        for half in range(2):
            at = 2 * place + half
            down = col_ref[half] if slot == 7 else col_in[2 * slot + half]
            other_ref[at : at + 1, :] = jnp.max(down, axis=0, keepdims=True)


def final_call(plan, *operands):
    outs = (f32(8, SHARD), f32(8, SHARD), f32(16, SHARD))
    scratch = [shards(2), shards(2), rows_of(2), cols_of(2)]
    return kernel_call(final_kernel, [*plan, *operands], outs, scratch, 500000000)


def swap(x):
    return lax.ppermute(x, ("row", "col"), [(s, s ^ CORE) for s in range(128)])


def exchange(x, generator):
    pairs = [(s, s ^ GENERATORS[(s >> 4) & 1][generator]) for s in range(128)]
    return lax.ppermute(x, ("row", "col"), pairs)


def after(x, *done):
    return lax.optimization_barrier((x, *done))[0]


def body(embeddings, block_cluster):
    here = (lax.axis_index("row") * 16 + lax.axis_index("col")).astype(jnp.int32).reshape(1)
    unit = unit_call(here, embeddings, swap(embeddings))
    plan = plan_call(here, block_cluster)
    mine = [unit]

    def step(slots):
        return [exchange(mine[SENDS[k - 1][0]], SENDS[k - 1][1]) for k in slots]

    own = own_call(here, block_cluster, unit)
    mine.extend(after(x, plan[2], own) for x in step((1, 2, 3)))
    a_low = kernel_call(pack_kernel, mine[1:4], shards(6), [], 1000000000, 0)
    b_low = swap(a_low)
    rows0, cols = early_call(plan, a_low, unit)
    rows0, cols, b_low = second_call(plan, a_low, unit, b_low, rows0, cols)
    mine.extend(after(x, cols) for x in step((4, 5, 6)))
    halves = [
        exchange(mine[source][half], generator) for half, (source, generator) in enumerate(HALVES)
    ]
    a_mid = kernel_call(pack_kernel, mine[4:7], shards(6), [], 1000000000, 0)
    b_mid = swap(a_mid)
    rows1, cols = middle_call(plan, a_mid, b_low, cols)
    halves = [after(x, cols) for x in halves]
    swapped = [swap(x) for x in halves]
    rows1, cols = last_call(plan, *halves, a_mid, b_low, b_mid, rows1, cols)
    keep, send, other = final_call(plan, *halves, *swapped, rows0, rows1, cols)
    other = swap(other)
    keep = jnp.maximum(keep, other[:8])
    send = jnp.maximum(send, other[8:])
    keep = jnp.maximum(keep, exchange(send, 2))
    keep = jnp.maximum(keep[:4], exchange(keep[4:], 1))
    keep = jnp.maximum(keep[:2], exchange(keep[2:], 0))
    second = (here & CORE) != 0
    ours = jnp.where(second, keep[1], keep[0])
    other = swap(jnp.where(second, keep[0], keep[1]))
    return jnp.maximum(own.reshape(SHARD), jnp.maximum(ours, other))


def solution(mesh):
    placed = (P(("row", "col"), None), P())
    return jax.shard_map(
        body, mesh=mesh, in_specs=placed, out_specs=P(("row", "col")), check_vma=False
    )
```

```python
import jax
import jax.numpy as jnp
from jax import lax
from jax.experimental import pallas as pl
from jax.experimental.pallas import tpu as pltpu
from jax.sharding import PartitionSpec as P

BLK = 256
SHARD = 512
D = 384
VMEM_LIMIT = 20 * 1024 * 1024

CORE = 16
X1, X3, Y1, Y3, Z1, Z3 = 32, 96, 4, 12, 1, 3
GENERATORS = ((X1, Y1, Y3), (X3, Z1, Z3))
SLOTS = ((), (0,), (1,), (2,), (0, 1), (1, 2), (2, 0), (0, 1, 2))
SENDS = ((0, 0), (0, 1), (0, 2), (1, 1), (2, 2), (3, 0))
HALVES = ((5, 0), (6, 1))


def mask_of(core, slot):
    mask = 0
    for generator in SLOTS[slot]:
        mask ^= GENERATORS[core][generator]
    return mask


EARLY = [(g, 0) for g in (1, 2, 3)]
SECOND = [(g, h) for g in (1, 2, 3) for h in range(1, g + 1)]
MIDDLE = [(g, h) for g in (4, 5, 6) for h in range(4)]
LATE = [(g, h) for g in (4, 5, 6) for h in (4, 5, 6)]
LAST = [(7, h) for h in range(4)]
LAST2 = [(7, h) for h in (4, 5, 6)]
FINAL = [(7, 7)]
PHASES = (
    (EARLY, 1, 0),
    (SECOND, 1, 1),
    (MIDDLE, 4, 0),
    (LATE, 4, 4),
    (LAST, 7, 0),
    (LAST2, 7, 4),
    (FINAL, 7, 7),
)


def shared(g, h):
    return g == h or 4 <= min(g, h) <= max(g, h) <= 6


COUNTS = [sum(2 if shared(g, h) else 4 for g, h in phase[0]) for phase in PHASES]
STARTS = [sum(COUNTS[:n]) + n for n in range(len(PHASES))]
LISTS = sum(COUNTS) + len(PHASES)
MARGIN = 24
MOST = 160
VMEM = pltpu.VMEM
SMEM = pltpu.SMEM


def spec(space):
    return pl.BlockSpec(memory_space=space)


def params():
    return pltpu.CompilerParams(vmem_limit_bytes=VMEM_LIMIT)


def unit_of(x):
    values = x.astype(jnp.float32)
    squares = jnp.sum(values * values, axis=1, keepdims=True)
    return (values * lax.rsqrt(squares + 1e-06)).astype(jnp.bfloat16)


def first_kernel(x_ref, out_ref):
    out_ref[...] = unit_of(x_ref[...])


def pair_kernel(here_ref, own_ref, other_ref, out_ref):
    core = (here_ref[0] >> 4) & 1
    out_ref[core] = own_ref[...]
    out_ref[1 - core] = unit_of(other_ref[...])


def unit_call(here, x, other):
    cost = pl.CostEstimate(flops=1000000, bytes_accessed=1600000, transcendentals=512)
    own = pl.pallas_call(
        first_kernel,
        out_shape=jax.ShapeDtypeStruct((SHARD, D), jnp.bfloat16),
        in_specs=[spec(VMEM)],
        out_specs=spec(VMEM),
        compiler_params=params(),
        cost_estimate=cost,
    )(x)
    return pl.pallas_call(
        pair_kernel,
        out_shape=jax.ShapeDtypeStruct((2, SHARD, D), jnp.bfloat16),
        in_specs=[spec(SMEM), spec(VMEM), spec(VMEM)],
        out_specs=spec(VMEM),
        compiler_params=params(),
        cost_estimate=cost,
    )(here, own, other)


def dot(a, b):
    return lax.dot_general(a, b, (((1,), (1,)), ((), ())), preferred_element_type=jnp.float32)


def plan_kernel(here_ref, cluster_ref, blocks_ref, full_ref, part_ref, count_ref, mine, theirs, share):
    here = here_ref[0]
    core = (here >> 4) & 1
    masks = [[mask_of(c, slot) for slot in range(8)] for c in range(2)]
    for slot in range(8):
        for ref, one, two in ((mine, 0, 1), (theirs, 1, 0)):
            chip = (here ^ jnp.where(core == 0, masks[one][slot], masks[two][slot])) & ~CORE
            for half in range(2):
                block = 2 * (chip | (half * CORE))
                ref[2 * slot + half] = cluster_ref[block] | (cluster_ref[block + 1] << 4)

    first = jnp.sum(jnp.where(blocks_ref[...] < cluster_ref[128], 1, 0))

    def held(slab):
        low, high = slab * 64, slab * 64 + 64
        return jnp.maximum(jnp.minimum(high, first + MOST) - jnp.maximum(low, first), 0)

    slab = here >> 5
    ours = held(slab)
    share[0] = 0
    for other in range(1, 4):
        there = held(slab ^ other)
        share[other] = jnp.where(
            ours + MARGIN <= there, 1, jnp.where(there + MARGIN <= ours, 2, 0)
        )

    for phase, (pairs, base_a, base_b) in enumerate(PHASES):
        full = jnp.int32(STARTS[phase])
        part = jnp.int32(STARTS[phase])

        def candidate(full, part, wanted, g, side, h, far):
            a, b = mine[2 * g + side], theirs[2 * h + far]
            same = a ^ b
            left, right = (a >> 4) ^ b, a ^ (b >> 4)
            quads = (
                jnp.where((same & 15) == 0, 1, 0)
                | jnp.where((right & 15) == 0, 2, 0)
                | jnp.where((left & 15) == 0, 4, 0)
                | jnp.where((same & 240) == 0, 8, 0)
            )
            code = (2 * (g - base_a) + side) | ((2 * (h - base_b) + far) << 4)
            full_ref[full] = code
            part_ref[part] = code | (quads << 8)
            whole = quads == 15
            full = full + jnp.where(wanted & whole, 1, 0)
            part = part + jnp.where(wanted & (quads != 0) & jnp.logical_not(whole), 1, 0)
            return full, part

        for g, h in pairs:
            w = jnp.where(
                core == 0, masks[0][g] ^ masks[1][h], masks[1][g] ^ masks[0][h]
            )
            kind = share[(w >> 5) & 3]
            bit = jnp.where((here & (w & -w)) != 0, 1, 0) ^ ((g + h) % 2)
            whole, half = kind == 1, kind == 0
            mixed = ((whole | half, core, 1 - core), (whole, 1 - core, core))
            plain = ((whole | (half & (bit == 0)), 0, 0), (whole | (half & (bit == 1)), 1, 1))
            if shared(g, h):
                for (one, side, far), (two, _, _), n in zip(mixed, plain, (0, 1)):
                    wanted = ((core == 0) & one) | ((core == 1) & two)
                    side = jnp.where(core == 0, side, n)
                    far = jnp.where(core == 0, far, n)
                    full, part = candidate(full, part, wanted, g, side, h, far)
            else:
                for wanted, side, far in mixed + plain:
                    full, part = candidate(full, part, wanted, g, side, h, far)
        count_ref[2 * phase] = full - STARTS[phase]
        count_ref[2 * phase + 1] = part - STARTS[phase]


def own_kernel(here_ref, cluster_ref, unit_ref, own_ref):
    here = here_ref[0]
    core = (here >> 4) & 1
    first0 = cluster_ref[2 * here]
    first1 = cluster_ref[2 * here + 1]
    there = here ^ CORE
    second0 = cluster_ref[2 * there]
    second1 = cluster_ref[2 * there + 1]
    mine = unit_ref[core]
    best = jnp.full((8, SHARD), -2.0, jnp.float32)
    col = lax.broadcasted_iota(jnp.int32, (BLK, SHARD), 1)
    row = lax.broadcasted_iota(jnp.int32, (BLK, SHARD), 0)
    label = jnp.where(col[:1] < BLK, first0, first1)
    for half, name in ((0, first0), (1, first1)):
        scores = dot(unit_ref[core, half * BLK : half * BLK + BLK, :], mine)
        keep = (row + half * BLK != col) & (label == name)
        scores = jnp.where(keep, scores, jnp.float32(-2.0))
        best = jnp.maximum(best, jnp.max(scores.reshape(BLK // 8, 8, SHARD), axis=0))
    for half, name in ((0, second0), (1, second1)):
        scores = dot(unit_ref[1 - core, half * BLK : half * BLK + BLK, :], mine)
        scores = jnp.where(label == name, scores, jnp.float32(-2.0))
        best = jnp.maximum(best, jnp.max(scores.reshape(BLK // 8, 8, SHARD), axis=0))
    own_ref[...] = jnp.max(best, axis=0, keepdims=True)


def plan_call(here, cluster):
    lists = jax.ShapeDtypeStruct((LISTS,), jnp.int32)
    return pl.pallas_call(
        plan_kernel,
        out_shape=(lists, lists, jax.ShapeDtypeStruct((2 * len(PHASES),), jnp.int32)),
        in_specs=[spec(SMEM), spec(SMEM), spec(VMEM)],
        out_specs=(spec(SMEM),) * 3,
        scratch_shapes=[SMEM((16,), jnp.int32), SMEM((16,), jnp.int32), SMEM((4,), jnp.int32)],
        compiler_params=params(),
        cost_estimate=pl.CostEstimate(flops=3000000000, bytes_accessed=10000, transcendentals=0),
    )(here, cluster, cluster.reshape(2, 128))


def own_call(here, cluster, unit):
    return pl.pallas_call(
        own_kernel,
        out_shape=jax.ShapeDtypeStruct((1, SHARD), jnp.float32),
        in_specs=[spec(SMEM), spec(SMEM), spec(VMEM)],
        out_specs=spec(VMEM),
        compiler_params=params(),
        cost_estimate=pl.CostEstimate(flops=1000000000, bytes_accessed=1000000, transcendentals=0),
    )(here, cluster, unit)


def fold(row_ref, col_ref, i, j, rows, cols, scores):
    best = scores[:, :128]
    for k in range(1, scores.shape[1] // 128):
        best = jnp.maximum(best, scores[:, 128 * k : 128 * k + 128])
    row_ref[i, rows, :] = jnp.maximum(row_ref[i, rows, :], best)
    down = jnp.max(scores.reshape(scores.shape[0] // 8, 8, scores.shape[1]), axis=0)
    col_ref[j, :, cols] = jnp.maximum(col_ref[j, :, cols], down)


def score_full(a_ref, b_ref, row_ref, col_ref, word):
    i = word & 15
    j = (word >> 4) & 15
    scores = dot(a_ref[i], b_ref[j])
    fold(row_ref, col_ref, i, j, slice(None), slice(None), scores)


def score_part(a_ref, b_ref, row_ref, col_ref, word):
    i = word & 15
    j = (word >> 4) & 15
    for quad in range(4):

        @pl.when(((word >> (8 + quad)) & 1) == 1)
        def _():
            rows = pl.ds((quad // 2) * BLK, BLK)
            cols = pl.ds((quad % 2) * BLK, BLK)
            scores = dot(a_ref[i, rows, :], b_ref[j, cols, :])
            fold(row_ref, col_ref, i, j, rows, cols, scores)


def score_lists(phase, full_ref, part_ref, count_ref, *refs):
    first = STARTS[phase]
    full = count_ref[2 * phase]
    fours = full & ~3

    def items(n, count):
        for k in range(count):
            score_full(*refs, full_ref[first + n + k])

    @pl.loop(0, fours, step=4)
    def _(n):
        items(n, 4)

    @pl.when((full & 2) != 0)
    def _():
        items(fours, 2)

    @pl.when((full & 1) != 0)
    def _():
        items(full - 1, 1)

    @pl.loop(0, count_ref[2 * phase + 1])
    def _(n):
        score_part(*refs, part_ref[first + n])


def put_rows(out_ref, place, first, *row_refs):
    for half in range(2):
        at = place + half
        for k in range(SHARD // 128):
            lines = slice(128 * k, 128 * k + 128)
            part = row_refs[0][first + half, lines, :]
            for ref in row_refs[1:]:
                part = jnp.maximum(part, ref[first + half, lines, :])
            out_ref[at : at + 1, lines] = jnp.max(part.T, axis=0, keepdims=True)


def clear(*refs):
    for ref in refs:
        ref[...] = jnp.full(ref.shape, -2.0, jnp.float32)


def put(buf, refs):
    for n, ref in enumerate(refs):
        buf[2 * n : 2 * n + 2] = ref[...]


def pack_kernel(a_ref, b_ref, c_ref, out_ref):
    put(out_ref, (a_ref, b_ref, c_ref))


def early_kernel(*refs):
    plan, (a_low, unit, row_ref, col_ref) = refs[:3], refs[3:]
    clear(row_ref, col_ref)
    score_lists(0, *plan, a_low, unit, row_ref, col_ref)


def second_kernel(*refs):
    plan, (a_low, unit, b_in, row_in, col_in), outs = refs[:3], refs[3:8], refs[8:]
    rows_out, col_ref, b_low, row_ref, col_low = outs
    b_low[:2] = unit[...]
    b_low[2:] = b_in[...]
    row_ref[...] = row_in[...]
    clear(col_low)
    score_lists(1, *plan, a_low, b_in, row_ref, col_low)
    col_ref[:2] = col_in[...]
    col_ref[2:] = col_low[...]
    for n in range(0, 6, 2):
        put_rows(rows_out, n, n, row_ref)


def middle_kernel(*refs):
    plan, (a_mid, b_low, col_in, row_ref, col_ref) = refs[:3], refs[3:]
    clear(row_ref)
    col_ref[...] = col_in[...]
    score_lists(2, *plan, a_mid, b_low, row_ref, col_ref)


def f32(*shape):
    return jax.ShapeDtypeStruct(shape, jnp.float32)


def shards(n):
    return jax.ShapeDtypeStruct((n, SHARD, D), jnp.bfloat16)


def rows_of(n):
    return f32(n, SHARD, 128)


def cols_of(n):
    return f32(n, 8, SHARD)


def kernel_call(kernel, operands, outs, scratch, flops, smem=3):
    return pl.pallas_call(
        kernel,
        out_shape=outs,
        in_specs=[spec(SMEM)] * smem + [spec(VMEM)] * (len(operands) - smem),
        out_specs=jax.tree.map(lambda _: spec(VMEM), outs),
        scratch_shapes=[VMEM(x.shape, x.dtype) for x in scratch],
        compiler_params=params(),
        cost_estimate=pl.CostEstimate(flops=flops, bytes_accessed=8000000, transcendentals=0),
    )(*operands)


def early_call(plan, *operands):
    outs = (rows_of(6), cols_of(2))
    return kernel_call(early_kernel, [*plan, *operands], outs, [], 30000000000)


def second_call(plan, *operands):
    outs = (f32(6, SHARD), cols_of(8), shards(8))
    scratch = [rows_of(6), cols_of(6)]
    return kernel_call(second_kernel, [*plan, *operands], outs, scratch, 3000000000)


def middle_call(plan, *operands):
    outs = (rows_of(6), cols_of(8))
    return kernel_call(middle_kernel, [*plan, *operands], outs, [], 30000000000)


KEPT = (0, 1, 2, 4)
SENT = (3, 6, 5, 7)


def last_kernel(*refs):
    plan, mine, refs = refs[:3], refs[3:5], refs[5:]
    a_mid, b_low, b_mid, col_in, row_mid, row_last, col_low, col_mid, a_last = refs
    clear(row_mid, row_last, col_mid)
    for half in range(2):
        a_last[half] = mine[half][...]
    col_low[...] = col_in[...]
    score_lists(3, *plan, a_mid, b_mid, row_mid, col_mid)
    score_lists(4, *plan, a_last, b_low, row_last, col_low)
    score_lists(5, *plan, a_last, b_mid, row_last, col_mid)


def last_call(plan, *operands):
    outs = (rows_of(6), rows_of(2), cols_of(8), cols_of(6))
    return kernel_call(last_kernel, [*plan, *operands], outs, [shards(2)], 5000000000)


def final_kernel(*refs):
    plan, mine, theirs, refs = refs[:3], refs[3:5], refs[5:7], refs[7:]
    rows0, row_one, row_two, row_in, low_in, mid_in, refs = *refs[:6], refs[6:]
    keep_ref, send_ref, other_ref, a_buf, b_buf, row_ref, col_ref = refs
    for half in range(2):
        a_buf[half] = mine[half][...]
        b_buf[half] = theirs[half][...]
    row_ref[...] = row_in[...]
    clear(col_ref)
    score_lists(6, *plan, a_buf, b_buf, row_ref, col_ref)
    keep_ref[0:2] = jnp.full((2, SHARD), -2.0, jnp.float32)
    for out_ref, slots in ((keep_ref, KEPT), (send_ref, SENT)):
        for place, slot in enumerate(slots):
            if slot == 7:
                put_rows(out_ref, 2 * place, 0, row_ref)
            elif slot > 3:
                put_rows(out_ref, 2 * place, 2 * slot - 8, row_one, row_two)
            elif slot > 0:
                out_ref[2 * place : 2 * place + 2] = rows0[2 * slot - 2 : 2 * slot]
    for place, slot in enumerate(KEPT + SENT):
        for half in range(2):
            at = 2 * place + half
            if slot == 7:
                down = col_ref[half]
            elif slot > 3:
                down = mid_in[2 * slot - 8 + half]
            else:
                down = low_in[2 * slot + half]
            other_ref[at : at + 1, :] = jnp.max(down, axis=0, keepdims=True)


def final_call(plan, *operands):
    outs = (f32(8, SHARD), f32(8, SHARD), f32(16, SHARD))
    scratch = [shards(2), shards(2), rows_of(2), cols_of(2)]
    return kernel_call(final_kernel, [*plan, *operands], outs, scratch, 500000000)


def swap(x):
    return lax.ppermute(x, ("row", "col"), [(s, s ^ CORE) for s in range(128)])


def exchange(x, generator):
    pairs = [(s, s ^ GENERATORS[(s >> 4) & 1][generator]) for s in range(128)]
    return lax.ppermute(x, ("row", "col"), pairs)


def after(x, *done):
    return lax.optimization_barrier((x, *done))[0]


def body(embeddings, block_cluster):
    here = (lax.axis_index("row") * 16 + lax.axis_index("col")).astype(jnp.int32).reshape(1)
    unit = unit_call(here, embeddings, swap(embeddings))
    plan = plan_call(here, block_cluster)
    mine = [unit]

    def step(slots):
        return [exchange(mine[SENDS[k - 1][0]], SENDS[k - 1][1]) for k in slots]

    own = own_call(here, block_cluster, unit)
    mine.extend(after(x, plan[2], own) for x in step((1, 2, 3)))
    a_low = kernel_call(pack_kernel, mine[1:4], shards(6), [], 1000000000, 0)
    b_low = swap(a_low)
    rows0, cols = early_call(plan, a_low, unit)
    rows0, cols, b_low = second_call(plan, a_low, unit, b_low, rows0, cols)
    mine.extend(after(x, cols) for x in step((4, 5, 6)))
    halves = [
        exchange(mine[source][half], generator) for half, (source, generator) in enumerate(HALVES)
    ]
    a_mid = kernel_call(pack_kernel, mine[4:7], shards(6), [], 1000000000, 0)
    b_mid = swap(a_mid)
    rows1, cols = middle_call(plan, a_mid, b_low, cols)
    halves = [after(x, cols) for x in halves]
    swapped = [swap(x) for x in halves]
    rows2, rows3, cols, cols2 = last_call(plan, *halves, a_mid, b_low, b_mid, cols)
    keep, send, other = final_call(
        plan, *halves, *swapped, rows0, rows1, rows2, rows3, cols, cols2
    )
    other = swap(other)
    keep = jnp.maximum(keep, other[:8])
    send = jnp.maximum(send, other[8:])
    keep = jnp.maximum(keep, exchange(send, 2))
    keep = jnp.maximum(keep[:4], exchange(keep[4:], 1))
    keep = jnp.maximum(keep[:2], exchange(keep[2:], 0))
    second = (here & CORE) != 0
    ours = jnp.where(second, keep[1], keep[0])
    other = swap(jnp.where(second, keep[0], keep[1]))
    return jnp.maximum(own.reshape(SHARD), jnp.maximum(ours, other))


def solution(mesh):
    placed = (P(("row", "col"), None), P())
    return jax.shard_map(
        body, mesh=mesh, in_specs=placed, out_specs=P(("row", "col")), check_vma=False
    )
```

```python
import jax
import jax.numpy as jnp
from jax import lax
from jax.experimental import pallas as pl
from jax.experimental.pallas import tpu as pltpu
from jax.sharding import PartitionSpec as P

BLK = 256
SHARD = 512
D = 384
VMEM_LIMIT = 20 * 1024 * 1024

CORE = 16
X1, X3, Y1, Y3, Z1, Z3 = 32, 96, 4, 12, 1, 3
GENERATORS = ((X1, Y1, Y3), (X3, Z1, Z3))
SLOTS = ((), (0,), (1,), (2,), (0, 1), (1, 2), (2, 0), (0, 1, 2))
SENDS = ((0, 0), (0, 1), (0, 2), (1, 1), (2, 2), (3, 0))
HALVES = ((5, 0), (6, 1))


def mask_of(core, slot):
    mask = 0
    for generator in SLOTS[slot]:
        mask ^= GENERATORS[core][generator]
    return mask


EARLY = [(g, 0) for g in (1, 2, 3)]
SECOND = [(g, h) for g in (1, 2, 3) for h in range(1, g + 1)]
MIDDLE = [(g, h) for g in (4, 5, 6) for h in range(4)]
LATE = [(g, h) for g in (4, 5, 6) for h in (4, 5, 6)]
LAST = [(7, h) for h in range(4)]
LAST2 = [(7, h) for h in (4, 5, 6)]
FINAL = [(7, 7)]
PHASES = (
    (EARLY, 1, 0),
    (SECOND, 1, 1),
    (MIDDLE, 4, 0),
    (LATE, 4, 4),
    (LAST, 7, 0),
    (LAST2, 7, 4),
    (FINAL, 7, 7),
)


def shared(g, h):
    return g == h or 4 <= min(g, h) <= max(g, h) <= 6


COUNTS = [sum(2 if shared(g, h) else 4 for g, h in phase[0]) for phase in PHASES]
STARTS = [sum(COUNTS[:n]) + n for n in range(len(PHASES))]
LISTS = sum(COUNTS) + len(PHASES)
MARGIN = 24
MOST = 160
VMEM = pltpu.VMEM
SMEM = pltpu.SMEM


def spec(space):
    return pl.BlockSpec(memory_space=space)


def params():
    return pltpu.CompilerParams(vmem_limit_bytes=VMEM_LIMIT)


def unit_of(x):
    values = x.astype(jnp.float32)
    squares = jnp.sum(values * values, axis=1, keepdims=True)
    return (values * lax.rsqrt(squares + 1e-06)).astype(jnp.bfloat16)


def first_kernel(x_ref, out_ref):
    out_ref[...] = unit_of(x_ref[...])


def pair_kernel(here_ref, own_ref, other_ref, out_ref):
    core = (here_ref[0] >> 4) & 1
    out_ref[core] = own_ref[...]
    out_ref[1 - core] = unit_of(other_ref[...])


def unit_call(here, x, other):
    cost = pl.CostEstimate(flops=1000000, bytes_accessed=1600000, transcendentals=512)
    own = pl.pallas_call(
        first_kernel,
        out_shape=jax.ShapeDtypeStruct((SHARD, D), jnp.bfloat16),
        in_specs=[spec(VMEM)],
        out_specs=spec(VMEM),
        compiler_params=params(),
        cost_estimate=cost,
    )(x)
    return pl.pallas_call(
        pair_kernel,
        out_shape=jax.ShapeDtypeStruct((2, SHARD, D), jnp.bfloat16),
        in_specs=[spec(SMEM), spec(VMEM), spec(VMEM)],
        out_specs=spec(VMEM),
        compiler_params=params(),
        cost_estimate=cost,
    )(here, own, other)


def dot(a, b):
    return lax.dot_general(a, b, (((1,), (1,)), ((), ())), preferred_element_type=jnp.float32)


def plan_kernel(here_ref, cluster_ref, blocks_ref, full_ref, part_ref, count_ref, mine, theirs, share):
    here = here_ref[0]
    core = (here >> 4) & 1
    masks = [[mask_of(c, slot) for slot in range(8)] for c in range(2)]
    for slot in range(8):
        for ref, one, two in ((mine, 0, 1), (theirs, 1, 0)):
            chip = (here ^ jnp.where(core == 0, masks[one][slot], masks[two][slot])) & ~CORE
            for half in range(2):
                block = 2 * (chip | (half * CORE))
                ref[2 * slot + half] = cluster_ref[block] | (cluster_ref[block + 1] << 4)

    first = jnp.sum(jnp.where(blocks_ref[...] < cluster_ref[128], 1, 0))

    def held(slab):
        low, high = slab * 64, slab * 64 + 64
        return jnp.maximum(jnp.minimum(high, first + MOST) - jnp.maximum(low, first), 0)

    slab = here >> 5
    ours = held(slab)
    share[0] = 0
    for other in range(1, 4):
        there = held(slab ^ other)
        share[other] = jnp.where(
            ours + MARGIN <= there, 1, jnp.where(there + MARGIN <= ours, 2, 0)
        )

    for phase, (pairs, base_a, base_b) in enumerate(PHASES):
        full = jnp.int32(STARTS[phase])
        part = jnp.int32(STARTS[phase])

        def candidate(full, part, wanted, g, side, h, far):
            a, b = mine[2 * g + side], theirs[2 * h + far]
            same = a ^ b
            left, right = (a >> 4) ^ b, a ^ (b >> 4)
            quads = (
                jnp.where((same & 15) == 0, 1, 0)
                | jnp.where((right & 15) == 0, 2, 0)
                | jnp.where((left & 15) == 0, 4, 0)
                | jnp.where((same & 240) == 0, 8, 0)
            )
            code = (2 * (g - base_a) + side) | ((2 * (h - base_b) + far) << 4)
            full_ref[full] = code
            part_ref[part] = code | (quads << 8)
            whole = quads == 15
            full = full + jnp.where(wanted & whole, 1, 0)
            part = part + jnp.where(wanted & (quads != 0) & jnp.logical_not(whole), 1, 0)
            return full, part

        for g, h in pairs:
            w = jnp.where(
                core == 0, masks[0][g] ^ masks[1][h], masks[1][g] ^ masks[0][h]
            )
            kind = share[(w >> 5) & 3]
            bit = jnp.where((here & (w & -w)) != 0, 1, 0) ^ ((g + h) % 2)
            whole, half = kind == 1, kind == 0
            mixed = ((whole | half, core, 1 - core), (whole, 1 - core, core))
            plain = ((whole | (half & (bit == 0)), 0, 0), (whole | (half & (bit == 1)), 1, 1))
            if shared(g, h):
                for (one, side, far), (two, _, _), n in zip(mixed, plain, (0, 1)):
                    wanted = ((core == 0) & one) | ((core == 1) & two)
                    side = jnp.where(core == 0, side, n)
                    far = jnp.where(core == 0, far, n)
                    full, part = candidate(full, part, wanted, g, side, h, far)
            else:
                for wanted, side, far in mixed + plain:
                    full, part = candidate(full, part, wanted, g, side, h, far)
        count_ref[2 * phase] = full - STARTS[phase]
        count_ref[2 * phase + 1] = part - STARTS[phase]


def own_kernel(here_ref, cluster_ref, unit_ref, own_ref):
    here = here_ref[0]
    core = (here >> 4) & 1
    first0 = cluster_ref[2 * here]
    first1 = cluster_ref[2 * here + 1]
    there = here ^ CORE
    second0 = cluster_ref[2 * there]
    second1 = cluster_ref[2 * there + 1]
    mine = unit_ref[core]
    best = jnp.full((8, SHARD), -2.0, jnp.float32)
    col = lax.broadcasted_iota(jnp.int32, (BLK, SHARD), 1)
    row = lax.broadcasted_iota(jnp.int32, (BLK, SHARD), 0)
    label = jnp.where(col[:1] < BLK, first0, first1)
    for half, name in ((0, first0), (1, first1)):
        scores = dot(unit_ref[core, half * BLK : half * BLK + BLK, :], mine)
        keep = (row + half * BLK != col) & (label == name)
        scores = jnp.where(keep, scores, jnp.float32(-2.0))
        best = jnp.maximum(best, jnp.max(scores.reshape(BLK // 8, 8, SHARD), axis=0))
    for half, name in ((0, second0), (1, second1)):
        scores = dot(unit_ref[1 - core, half * BLK : half * BLK + BLK, :], mine)
        scores = jnp.where(label == name, scores, jnp.float32(-2.0))
        best = jnp.maximum(best, jnp.max(scores.reshape(BLK // 8, 8, SHARD), axis=0))
    own_ref[...] = jnp.max(best, axis=0, keepdims=True)


def plan_call(here, cluster):
    lists = jax.ShapeDtypeStruct((LISTS,), jnp.int32)
    return pl.pallas_call(
        plan_kernel,
        out_shape=(lists, lists, jax.ShapeDtypeStruct((2 * len(PHASES),), jnp.int32)),
        in_specs=[spec(SMEM), spec(SMEM), spec(VMEM)],
        out_specs=(spec(SMEM),) * 3,
        scratch_shapes=[SMEM((16,), jnp.int32), SMEM((16,), jnp.int32), SMEM((4,), jnp.int32)],
        compiler_params=params(),
        cost_estimate=pl.CostEstimate(flops=3000000000, bytes_accessed=10000, transcendentals=0),
    )(here, cluster, cluster.reshape(2, 128))


def own_call(here, cluster, unit):
    return pl.pallas_call(
        own_kernel,
        out_shape=jax.ShapeDtypeStruct((1, SHARD), jnp.float32),
        in_specs=[spec(SMEM), spec(SMEM), spec(VMEM)],
        out_specs=spec(VMEM),
        compiler_params=params(),
        cost_estimate=pl.CostEstimate(flops=1000000000, bytes_accessed=1000000, transcendentals=0),
    )(here, cluster, unit)


def fold(row_ref, col_ref, i, j, rows, cols, scores):
    best = scores[:, :128]
    for k in range(1, scores.shape[1] // 128):
        best = jnp.maximum(best, scores[:, 128 * k : 128 * k + 128])
    row_ref[i, rows, :] = jnp.maximum(row_ref[i, rows, :], best)
    down = jnp.max(scores.reshape(scores.shape[0] // 8, 8, scores.shape[1]), axis=0)
    col_ref[j, :, cols] = jnp.maximum(col_ref[j, :, cols], down)


def score_full(a_ref, b_ref, row_ref, col_ref, word):
    i = word & 15
    j = (word >> 4) & 15
    scores = dot(a_ref[i], b_ref[j])
    fold(row_ref, col_ref, i, j, slice(None), slice(None), scores)


def score_part(a_ref, b_ref, row_ref, col_ref, word):
    i = word & 15
    j = (word >> 4) & 15
    for quad in range(4):

        @pl.when(((word >> (8 + quad)) & 1) == 1)
        def _():
            rows = pl.ds((quad // 2) * BLK, BLK)
            cols = pl.ds((quad % 2) * BLK, BLK)
            scores = dot(a_ref[i, rows, :], b_ref[j, cols, :])
            fold(row_ref, col_ref, i, j, rows, cols, scores)


def score_lists(phase, full_ref, part_ref, count_ref, *refs):
    first = STARTS[phase]
    full = count_ref[2 * phase]
    fours = full & ~3

    def items(n, count):
        for k in range(count):
            score_full(*refs, full_ref[first + n + k])

    @pl.loop(0, fours, step=4)
    def _(n):
        items(n, 4)

    @pl.when((full & 2) != 0)
    def _():
        items(fours, 2)

    @pl.when((full & 1) != 0)
    def _():
        items(full - 1, 1)

    @pl.loop(0, count_ref[2 * phase + 1])
    def _(n):
        score_part(*refs, part_ref[first + n])


def put_rows(out_ref, place, first, *row_refs):
    for half in range(2):
        at = place + half
        for k in range(SHARD // 128):
            lines = slice(128 * k, 128 * k + 128)
            part = row_refs[0][first + half, lines, :]
            for ref in row_refs[1:]:
                part = jnp.maximum(part, ref[first + half, lines, :])
            out_ref[at : at + 1, lines] = jnp.max(part.T, axis=0, keepdims=True)


def clear(*refs):
    for ref in refs:
        ref[...] = jnp.full(ref.shape, -2.0, jnp.float32)


def put(buf, refs):
    for n, ref in enumerate(refs):
        buf[2 * n : 2 * n + 2] = ref[...]


def pack_kernel(a_ref, b_ref, c_ref, out_ref):
    put(out_ref, (a_ref, b_ref, c_ref))


def early_kernel(*refs):
    plan, (a_low, unit, row_ref, col_ref) = refs[:3], refs[3:]
    clear(row_ref, col_ref)
    score_lists(0, *plan, a_low, unit, row_ref, col_ref)


def second_kernel(*refs):
    plan, (a_low, unit, b_in, row_in, col_in), outs = refs[:3], refs[3:8], refs[8:]
    rows_out, col_ref, b_low, row_ref, col_low = outs
    b_low[:2] = unit[...]
    b_low[2:] = b_in[...]
    row_ref[...] = row_in[...]
    clear(col_low)
    score_lists(1, *plan, a_low, b_in, row_ref, col_low)
    col_ref[:2] = col_in[...]
    col_ref[2:] = col_low[...]
    for n in range(0, 6, 2):
        put_rows(rows_out, n, n, row_ref)


def middle_kernel(*refs):
    plan, (a_mid, b_low, col_in, row_ref, col_ref) = refs[:3], refs[3:]
    clear(row_ref)
    col_ref[...] = col_in[...]
    score_lists(2, *plan, a_mid, b_low, row_ref, col_ref)


def f32(*shape):
    return jax.ShapeDtypeStruct(shape, jnp.float32)


def shards(n):
    return jax.ShapeDtypeStruct((n, SHARD, D), jnp.bfloat16)


def rows_of(n):
    return f32(n, SHARD, 128)


def cols_of(n):
    return f32(n, 8, SHARD)


def kernel_call(kernel, operands, outs, scratch, flops, smem=3):
    return pl.pallas_call(
        kernel,
        out_shape=outs,
        in_specs=[spec(SMEM)] * smem + [spec(VMEM)] * (len(operands) - smem),
        out_specs=jax.tree.map(lambda _: spec(VMEM), outs),
        scratch_shapes=[VMEM(x.shape, x.dtype) for x in scratch],
        compiler_params=params(),
        cost_estimate=pl.CostEstimate(flops=flops, bytes_accessed=8000000, transcendentals=0),
    )(*operands)


def early_call(plan, *operands):
    outs = (rows_of(6), cols_of(2))
    return kernel_call(early_kernel, [*plan, *operands], outs, [], 30000000000)


def second_call(plan, *operands):
    outs = (f32(6, SHARD), cols_of(8), shards(8))
    scratch = [rows_of(6), cols_of(6)]
    return kernel_call(second_kernel, [*plan, *operands], outs, scratch, 3000000000)


def middle_call(plan, *operands):
    outs = (rows_of(6), cols_of(8))
    return kernel_call(middle_kernel, [*plan, *operands], outs, [], 30000000000)


KEPT = (0, 1, 2, 4)
SENT = (3, 6, 5, 7)


def last_kernel(*refs):
    plan, mine, refs = refs[:3], refs[3:5], refs[5:]
    a_mid, b_low, b_mid, col_in, row_mid, row_last, col_low, col_mid, a_last = refs
    clear(row_mid, row_last, col_mid)
    for half in range(2):
        a_last[half] = mine[half][...]
    col_low[...] = col_in[...]
    score_lists(3, *plan, a_mid, b_mid, row_mid, col_mid)
    score_lists(4, *plan, a_last, b_low, row_last, col_low)
    score_lists(5, *plan, a_last, b_mid, row_last, col_mid)


def last_call(plan, *operands):
    outs = (rows_of(6), rows_of(2), cols_of(8), cols_of(6))
    return kernel_call(last_kernel, [*plan, *operands], outs, [shards(2)], 5000000000)


def final_kernel(*refs):
    plan, mine, theirs, refs = refs[:3], refs[3:5], refs[5:7], refs[7:]
    row_in, low_in, mid_in, other_ref, row_ref, a_buf, b_buf, col_ref = refs
    for half in range(2):
        a_buf[half] = mine[half][...]
        b_buf[half] = theirs[half][...]
    row_ref[...] = row_in[...]
    clear(col_ref)
    score_lists(6, *plan, a_buf, b_buf, row_ref, col_ref)
    for place, slot in enumerate(KEPT + SENT):
        for half in range(2):
            at = 2 * place + half
            if slot == 7:
                down = col_ref[half]
            elif slot > 3:
                down = mid_in[2 * slot - 8 + half]
            else:
                down = low_in[2 * slot + half]
            other_ref[at : at + 1, :] = jnp.max(down, axis=0, keepdims=True)


def final_call(plan, *operands):
    outs = (f32(16, SHARD), rows_of(2))
    scratch = [shards(2), shards(2), cols_of(2)]
    return kernel_call(final_kernel, [*plan, *operands], outs, scratch, 500000000)


def rows_kernel(rows0, row_one, row_two, row_last, keep_ref, send_ref):
    keep_ref[0:2] = jnp.full((2, SHARD), -2.0, jnp.float32)
    for out_ref, slots in ((keep_ref, KEPT), (send_ref, SENT)):
        for place, slot in enumerate(slots):
            if slot == 7:
                put_rows(out_ref, 2 * place, 0, row_last)
            elif slot > 3:
                put_rows(out_ref, 2 * place, 2 * slot - 8, row_one, row_two)
            elif slot > 0:
                out_ref[2 * place : 2 * place + 2] = rows0[2 * slot - 2 : 2 * slot]


def rows_call(*operands):
    outs = (f32(8, SHARD), f32(8, SHARD))
    return kernel_call(rows_kernel, operands, outs, [], 500000000, 0)


def swap(x):
    return lax.ppermute(x, ("row", "col"), [(s, s ^ CORE) for s in range(128)])


def exchange(x, generator):
    pairs = [(s, s ^ GENERATORS[(s >> 4) & 1][generator]) for s in range(128)]
    return lax.ppermute(x, ("row", "col"), pairs)


def after(x, *done):
    return lax.optimization_barrier((x, *done))[0]


def body(embeddings, block_cluster):
    here = (lax.axis_index("row") * 16 + lax.axis_index("col")).astype(jnp.int32).reshape(1)
    unit = unit_call(here, embeddings, swap(embeddings))
    plan = plan_call(here, block_cluster)
    mine = [unit]

    def step(slots):
        return [exchange(mine[SENDS[k - 1][0]], SENDS[k - 1][1]) for k in slots]

    own = own_call(here, block_cluster, unit)
    mine.extend(after(x, plan[2], own) for x in step((1, 2, 3)))
    a_low = kernel_call(pack_kernel, mine[1:4], shards(6), [], 1000000000, 0)
    b_low = swap(a_low)
    rows0, cols = early_call(plan, a_low, unit)
    rows0, cols, b_low = second_call(plan, a_low, unit, b_low, rows0, cols)
    mine.extend(after(x, cols) for x in step((4, 5, 6)))
    halves = [
        exchange(mine[source][half], generator) for half, (source, generator) in enumerate(HALVES)
    ]
    a_mid = kernel_call(pack_kernel, mine[4:7], shards(6), [], 1000000000, 0)
    b_mid = swap(a_mid)
    rows1, cols = middle_call(plan, a_mid, b_low, cols)
    halves = [after(x, cols) for x in halves]
    swapped = [swap(x) for x in halves]
    rows2, rows3, cols, cols2 = last_call(plan, *halves, a_mid, b_low, b_mid, cols)
    other, row7 = final_call(plan, *halves, *swapped, rows3, cols, cols2)
    keep, send = rows_call(rows0, rows1, rows2, row7)
    other = swap(other)
    keep = jnp.maximum(keep, other[:8])
    send = jnp.maximum(send, other[8:])
    keep = jnp.maximum(keep, exchange(send, 2))
    keep = jnp.maximum(keep[:4], exchange(keep[4:], 1))
    keep = jnp.maximum(keep[:2], exchange(keep[2:], 0))
    second = (here & CORE) != 0
    ours = jnp.where(second, keep[1], keep[0])
    other = swap(jnp.where(second, keep[0], keep[1]))
    return jnp.maximum(own.reshape(SHARD), jnp.maximum(ours, other))


def solution(mesh):
    placed = (P(("row", "col"), None), P())
    return jax.shard_map(
        body, mesh=mesh, in_specs=placed, out_specs=P(("row", "col")), check_vma=False
    )
```

```python
import jax
import jax.numpy as jnp
from jax import lax
from jax.experimental import pallas as pl
from jax.experimental.pallas import tpu as pltpu
from jax.sharding import PartitionSpec as P

BLK = 256
SHARD = 512
D = 384
VMEM_LIMIT = 20 * 1024 * 1024

CORE = 16
X1, X3, Y1, Y3, Z1, Z3 = 32, 96, 4, 12, 1, 3
GENERATORS = ((X1, Y1, Y3), (X3, Z1, Z3))
SLOTS = ((), (0,), (1,), (2,), (0, 1), (1, 2), (2, 0), (0, 1, 2))
SENDS = ((0, 0), (0, 1), (0, 2), (1, 1), (2, 2), (3, 0))
HALVES = ((5, 0), (6, 1))


def mask_of(core, slot):
    mask = 0
    for generator in SLOTS[slot]:
        mask ^= GENERATORS[core][generator]
    return mask


EARLY = [(g, 0) for g in (1, 2, 3)]
SECOND = [(g, h) for g in (1, 2, 3) for h in range(1, g + 1)]
MIDDLE = [(g, h) for g in (4, 5, 6) for h in range(4)]
LATE = [(g, h) for g in (4, 5, 6) for h in (4, 5, 6)]
LAST = [(7, h) for h in range(4)]
LAST2 = [(7, h) for h in (4, 5, 6)]
FINAL = [(7, 7)]
PHASES = (
    (EARLY, 1, 0),
    (SECOND, 1, 1),
    (MIDDLE, 4, 0),
    (LATE, 4, 4),
    (LAST, 7, 0),
    (LAST2, 7, 4),
    (FINAL, 7, 7),
)


def shared(g, h):
    return g == h or 4 <= min(g, h) <= max(g, h) <= 6


COUNTS = [sum(2 if shared(g, h) else 4 for g, h in phase[0]) for phase in PHASES]
STARTS = [sum(COUNTS[:n]) + n for n in range(len(PHASES))]
LISTS = sum(COUNTS) + len(PHASES)
MARGIN = 24
MOST = 160
VMEM = pltpu.VMEM
SMEM = pltpu.SMEM


def spec(space):
    return pl.BlockSpec(memory_space=space)


def params():
    return pltpu.CompilerParams(vmem_limit_bytes=VMEM_LIMIT)


def unit_of(x):
    values = x.astype(jnp.float32)
    squares = jnp.sum(values * values, axis=1, keepdims=True)
    return (values * lax.rsqrt(squares + 1e-06)).astype(jnp.bfloat16)


def first_kernel(x_ref, out_ref):
    out_ref[...] = unit_of(x_ref[...])


def pair_kernel(here_ref, own_ref, other_ref, out_ref):
    core = (here_ref[0] >> 4) & 1
    out_ref[core] = own_ref[...]
    out_ref[1 - core] = unit_of(other_ref[...])


def unit_call(here, x, other):
    cost = pl.CostEstimate(flops=1000000, bytes_accessed=1600000, transcendentals=512)
    own = pl.pallas_call(
        first_kernel,
        out_shape=jax.ShapeDtypeStruct((SHARD, D), jnp.bfloat16),
        in_specs=[spec(VMEM)],
        out_specs=spec(VMEM),
        compiler_params=params(),
        cost_estimate=cost,
    )(x)
    return pl.pallas_call(
        pair_kernel,
        out_shape=jax.ShapeDtypeStruct((2, SHARD, D), jnp.bfloat16),
        in_specs=[spec(SMEM), spec(VMEM), spec(VMEM)],
        out_specs=spec(VMEM),
        compiler_params=params(),
        cost_estimate=cost,
    )(here, own, other)


def dot(a, b):
    return lax.dot_general(a, b, (((1,), (1,)), ((), ())), preferred_element_type=jnp.float32)


def plan_kernel(here_ref, cluster_ref, blocks_ref, full_ref, part_ref, count_ref, mine, theirs, share):
    here = here_ref[0]
    core = (here >> 4) & 1
    masks = [[mask_of(c, slot) for slot in range(8)] for c in range(2)]
    for slot in range(8):
        for ref, one, two in ((mine, 0, 1), (theirs, 1, 0)):
            chip = (here ^ jnp.where(core == 0, masks[one][slot], masks[two][slot])) & ~CORE
            for half in range(2):
                block = 2 * (chip | (half * CORE))
                ref[2 * slot + half] = cluster_ref[block] | (cluster_ref[block + 1] << 4)

    first = jnp.sum(jnp.where(blocks_ref[...] < cluster_ref[128], 1, 0))

    def held(slab):
        low, high = slab * 64, slab * 64 + 64
        return jnp.maximum(jnp.minimum(high, first + MOST) - jnp.maximum(low, first), 0)

    slab = here >> 5
    ours = held(slab)
    share[0] = 0
    for other in range(1, 4):
        there = held(slab ^ other)
        share[other] = jnp.where(
            ours + MARGIN <= there, 1, jnp.where(there + MARGIN <= ours, 2, 0)
        )

    for phase, (pairs, base_a, base_b) in enumerate(PHASES):
        full = jnp.int32(STARTS[phase])
        part = jnp.int32(STARTS[phase])

        def candidate(full, part, wanted, g, side, h, far):
            a, b = mine[2 * g + side], theirs[2 * h + far]
            same = a ^ b
            left, right = (a >> 4) ^ b, a ^ (b >> 4)
            quads = (
                jnp.where((same & 15) == 0, 1, 0)
                | jnp.where((right & 15) == 0, 2, 0)
                | jnp.where((left & 15) == 0, 4, 0)
                | jnp.where((same & 240) == 0, 8, 0)
            )
            code = (2 * (g - base_a) + side) | ((2 * (h - base_b) + far) << 4)
            full_ref[full] = code
            part_ref[part] = code | (quads << 8)
            whole = quads == 15
            full = full + jnp.where(wanted & whole, 1, 0)
            part = part + jnp.where(wanted & (quads != 0) & jnp.logical_not(whole), 1, 0)
            return full, part

        for g, h in pairs:
            w = jnp.where(
                core == 0, masks[0][g] ^ masks[1][h], masks[1][g] ^ masks[0][h]
            )
            kind = share[(w >> 5) & 3]
            bit = jnp.where((here & (w & -w)) != 0, 1, 0) ^ ((g + h) % 2)
            whole, half = kind == 1, kind == 0
            mixed = ((whole | half, core, 1 - core), (whole, 1 - core, core))
            plain = ((whole | (half & (bit == 0)), 0, 0), (whole | (half & (bit == 1)), 1, 1))
            if shared(g, h):
                for (one, side, far), (two, _, _), n in zip(mixed, plain, (0, 1)):
                    wanted = ((core == 0) & one) | ((core == 1) & two)
                    side = jnp.where(core == 0, side, n)
                    far = jnp.where(core == 0, far, n)
                    full, part = candidate(full, part, wanted, g, side, h, far)
            else:
                for wanted, side, far in mixed + plain:
                    full, part = candidate(full, part, wanted, g, side, h, far)
        count_ref[2 * phase] = full - STARTS[phase]
        count_ref[2 * phase + 1] = part - STARTS[phase]


def own_kernel(here_ref, cluster_ref, unit_ref, own_ref):
    here = here_ref[0]
    core = (here >> 4) & 1
    first0 = cluster_ref[2 * here]
    first1 = cluster_ref[2 * here + 1]
    there = here ^ CORE
    second0 = cluster_ref[2 * there]
    second1 = cluster_ref[2 * there + 1]
    mine = unit_ref[core]
    best = jnp.full((8, SHARD), -2.0, jnp.float32)
    col = lax.broadcasted_iota(jnp.int32, (BLK, SHARD), 1)
    row = lax.broadcasted_iota(jnp.int32, (BLK, SHARD), 0)
    label = jnp.where(col[:1] < BLK, first0, first1)
    for half, name in ((0, first0), (1, first1)):
        scores = dot(unit_ref[core, half * BLK : half * BLK + BLK, :], mine)
        keep = (row + half * BLK != col) & (label == name)
        scores = jnp.where(keep, scores, jnp.float32(-2.0))
        best = jnp.maximum(best, jnp.max(scores.reshape(BLK // 8, 8, SHARD), axis=0))
    for half, name in ((0, second0), (1, second1)):
        scores = dot(unit_ref[1 - core, half * BLK : half * BLK + BLK, :], mine)
        scores = jnp.where(label == name, scores, jnp.float32(-2.0))
        best = jnp.maximum(best, jnp.max(scores.reshape(BLK // 8, 8, SHARD), axis=0))
    own_ref[...] = jnp.max(best, axis=0, keepdims=True)


def plan_call(here, cluster):
    lists = jax.ShapeDtypeStruct((LISTS,), jnp.int32)
    return pl.pallas_call(
        plan_kernel,
        out_shape=(lists, lists, jax.ShapeDtypeStruct((2 * len(PHASES),), jnp.int32)),
        in_specs=[spec(SMEM), spec(SMEM), spec(VMEM)],
        out_specs=(spec(SMEM),) * 3,
        scratch_shapes=[SMEM((16,), jnp.int32), SMEM((16,), jnp.int32), SMEM((4,), jnp.int32)],
        compiler_params=params(),
        cost_estimate=pl.CostEstimate(flops=3000000000, bytes_accessed=10000, transcendentals=0),
    )(here, cluster, cluster.reshape(2, 128))


def own_call(here, cluster, unit):
    return pl.pallas_call(
        own_kernel,
        out_shape=jax.ShapeDtypeStruct((1, SHARD), jnp.float32),
        in_specs=[spec(SMEM), spec(SMEM), spec(VMEM)],
        out_specs=spec(VMEM),
        compiler_params=params(),
        cost_estimate=pl.CostEstimate(flops=1000000000, bytes_accessed=1000000, transcendentals=0),
    )(here, cluster, unit)


def fold(row_ref, col_ref, i, j, rows, cols, scores):
    best = scores[:, :128]
    for k in range(1, scores.shape[1] // 128):
        best = jnp.maximum(best, scores[:, 128 * k : 128 * k + 128])
    row_ref[i, rows, :] = jnp.maximum(row_ref[i, rows, :], best)
    down = jnp.max(scores.reshape(scores.shape[0] // 8, 8, scores.shape[1]), axis=0)
    col_ref[j, :, cols] = jnp.maximum(col_ref[j, :, cols], down)


def score_full(a_ref, b_ref, row_ref, col_ref, word):
    i = word & 15
    j = (word >> 4) & 15
    scores = dot(a_ref[i], b_ref[j])
    fold(row_ref, col_ref, i, j, slice(None), slice(None), scores)


def score_part(a_ref, b_ref, row_ref, col_ref, word):
    i = word & 15
    j = (word >> 4) & 15
    for quad in range(4):

        @pl.when(((word >> (8 + quad)) & 1) == 1)
        def _():
            rows = pl.ds((quad // 2) * BLK, BLK)
            cols = pl.ds((quad % 2) * BLK, BLK)
            scores = dot(a_ref[i, rows, :], b_ref[j, cols, :])
            fold(row_ref, col_ref, i, j, rows, cols, scores)


def score_lists(phase, full_ref, part_ref, count_ref, *refs):
    first = STARTS[phase]
    full = count_ref[2 * phase]
    fours = full & ~3

    def items(n, count):
        for k in range(count):
            score_full(*refs, full_ref[first + n + k])

    @pl.loop(0, fours, step=4)
    def _(n):
        items(n, 4)

    @pl.when((full & 2) != 0)
    def _():
        items(fours, 2)

    @pl.when((full & 1) != 0)
    def _():
        items(full - 1, 1)

    @pl.loop(0, count_ref[2 * phase + 1])
    def _(n):
        score_part(*refs, part_ref[first + n])


def put_rows(out_ref, place, first, *row_refs):
    for half in range(2):
        at = place + half
        for k in range(SHARD // 128):
            lines = slice(128 * k, 128 * k + 128)
            part = row_refs[0][first + half, lines, :]
            for ref in row_refs[1:]:
                part = jnp.maximum(part, ref[first + half, lines, :])
            out_ref[at : at + 1, lines] = jnp.max(part.T, axis=0, keepdims=True)


def clear(*refs):
    for ref in refs:
        ref[...] = jnp.full(ref.shape, -2.0, jnp.float32)


def put(buf, refs):
    for n, ref in enumerate(refs):
        buf[2 * n : 2 * n + 2] = ref[...]


def pack_kernel(a_ref, b_ref, c_ref, out_ref):
    put(out_ref, (a_ref, b_ref, c_ref))


def early_kernel(*refs):
    plan, (a_low, unit, row_ref, col_ref) = refs[:3], refs[3:]
    clear(row_ref, col_ref)
    score_lists(0, *plan, a_low, unit, row_ref, col_ref)


def second_kernel(*refs):
    plan, (a_low, unit, b_in, row_in, col_in), outs = refs[:3], refs[3:8], refs[8:]
    row_ref, col_ref, b_low, col_low = outs
    b_low[:2] = unit[...]
    b_low[2:] = b_in[...]
    row_ref[...] = row_in[...]
    clear(col_low)
    score_lists(1, *plan, a_low, b_in, row_ref, col_low)
    col_ref[:2] = col_in[...]
    col_ref[2:] = col_low[...]


def middle_kernel(*refs):
    plan, (a_mid, b_low, col_in, row_ref, col_ref) = refs[:3], refs[3:]
    clear(row_ref)
    col_ref[...] = col_in[...]
    score_lists(2, *plan, a_mid, b_low, row_ref, col_ref)


def f32(*shape):
    return jax.ShapeDtypeStruct(shape, jnp.float32)


def shards(n):
    return jax.ShapeDtypeStruct((n, SHARD, D), jnp.bfloat16)


def rows_of(n):
    return f32(n, SHARD, 128)


def cols_of(n):
    return f32(n, 8, SHARD)


def kernel_call(kernel, operands, outs, scratch, flops, smem=3):
    return pl.pallas_call(
        kernel,
        out_shape=outs,
        in_specs=[spec(SMEM)] * smem + [spec(VMEM)] * (len(operands) - smem),
        out_specs=jax.tree.map(lambda _: spec(VMEM), outs),
        scratch_shapes=[VMEM(x.shape, x.dtype) for x in scratch],
        compiler_params=params(),
        cost_estimate=pl.CostEstimate(flops=flops, bytes_accessed=8000000, transcendentals=0),
    )(*operands)


def early_call(plan, *operands):
    outs = (rows_of(6), cols_of(2))
    return kernel_call(early_kernel, [*plan, *operands], outs, [], 30000000000)


def second_call(plan, *operands):
    outs = (rows_of(6), cols_of(8), shards(8))
    scratch = [cols_of(6)]
    return kernel_call(second_kernel, [*plan, *operands], outs, scratch, 3000000000)


def middle_call(plan, *operands):
    outs = (rows_of(6), cols_of(8))
    return kernel_call(middle_kernel, [*plan, *operands], outs, [], 30000000000)


KEPT = (0, 1, 2, 4)
SENT = (3, 6, 5, 7)


def last_kernel(*refs):
    plan, mine, refs = refs[:3], refs[3:5], refs[5:]
    a_mid, b_low, b_mid, col_in, row_mid, row_last, col_low, col_mid, a_last = refs
    clear(row_mid, row_last, col_mid)
    for half in range(2):
        a_last[half] = mine[half][...]
    col_low[...] = col_in[...]
    score_lists(3, *plan, a_mid, b_mid, row_mid, col_mid)
    score_lists(4, *plan, a_last, b_low, row_last, col_low)
    score_lists(5, *plan, a_last, b_mid, row_last, col_mid)


def last_call(plan, *operands):
    outs = (rows_of(6), rows_of(2), cols_of(8), cols_of(6))
    return kernel_call(last_kernel, [*plan, *operands], outs, [shards(2)], 5000000000)


def final_kernel(*refs):
    plan, mine, theirs, refs = refs[:3], refs[3:5], refs[5:7], refs[7:]
    row_in, low_in, mid_in, other_ref, row_ref, a_buf, b_buf, col_ref = refs
    for half in range(2):
        a_buf[half] = mine[half][...]
        b_buf[half] = theirs[half][...]
    row_ref[...] = row_in[...]
    clear(col_ref)
    score_lists(6, *plan, a_buf, b_buf, row_ref, col_ref)
    for place, slot in enumerate(KEPT + SENT):
        for half in range(2):
            at = 2 * place + half
            if slot == 7:
                down = col_ref[half]
            elif slot > 3:
                down = mid_in[2 * slot - 8 + half]
            else:
                down = low_in[2 * slot + half]
            other_ref[at : at + 1, :] = jnp.max(down, axis=0, keepdims=True)


def final_call(plan, *operands):
    outs = (f32(16, SHARD), rows_of(2))
    scratch = [shards(2), shards(2), cols_of(2)]
    return kernel_call(final_kernel, [*plan, *operands], outs, scratch, 500000000)


def rows_kernel(rows0, row_one, row_two, row_last, keep_ref, send_ref):
    keep_ref[0:2] = jnp.full((2, SHARD), -2.0, jnp.float32)
    for out_ref, slots in ((keep_ref, KEPT), (send_ref, SENT)):
        for place, slot in enumerate(slots):
            if slot == 7:
                put_rows(out_ref, 2 * place, 0, row_last)
            elif slot > 3:
                put_rows(out_ref, 2 * place, 2 * slot - 8, row_one, row_two)
            elif slot > 0:
                put_rows(out_ref, 2 * place, 2 * slot - 2, rows0)


def rows_call(*operands):
    outs = (f32(8, SHARD), f32(8, SHARD))
    return kernel_call(rows_kernel, operands, outs, [], 500000000, 0)


def swap(x):
    return lax.ppermute(x, ("row", "col"), [(s, s ^ CORE) for s in range(128)])


def exchange(x, generator):
    pairs = [(s, s ^ GENERATORS[(s >> 4) & 1][generator]) for s in range(128)]
    return lax.ppermute(x, ("row", "col"), pairs)


def after(x, *done):
    return lax.optimization_barrier((x, *done))[0]


def body(embeddings, block_cluster):
    here = (lax.axis_index("row") * 16 + lax.axis_index("col")).astype(jnp.int32).reshape(1)
    unit = unit_call(here, embeddings, swap(embeddings))
    plan = plan_call(here, block_cluster)
    mine = [unit]

    def step(slots):
        return [exchange(mine[SENDS[k - 1][0]], SENDS[k - 1][1]) for k in slots]

    own = own_call(here, block_cluster, unit)
    mine.extend(after(x, plan[2], own) for x in step((1, 2, 3)))
    a_low = kernel_call(pack_kernel, mine[1:4], shards(6), [], 1000000000, 0)
    b_low = swap(a_low)
    rows0, cols = early_call(plan, a_low, unit)
    rows0, cols, b_low = second_call(plan, a_low, unit, b_low, rows0, cols)
    mine.extend(after(x, cols) for x in step((4, 5, 6)))
    halves = [
        exchange(mine[source][half], generator) for half, (source, generator) in enumerate(HALVES)
    ]
    a_mid = kernel_call(pack_kernel, mine[4:7], shards(6), [], 1000000000, 0)
    b_mid = swap(a_mid)
    rows1, cols = middle_call(plan, a_mid, b_low, cols)
    halves = [after(x, cols) for x in halves]
    swapped = [swap(x) for x in halves]
    rows2, rows3, cols, cols2 = last_call(plan, *halves, a_mid, b_low, b_mid, cols)
    other, row7 = final_call(plan, *halves, *swapped, rows3, cols, cols2)
    keep, send = rows_call(rows0, rows1, rows2, row7)
    other = swap(other)
    keep = jnp.maximum(keep, other[:8])
    send = jnp.maximum(send, other[8:])
    keep = jnp.maximum(keep, exchange(send, 2))
    keep = jnp.maximum(keep[:4], exchange(keep[4:], 1))
    keep = jnp.maximum(keep[:2], exchange(keep[2:], 0))
    second = (here & CORE) != 0
    ours = jnp.where(second, keep[1], keep[0])
    other = swap(jnp.where(second, keep[0], keep[1]))
    return jnp.maximum(own.reshape(SHARD), jnp.maximum(ours, other))


def solution(mesh):
    placed = (P(("row", "col"), None), P())
    return jax.shard_map(
        body, mesh=mesh, in_specs=placed, out_specs=P(("row", "col")), check_vma=False
    )
```

```python
import jax
import jax.numpy as jnp
from jax import lax
from jax.experimental import pallas as pl
from jax.experimental.pallas import tpu as pltpu
from jax.sharding import PartitionSpec as P

BLK = 256
SHARD = 512
D = 384
VMEM_LIMIT = 20 * 1024 * 1024

CORE = 16
X1, X3, Y1, Y3, Z1, Z3 = 32, 96, 4, 12, 1, 3
GENERATORS = ((X1, Y1, Y3), (X3, Z1, Z3))
SLOTS = ((), (0,), (1,), (2,), (0, 1), (1, 2), (2, 0), (0, 1, 2))
SENDS = ((0, 0), (0, 1), (0, 2), (1, 1), (2, 2), (3, 0))
HALVES = ((5, 0), (6, 1))


def mask_of(core, slot):
    mask = 0
    for generator in SLOTS[slot]:
        mask ^= GENERATORS[core][generator]
    return mask


EARLY = [(g, 0) for g in (1, 2, 3)]
SECOND = [(g, h) for g in (1, 2, 3) for h in range(1, g + 1)]
MIDDLE = [(g, h) for g in (4, 5, 6) for h in range(4)]
LATE = [(g, h) for g in (4, 5, 6) for h in (4, 5, 6)]
LAST = [(7, h) for h in range(4)]
LAST2 = [(7, h) for h in (4, 5, 6)]
FINAL = [(7, 7)]
PHASES = (
    (EARLY, 1, 0),
    (SECOND, 1, 1),
    (MIDDLE, 4, 0),
    (LATE, 4, 4),
    (LAST, 7, 0),
    (LAST2, 7, 4),
    (FINAL, 7, 7),
)


def shared(g, h):
    return g == h or 4 <= min(g, h) <= max(g, h) <= 6


COUNTS = [sum(2 if shared(g, h) else 4 for g, h in phase[0]) for phase in PHASES]
STARTS = [sum(COUNTS[:n]) + n for n in range(len(PHASES))]
LISTS = sum(COUNTS) + len(PHASES)
MARGIN = 24
MOST = 160
VMEM = pltpu.VMEM
SMEM = pltpu.SMEM


def spec(space):
    return pl.BlockSpec(memory_space=space)


def params():
    return pltpu.CompilerParams(vmem_limit_bytes=VMEM_LIMIT)


def unit_of(x):
    values = x.astype(jnp.float32)
    squares = jnp.sum(values * values, axis=1, keepdims=True)
    return (values * lax.rsqrt(squares + 1e-06)).astype(jnp.bfloat16)


def first_kernel(x_ref, out_ref):
    out_ref[...] = unit_of(x_ref[...])


def pair_kernel(here_ref, own_ref, other_ref, out_ref):
    core = (here_ref[0] >> 4) & 1
    out_ref[core] = own_ref[...]
    out_ref[1 - core] = unit_of(other_ref[...])


def unit_call(here, x, other):
    cost = pl.CostEstimate(flops=1000000, bytes_accessed=1600000, transcendentals=512)
    own = pl.pallas_call(
        first_kernel,
        out_shape=jax.ShapeDtypeStruct((SHARD, D), jnp.bfloat16),
        in_specs=[spec(VMEM)],
        out_specs=spec(VMEM),
        compiler_params=params(),
        cost_estimate=cost,
    )(x)
    return pl.pallas_call(
        pair_kernel,
        out_shape=jax.ShapeDtypeStruct((2, SHARD, D), jnp.bfloat16),
        in_specs=[spec(SMEM), spec(VMEM), spec(VMEM)],
        out_specs=spec(VMEM),
        compiler_params=params(),
        cost_estimate=cost,
    )(here, own, other)


def dot(a, b):
    return lax.dot_general(a, b, (((1,), (1,)), ((), ())), preferred_element_type=jnp.float32)


def plan_kernel(here_ref, cluster_ref, blocks_ref, full_ref, part_ref, count_ref, mine, theirs, share):
    here = here_ref[0]
    core = (here >> 4) & 1
    masks = [[mask_of(c, slot) for slot in range(8)] for c in range(2)]
    for slot in range(8):
        for ref, one, two in ((mine, 0, 1), (theirs, 1, 0)):
            chip = (here ^ jnp.where(core == 0, masks[one][slot], masks[two][slot])) & ~CORE
            for half in range(2):
                block = 2 * (chip | (half * CORE))
                ref[2 * slot + half] = cluster_ref[block] | (cluster_ref[block + 1] << 4)

    first = jnp.sum(jnp.where(blocks_ref[...] < cluster_ref[128], 1, 0))

    def held(slab):
        low, high = slab * 64, slab * 64 + 64
        return jnp.maximum(jnp.minimum(high, first + MOST) - jnp.maximum(low, first), 0)

    slab = here >> 5
    ours = held(slab)
    share[0] = 0
    for other in range(1, 4):
        there = held(slab ^ other)
        share[other] = jnp.where(
            ours + MARGIN <= there, 1, jnp.where(there + MARGIN <= ours, 2, 0)
        )

    for phase, (pairs, base_a, base_b) in enumerate(PHASES):
        full = jnp.int32(STARTS[phase])
        part = jnp.int32(STARTS[phase])

        def candidate(full, part, wanted, g, side, h, far):
            a, b = mine[2 * g + side], theirs[2 * h + far]
            same = a ^ b
            left, right = (a >> 4) ^ b, a ^ (b >> 4)
            quads = (
                jnp.where((same & 15) == 0, 1, 0)
                | jnp.where((right & 15) == 0, 2, 0)
                | jnp.where((left & 15) == 0, 4, 0)
                | jnp.where((same & 240) == 0, 8, 0)
            )
            code = (2 * (g - base_a) + side) | ((2 * (h - base_b) + far) << 4)
            full_ref[full] = code
            part_ref[part] = code | (quads << 8)
            whole = quads == 15
            full = full + jnp.where(wanted & whole, 1, 0)
            part = part + jnp.where(wanted & (quads != 0) & jnp.logical_not(whole), 1, 0)
            return full, part

        for g, h in pairs:
            w = jnp.where(
                core == 0, masks[0][g] ^ masks[1][h], masks[1][g] ^ masks[0][h]
            )
            kind = share[(w >> 5) & 3]
            bit = jnp.where((here & (w & -w)) != 0, 1, 0) ^ ((g + h) % 2)
            whole, half = kind == 1, kind == 0
            mixed = ((whole | half, core, 1 - core), (whole, 1 - core, core))
            plain = ((whole | (half & (bit == 0)), 0, 0), (whole | (half & (bit == 1)), 1, 1))
            if shared(g, h):
                for (one, side, far), (two, _, _), n in zip(mixed, plain, (0, 1)):
                    wanted = ((core == 0) & one) | ((core == 1) & two)
                    side = jnp.where(core == 0, side, n)
                    far = jnp.where(core == 0, far, n)
                    full, part = candidate(full, part, wanted, g, side, h, far)
            else:
                for wanted, side, far in mixed + plain:
                    full, part = candidate(full, part, wanted, g, side, h, far)
        count_ref[2 * phase] = full - STARTS[phase]
        count_ref[2 * phase + 1] = part - STARTS[phase]


def own_kernel(here_ref, cluster_ref, unit_ref, own_ref):
    here = here_ref[0]
    core = (here >> 4) & 1
    first0 = cluster_ref[2 * here]
    first1 = cluster_ref[2 * here + 1]
    there = here ^ CORE
    second0 = cluster_ref[2 * there]
    second1 = cluster_ref[2 * there + 1]
    mine = unit_ref[core]
    best = jnp.full((8, SHARD), -2.0, jnp.float32)
    col = lax.broadcasted_iota(jnp.int32, (BLK, SHARD), 1)
    row = lax.broadcasted_iota(jnp.int32, (BLK, SHARD), 0)
    label = jnp.where(col[:1] < BLK, first0, first1)
    for half, name in ((0, first0), (1, first1)):
        scores = dot(unit_ref[core, half * BLK : half * BLK + BLK, :], mine)
        keep = (row + half * BLK != col) & (label == name)
        scores = jnp.where(keep, scores, jnp.float32(-2.0))
        best = jnp.maximum(best, jnp.max(scores.reshape(BLK // 8, 8, SHARD), axis=0))
    for half, name in ((0, second0), (1, second1)):
        scores = dot(unit_ref[1 - core, half * BLK : half * BLK + BLK, :], mine)
        scores = jnp.where(label == name, scores, jnp.float32(-2.0))
        best = jnp.maximum(best, jnp.max(scores.reshape(BLK // 8, 8, SHARD), axis=0))
    own_ref[...] = jnp.max(best, axis=0, keepdims=True)


def plan_call(here, cluster):
    lists = jax.ShapeDtypeStruct((LISTS,), jnp.int32)
    return pl.pallas_call(
        plan_kernel,
        out_shape=(lists, lists, jax.ShapeDtypeStruct((2 * len(PHASES),), jnp.int32)),
        in_specs=[spec(SMEM), spec(SMEM), spec(VMEM)],
        out_specs=(spec(SMEM),) * 3,
        scratch_shapes=[SMEM((16,), jnp.int32), SMEM((16,), jnp.int32), SMEM((4,), jnp.int32)],
        compiler_params=params(),
        cost_estimate=pl.CostEstimate(flops=3000000000, bytes_accessed=10000, transcendentals=0),
    )(here, cluster, cluster.reshape(2, 128))


def own_call(here, cluster, unit):
    return pl.pallas_call(
        own_kernel,
        out_shape=jax.ShapeDtypeStruct((1, SHARD), jnp.float32),
        in_specs=[spec(SMEM), spec(SMEM), spec(VMEM)],
        out_specs=spec(VMEM),
        compiler_params=params(),
        cost_estimate=pl.CostEstimate(flops=1000000000, bytes_accessed=1000000, transcendentals=0),
    )(here, cluster, unit)


def fold(row_ref, col_ref, i, j, rows, cols, scores):
    best = scores[:, :128]
    for k in range(1, scores.shape[1] // 128):
        best = jnp.maximum(best, scores[:, 128 * k : 128 * k + 128])
    row_ref[i, rows, :] = jnp.maximum(row_ref[i, rows, :], best)
    down = jnp.max(scores.reshape(scores.shape[0] // 8, 8, scores.shape[1]), axis=0)
    col_ref[j, :, cols] = jnp.maximum(col_ref[j, :, cols], down)


def score_full(a_ref, b_ref, row_ref, col_ref, word):
    i = word & 15
    j = (word >> 4) & 15
    scores = dot(a_ref[i], b_ref[j])
    fold(row_ref, col_ref, i, j, slice(None), slice(None), scores)


def score_part(a_ref, b_ref, row_ref, col_ref, word):
    i = word & 15
    j = (word >> 4) & 15
    for quad in range(4):

        @pl.when(((word >> (8 + quad)) & 1) == 1)
        def _():
            rows = pl.ds((quad // 2) * BLK, BLK)
            cols = pl.ds((quad % 2) * BLK, BLK)
            scores = dot(a_ref[i, rows, :], b_ref[j, cols, :])
            fold(row_ref, col_ref, i, j, rows, cols, scores)


def score_lists(phase, full_ref, part_ref, count_ref, *refs):
    first = STARTS[phase]
    full = count_ref[2 * phase]
    fours = full & ~3

    def items(n, count):
        for k in range(count):
            score_full(*refs, full_ref[first + n + k])

    @pl.loop(0, fours, step=4)
    def _(n):
        items(n, 4)

    @pl.when((full & 2) != 0)
    def _():
        items(fours, 2)

    @pl.when((full & 1) != 0)
    def _():
        items(full - 1, 1)

    @pl.loop(0, count_ref[2 * phase + 1])
    def _(n):
        score_part(*refs, part_ref[first + n])


def put_rows(out_ref, place, first, *row_refs):
    for half in range(2):
        at = place + half
        for k in range(SHARD // 128):
            lines = slice(128 * k, 128 * k + 128)
            part = row_refs[0][first + half, lines, :]
            for ref in row_refs[1:]:
                part = jnp.maximum(part, ref[first + half, lines, :])
            out_ref[at : at + 1, lines] = jnp.max(part.T, axis=0, keepdims=True)


def clear(*refs):
    for ref in refs:
        ref[...] = jnp.full(ref.shape, -2.0, jnp.float32)


def put(buf, refs):
    for n, ref in enumerate(refs):
        buf[2 * n : 2 * n + 2] = ref[...]


def pack_kernel(a_ref, b_ref, c_ref, out_ref):
    put(out_ref, (a_ref, b_ref, c_ref))


def early_kernel(*refs):
    plan, (a_low, unit, row_ref, col_ref) = refs[:3], refs[3:]
    clear(row_ref, col_ref)
    score_lists(0, *plan, a_low, unit, row_ref, col_ref)


def second_kernel(*refs):
    plan, (a_low, unit, b_in, row_in, col_in), outs = refs[:3], refs[3:8], refs[8:]
    row_ref, col_ref, b_low, col_low = outs
    b_low[:2] = unit[...]
    b_low[2:] = b_in[...]
    row_ref[...] = row_in[...]
    clear(col_low)
    score_lists(1, *plan, a_low, b_in, row_ref, col_low)
    col_ref[:2] = col_in[...]
    col_ref[2:] = col_low[...]


def middle_kernel(*refs):
    plan, (a_mid, b_low, col_in, row_ref, col_ref) = refs[:3], refs[3:]
    clear(row_ref)
    col_ref[...] = col_in[...]
    score_lists(2, *plan, a_mid, b_low, row_ref, col_ref)


def f32(*shape):
    return jax.ShapeDtypeStruct(shape, jnp.float32)


def shards(n):
    return jax.ShapeDtypeStruct((n, SHARD, D), jnp.bfloat16)


def rows_of(n):
    return f32(n, SHARD, 128)


def cols_of(n):
    return f32(n, 8, SHARD)


def kernel_call(kernel, operands, outs, scratch, flops, smem=3):
    return pl.pallas_call(
        kernel,
        out_shape=outs,
        in_specs=[spec(SMEM)] * smem + [spec(VMEM)] * (len(operands) - smem),
        out_specs=jax.tree.map(lambda _: spec(VMEM), outs),
        scratch_shapes=[VMEM(x.shape, x.dtype) for x in scratch],
        compiler_params=params(),
        cost_estimate=pl.CostEstimate(flops=flops, bytes_accessed=8000000, transcendentals=0),
    )(*operands)


def early_call(plan, *operands):
    outs = (rows_of(6), cols_of(2))
    return kernel_call(early_kernel, [*plan, *operands], outs, [], 30000000000)


def second_call(plan, *operands):
    outs = (rows_of(6), cols_of(8), shards(8))
    scratch = [cols_of(6)]
    return kernel_call(second_kernel, [*plan, *operands], outs, scratch, 3000000000)


def middle_call(plan, *operands):
    outs = (rows_of(6), cols_of(8))
    return kernel_call(middle_kernel, [*plan, *operands], outs, [], 30000000000)


KEPT = (0, 1, 2, 4)
SENT = (3, 6, 5, 7)


def last_kernel(*refs):
    plan, mine, refs = refs[:3], refs[3:5], refs[5:]
    a_mid, b_low, b_mid, col_in, row_mid, row_last, col_low, col_mid, a_last = refs
    clear(row_mid, row_last, col_mid)
    for half in range(2):
        a_last[half] = mine[half][...]
    col_low[...] = col_in[...]
    score_lists(3, *plan, a_mid, b_mid, row_mid, col_mid)
    score_lists(4, *plan, a_last, b_low, row_last, col_low)
    score_lists(5, *plan, a_last, b_mid, row_last, col_mid)


def last_call(plan, *operands):
    outs = (rows_of(6), rows_of(2), cols_of(8), cols_of(6))
    return kernel_call(last_kernel, [*plan, *operands], outs, [shards(2)], 5000000000)


def final_kernel(*refs):
    plan, mine, theirs, refs = refs[:3], refs[3:5], refs[5:7], refs[7:]
    row_in, low_in, mid_in, other_ref, row_ref, a_buf, b_buf, col_ref = refs
    for half in range(2):
        a_buf[half] = mine[half][...]
        b_buf[half] = theirs[half][...]
    row_ref[...] = row_in[...]
    clear(col_ref)
    score_lists(6, *plan, a_buf, b_buf, row_ref, col_ref)
    for place, slot in enumerate(KEPT + SENT):
        for half in range(2):
            at = 2 * place + half
            if slot == 7:
                down = col_ref[half]
            elif slot > 3:
                down = mid_in[2 * slot - 8 + half]
            else:
                down = low_in[2 * slot + half]
            other_ref[at : at + 1, :] = jnp.max(down, axis=0, keepdims=True)


def final_call(plan, *operands):
    outs = (f32(16, SHARD), rows_of(2))
    scratch = [shards(2), shards(2), cols_of(2)]
    return kernel_call(final_kernel, [*plan, *operands], outs, scratch, 500000000)


def rows_kernel(rows0, row_one, row_two, row_last, keep_ref, send_ref):
    keep_ref[0:2] = jnp.full((2, SHARD), -2.0, jnp.float32)
    for out_ref, slots in ((keep_ref, KEPT), (send_ref, SENT)):
        for place, slot in enumerate(slots):
            if slot == 7:
                put_rows(out_ref, 2 * place, 0, row_last)
            elif slot > 3:
                put_rows(out_ref, 2 * place, 2 * slot - 8, row_one, row_two)
            elif slot > 0:
                put_rows(out_ref, 2 * place, 2 * slot - 2, rows0)


def rows_call(*operands):
    outs = (f32(8, SHARD), f32(8, SHARD))
    return kernel_call(rows_kernel, operands, outs, [], 500000000, 0)


def swap(x):
    return lax.ppermute(x, ("row", "col"), [(s, s ^ CORE) for s in range(128)])


def exchange(x, generator):
    pairs = [(s, s ^ GENERATORS[(s >> 4) & 1][generator]) for s in range(128)]
    return lax.ppermute(x, ("row", "col"), pairs)


def after(x, *done):
    return lax.optimization_barrier((x, *done))[0]


def body(embeddings, block_cluster):
    here = (lax.axis_index("row") * 16 + lax.axis_index("col")).astype(jnp.int32).reshape(1)
    unit = unit_call(here, embeddings, swap(embeddings))
    plan = plan_call(here, block_cluster)
    mine = [unit]

    def step(slots):
        return [exchange(mine[SENDS[k - 1][0]], SENDS[k - 1][1]) for k in slots]

    mine.extend(after(x, plan[2]) for x in step((1, 2, 3)))
    a_low = kernel_call(pack_kernel, mine[1:4], shards(6), [], 1000000000, 0)
    b_low = swap(a_low)
    rows0, cols = early_call(plan, a_low, unit)
    rows0, cols, b_low = second_call(plan, a_low, unit, b_low, rows0, cols)
    mine.extend(after(x, cols) for x in step((4, 5, 6)))
    halves = [
        exchange(mine[source][half], generator) for half, (source, generator) in enumerate(HALVES)
    ]
    a_mid = kernel_call(pack_kernel, mine[4:7], shards(6), [], 1000000000, 0)
    b_mid = swap(a_mid)
    rows1, cols = middle_call(plan, a_mid, b_low, cols)
    halves = [after(x, cols) for x in halves]
    swapped = [swap(x) for x in halves]
    rows2, rows3, cols, cols2 = last_call(plan, *halves, a_mid, b_low, b_mid, cols)
    other, row7 = final_call(plan, *halves, *swapped, rows3, cols, cols2)
    keep, send = rows_call(rows0, rows1, rows2, row7)
    own = own_call(here, block_cluster, after(unit, send))
    other = swap(other)
    keep = jnp.maximum(keep, other[:8])
    send = jnp.maximum(send, other[8:])
    keep = jnp.maximum(keep, exchange(send, 2))
    keep = jnp.maximum(keep[:4], exchange(keep[4:], 1))
    keep = jnp.maximum(keep[:2], exchange(keep[2:], 0))
    second = (here & CORE) != 0
    ours = jnp.where(second, keep[1], keep[0])
    other = swap(jnp.where(second, keep[0], keep[1]))
    return jnp.maximum(own.reshape(SHARD), jnp.maximum(ours, other))


def solution(mesh):
    placed = (P(("row", "col"), None), P())
    return jax.shard_map(
        body, mesh=mesh, in_specs=placed, out_specs=P(("row", "col")), check_vma=False
    )
```
